32 devices in a mesh: gz: 2 (over core), row: 4 (over y, x), col: 4 (over z).
Axes of the slice: x: 2, y: 2, z: 4, core: 2. Of those that a mesh axis runs over, the one named last changes fastest.
Arguments:
- right_side: float32 [4, 16, 16384], P(None, 'col', 'row'), may hold values from -6 to 6
- layer_sums: float32 [2, 4, 16, 16384], P('gz', None, 'col', 'row'), may hold values from -6 to 6
- lower_blocks: float32 [6, 16, 256, 256], P(None, 'col', 'row'), may hold values from -0.1875 to 0.1875
- upper_blocks: float32 [6, 16, 256, 256], P(None, 'col', 'row'), may hold values from -0.1875 to 0.1875
- lower_inverse: float32 [4, 16, 256, 256], P(None, 'col'), may hold values from -1 to 2, as said below
- upper_diagonal_inverses: float32 [4, 16, 256, 256], P(None, 'col'), may hold values from -1 to 2
- pattern: int32 [6, 16], P(None, 'col'), may hold values 0 or 1
- parents: int32 [3, 16], replicated, may hold values from 0 to 15
Outputs:
- forward_solution: float32 [4, 16, 16384], P(None, 'col')
- solution: float32 [4, 16, 16384], P(None, 'col')
The draws below stay inside these ranges and needn't reach their ends.
Inputs may be any that keep to these rules, and one draw needn't show every extreme that they name: `lower_inverse`: inverses of the diagonal blocks of L.
All inputs are finite; a program needn't handle non-finite values. No bound on the sum of `pattern` on one device may be relied on, other than what follows from the above.
Results may differ from the reference program's by a relative error of at most 0.00013.
Values sent between devices are 32-bit elements; how exact they have to be, the bound alone decides.
No kernel may reach another device: no remote copies, remote signals or barrier semaphores. Data moves between devices by JAX's collectives and lax.ppermute only.
A program may use at most 128 MiB of HBM per device.

```python
import math
import jax
import jax.numpy as jnp
import numpy as np
from jax import lax

WIDTH = 256
COLUMNS = 64
NODES = 16
N_GZ = 2


def leading_block_rows(key):
    first, second = jax.random.split(key)
    shape = (4, NODES, WIDTH, WIDTH)
    diagonal = jax.random.uniform(first, (4, NODES, WIDTH), jnp.float32, 0.75, 1.5)
    spread = jax.random.normal(second, shape, jnp.float32)
    spread = spread * (0.6 / WIDTH ** 0.5)
    return spread + diagonal[..., None] * jnp.eye(WIDTH, dtype=jnp.float32)


def draw_lower_inverse(key, part):
    return leading_block_rows(jax.random.fold_in(key, 11))


def draw_upper_diagonal_inverses(key, part):
    return leading_block_rows(jax.random.fold_in(key, 23))


def plant(values, rng, smallest, largest):
    dims = values.shape
    index_at = [jax.random.randint(jax.random.fold_in(rng, axis), (), 0, dims[axis]) for axis in range(len(dims))]
    values = values.at[tuple(index_at)].set(smallest)
    longest = dims.index(max(dims))
    index_at[longest] = (index_at[longest] + 1) % dims[longest]
    return values.at[tuple(index_at)].set(largest)


def block_levels(stream_key, extent, cuts, low, largest):
    def one(position, shards_of):
        draws = jax.random.uniform(jax.random.fold_in(jax.random.fold_in(stream_key, 6), position), (shards_of,), jnp.float32, low / len(cuts), largest / len(cuts))
        return jnp.repeat(jnp.exp(draws), extent[position] // shards_of).reshape((-1,) + (1,) * (len(extent) - position - 1))

    level = one(*cuts[0])
    for cut in cuts[1:]:
        level = level * one(*cut)
    return level


def rank_table(count, slope):
    weights = [(1 << 20) // math.isqrt(rank ** slope) + 1 for rank in range(1, count + 1)]
    width = 1 + sum(weights) // (1 << 30)
    return np.cumsum(np.array([max(1, weight // width) for weight in weights]))


def skewed_ids(rng, shape, number_of, skew):
    grid = rank_table(number_of, skew)
    lot = jax.random.randint(jax.random.fold_in(rng, 1), shape, 0, int(grid[number_of - 1]))
    rank = jnp.searchsorted(jnp.asarray(grid, jnp.int32), lot, side="right")
    return jax.random.permutation(jax.random.fold_in(rng, 2), number_of)[rank].astype(jnp.int32)


def scatter_about(stream_key, shape, scale, bound, cuts=(), kind=jnp.bfloat16):
    gain = block_levels(stream_key, shape, cuts, -0.22, 0.18) if cuts else 1.0
    drawn = jax.random.normal(stream_key, shape, jnp.float32) * scale * gain
    return jnp.minimum(jnp.maximum(drawn, -bound), bound).astype(kind)


def setup_inputs(seed: int = 0) -> dict:
    keys = jax.random.split(jax.random.key(seed), 9)
    return {
        "right_side": scatter_about(keys[0], (4, NODES, WIDTH * COLUMNS), 1.0, 6.0, ((1, 4), (2, 4)), jnp.float32),
        "layer_sums": scatter_about(keys[1], (N_GZ, 4, NODES, WIDTH * COLUMNS), 1.0, 6.0, ((0, 2), (2, 4), (3, 4)), jnp.float32),
        "lower_blocks": scatter_about(keys[2], (6, NODES, WIDTH, WIDTH), (4 * WIDTH) ** -0.5, 0.1875, ((1, 4), (2, 4)), jnp.float32),
        "upper_blocks": scatter_about(keys[3], (6, NODES, WIDTH, WIDTH), (4 * WIDTH) ** -0.5, 0.1875, ((1, 4), (2, 4)), jnp.float32),
        "lower_inverse": draw_lower_inverse(jax.random.fold_in(keys[8], 71), 0),
        "upper_diagonal_inverses": draw_upper_diagonal_inverses(jax.random.fold_in(keys[8], 71), 0),
        "pattern": plant((jax.random.randint(keys[6], (6, NODES), 0, 4) < 3).astype(jnp.int32), jax.random.fold_in(keys[6], 1), 0, 1),
        "parents": plant(skewed_ids(keys[7], (3, NODES), NODES, 1), jax.random.fold_in(keys[7], 3), 0, NODES - 1).astype(jnp.int32),
    }


def place_of(height, distance):
    return height * (height - 1) // 2 + distance - 1


def ancestor_table(parents):
    ancestors = {}
    for height in range(1, 4):
        current = parents[height - 1]
        ancestors[(height, 1)] = current
        for distance in range(2, height + 1):
            current = parents[height - distance][current]
            ancestors[(height, distance)] = current
    return ancestors


def reference(right_side, layer_sums, lower_blocks, upper_blocks, lower_inverse, upper_diagonal_inverses, pattern, parents):
    present = pattern.astype(jnp.float32)
    ancestors = ancestor_table(parents)
    initial = (right_side - jnp.sum(layer_sums, axis=0)).reshape(4, NODES, WIDTH, COLUMNS)
    pending = [jnp.zeros((NODES, WIDTH, COLUMNS), jnp.float32) for height in range(4)]
    forward = [None] * 4
    for height in (3, 2, 1, 0):
        solved = jnp.einsum("jvw,jwk->jvk", lower_inverse[height], initial[height] - pending[height], precision=lax.Precision.HIGHEST)
        forward[height] = solved
        for distance in range(1, height + 1):
            block_place = place_of(height, distance)
            blocks = lower_blocks[block_place] * present[block_place][:, None, None]
            product = jnp.einsum("jvw,jwk->jvk", blocks, solved, precision=lax.Precision.HIGHEST)
            destination_rows = height - distance
            pending[destination_rows] = pending[destination_rows] + jax.ops.segment_sum(product, ancestors[(height, distance)], num_segments=NODES)
    backward = [None] * 4
    for height in range(4):
        accumulated = jnp.zeros((NODES, WIDTH, COLUMNS), jnp.float32)
        for distance in range(1, height + 1):
            block_place = place_of(height, distance)
            blocks = upper_blocks[block_place] * present[block_place][:, None, None]
            chosen = backward[height - distance][ancestors[(height, distance)]]
            accumulated = accumulated + jnp.einsum("jvw,jwk->jvk", blocks, chosen, precision=lax.Precision.HIGHEST)
        backward[height] = jnp.einsum("jvw,jwk->jvk", upper_diagonal_inverses[height], forward[height] - accumulated, precision=lax.Precision.HIGHEST)
    forward_all = jnp.stack(forward).reshape(4, NODES, WIDTH * COLUMNS)
    backward_sweep_levels = jnp.stack(backward).reshape(4, NODES, WIDTH * COLUMNS)
    return forward_all, backward_sweep_levels
```

```python
import functools

import jax
import jax.numpy as jnp
from jax import lax
from jax.experimental import pallas as pl
from jax.experimental.pallas import tpu as pltpu
from jax.sharding import PartitionSpec as P

WIDTH = 256
COLUMNS = 64
F32 = jnp.float32
BF16 = jnp.bfloat16


def place_of(height, distance):
    return height * (height - 1) // 2 + distance - 1


def partner_of(index, step, count):
    assert count & (count - 1) == 0
    return index ^ step


def exchange(value, axis, step):
    count = lax.axis_size(axis)
    return lax.ppermute(value, axis, [(i, partner_of(i, step, count)) for i in range(count)])


def split(value):
    high = value.astype(BF16)
    return high, (value - high.astype(F32)).astype(BF16)


def dot(left, right):
    return jnp.dot(left, right, preferred_element_type=F32)


def product(left, right_high, right_both):
    high, low = split(left)
    lanes = right_high.shape[1]
    both = dot(high, right_both)
    return both[:, :lanes] + both[:, lanes:] + dot(low, right_high)


def forward_kernel(height, sizes, *refs):
    nodes, part, own, row_count, col_count = sizes
    lanes = nodes * own
    pieces = refs[:row_count]
    parents, pattern, inverse, blocks = refs[row_count : row_count + 4]
    refs = refs[row_count + 4 :]
    pending_in = refs[: height] if height < 3 else ()
    refs = refs[len(pending_in) :]
    solved_ref = refs[0]
    sends = refs[1 : 1 + (col_count if height else 0)]
    refs = refs[1 + len(sends) :]
    pending_out = refs[: max(height - 1, 0)]
    refs = refs[len(pending_out) :]
    full, urgent = refs
    row = lax.axis_index("row")
    col = lax.axis_index("col")
    for step in range(row_count):
        start = partner_of(row, step, row_count) * part
        full[pl.ds(pl.multiple_of(start, part), part), :] = pieces[step][...]
    lane = lax.broadcasted_iota(jnp.int32, (1, lanes), 1) // own
    high, low = split(full[...])
    both = jnp.concatenate([high, low], axis=1)
    solved = jnp.zeros_like(full)
    for node in range(nodes):
        solved = jnp.where(lane == node, product(inverse[0, node], high, both), solved)
    solved_ref[...] = solved
    if height == 0:
        return
    high, low = split(solved)
    both = jnp.concatenate([high, low], axis=1)
    targets = []
    for level in range(height):
        target = urgent if level == height - 1 else pending_out[level]
        target[...] = pending_in[level][...] if pending_in else jnp.zeros_like(target)
        targets.append(target)
    for node in range(nodes):
        ancestor = col * nodes + node
        for distance in range(1, height + 1):
            place = place_of(height, distance)
            level = height - distance
            ancestor = parents[level, ancestor]
            slot = lax.rem(ancestor, nodes)
            where = partner_of(lax.div(ancestor, nodes), col, col_count)
            term = product(blocks[place, node], high, both)
            term = pltpu.roll(term, lax.rem(slot - node + nodes, nodes) * own, 1)
            keep = jnp.where(pattern[place, node] != 0, slot, -1)
            targets[level][where] += jnp.where(lane == keep, term, 0.0)
    for step in range(col_count):
        sends[step][...] = urgent[step]


def forward_step(height, pieces, parents, pattern, inverse, blocks, pending, sizes):
    nodes, part, own, row_count, col_count = sizes
    lanes = nodes * own
    rows = row_count * part
    smem = pl.BlockSpec(memory_space=pltpu.SMEM)
    vmem = pl.BlockSpec(memory_space=pltpu.VMEM)
    piece = jax.ShapeDtypeStruct((part, lanes), F32)
    stack = jax.ShapeDtypeStruct((col_count, part, lanes), F32)
    out_shape = [jax.ShapeDtypeStruct((rows, lanes), F32)]
    if height:
        out_shape += [piece] * col_count + [stack] * (height - 1)
    results = pl.pallas_call(
        functools.partial(forward_kernel, height, sizes),
        out_shape=out_shape,
        grid=(1,),
        in_specs=[vmem] * row_count
        + [smem, smem, pl.BlockSpec((1,) + inverse.shape[1:], lambda i: (height, 0, 0, 0)), vmem]
        + [vmem] * len(pending),
        out_specs=[vmem] * len(out_shape),
        scratch_shapes=[
            pltpu.VMEM((rows, lanes), F32),
            pltpu.VMEM((col_count, part, lanes), F32),
        ],
        compiler_params=pltpu.CompilerParams(vmem_limit_bytes=24 * 2**20),
        name="forward_level",
    )(*pieces, parents, pattern, inverse, blocks, *pending)
    solved = results[0]
    if height == 0:
        return solved, (), ()
    return solved, results[1 : 1 + col_count], results[1 + col_count :]


def solve_nodes(pieces, inverse):
    full_rows = lax.all_gather(pieces, "row", axis=1, tiled=True)
    return jnp.einsum("jvw,jwk->jvk", inverse, full_rows, precision=lax.Precision.HIGHEST)


def body(
    right_side,
    layer_sums,
    lower_blocks,
    upper_blocks,
    lower_inverse,
    upper_diagonal_inverses,
    pattern,
    parents,
):
    per_column = right_side.shape[1]
    part_rows = lower_blocks.shape[2]
    node_count = parents.shape[1]
    gz_count = lax.axis_size("gz")
    row_count = lax.axis_size("row")
    col_count = lax.axis_size("col")
    own_columns = COLUMNS // gz_count
    lanes = per_column * own_columns
    sizes = (per_column, part_rows, own_columns, row_count, col_count)
    grid_column = lax.axis_index("col")
    gz = lax.axis_index("gz")
    present = pattern.astype(F32)
    node_range = jnp.arange(node_count, dtype=jnp.int32)

    def columns_of(values, which):
        values = lax.dynamic_slice_in_dim(
            values.reshape(4, per_column, part_rows, COLUMNS), which * own_columns, own_columns, 3
        )
        return values.transpose(0, 2, 1, 3).reshape(4, part_rows, lanes)

    own_part = columns_of(right_side, gz) - columns_of(layer_sums[0], gz)
    away = [
        -columns_of(layer_sums[0], partner_of(gz, step, gz_count)) for step in range(1, gz_count)
    ]
    initial = [None] * 4
    count = gz_count * row_count

    def direct(value, gz_step, row_step):
        pairs = []
        for i in range(count):
            g, r = divmod(i, row_count)
            g, r = partner_of(g, gz_step, gz_count), partner_of(r, row_step, row_count)
            pairs.append((i, g * row_count + r))
        return lax.ppermute(value, ("gz", "row"), pairs)

    pieces = []
    for row_step in range(row_count):
        piece = own_part[3] if row_step == 0 else direct(own_part[3], 0, row_step)
        for gz_step in range(1, gz_count):
            piece = piece + direct(away[gz_step - 1][3], gz_step, row_step)
        pieces.append(piece)
    rest = own_part[:3]
    for gz_step in range(1, gz_count):
        rest = rest + exchange(away[gz_step - 1][:3], "gz", gz_step)

    forward = [None] * 4
    pending = ()
    for height in (3, 2, 1, 0):
        if height < 3:
            mine = rest[height] - sends[0]
            for step in range(1, col_count):
                mine = mine - exchange(sends[step], "col", step)
            pieces = [mine] + [exchange(mine, "row", step) for step in range(1, row_count)]
        forward[height], sends, pending = forward_step(
            height, pieces, parents, pattern, lower_inverse, lower_blocks, pending, sizes
        )
    forward = [
        value.reshape(WIDTH, per_column, own_columns).transpose(1, 0, 2) for value in forward
    ]

    picker_masks = {}
    for height in range(1, 4):
        current = lax.dynamic_slice_in_dim(
            parents[height - 1], grid_column * per_column, per_column, 0
        )
        for distance in range(1, height + 1):
            if distance > 1:
                lookup = parents[height - distance]
                current = jnp.sum(
                    jnp.where(current[:, None] == node_range[None, :], lookup[None, :], 0), axis=1
                )
            picker_masks[height, distance] = (current[:, None] == node_range[None, :]).astype(F32)
    backward = [None] * 4
    whole_levels = [None] * 3
    row_start = lax.axis_index("row") * part_rows
    for height in range(4):
        if height == 0:
            solved = jnp.einsum(
                "jvw,jwk->jvk",
                upper_diagonal_inverses[0],
                forward[0],
                precision=lax.Precision.HIGHEST,
            )
        else:
            remaining_right = lax.dynamic_slice_in_dim(forward[height], row_start, part_rows, 1)
            for distance in range(1, height + 1):
                block_place = place_of(height, distance)
                chosen = jnp.einsum(
                    "ja,awk->jwk",
                    picker_masks[height, distance],
                    whole_levels[height - distance],
                    precision=lax.Precision.HIGHEST,
                )
                update = jnp.einsum(
                    "jvw,jwk->jvk",
                    upper_blocks[block_place],
                    chosen,
                    precision=lax.Precision.HIGHEST,
                )
                remaining_right = remaining_right - update * present[block_place][:, None, None]
            solved = solve_nodes(remaining_right, upper_diagonal_inverses[height])
        backward[height] = solved
        if height < 3:
            whole_levels[height] = lax.all_gather(solved, "col", axis=0, tiled=True)
    forward_all = jnp.stack(forward)
    backward_sweep_levels = jnp.stack(backward)
    forward_all, backward_sweep_levels = (
        lax.all_gather(forward_all, "gz", axis=3, tiled=True),
        lax.all_gather(backward_sweep_levels, "gz", axis=3, tiled=True),
    )
    return (
        forward_all.reshape(4, per_column, WIDTH * COLUMNS),
        backward_sweep_levels.reshape(4, per_column, WIDTH * COLUMNS),
    )


def solution(mesh):
    in_specs = (
        P(None, "col", "row"),
        P("gz", None, "col", "row"),
        P(None, "col", "row", None),
        P(None, "col", "row", None),
        P(None, "col", None, None),
        P(None, "col", None, None),
        P(None, "col"),
        P(),
    )
    out_specs = (P(None, "col", None), P(None, "col", None))
    return jax.shard_map(body, mesh=mesh, in_specs=in_specs, out_specs=out_specs, check_vma=False)
```

```python
import functools

import jax
import jax.numpy as jnp
from jax import lax
from jax.experimental import pallas as pl
from jax.experimental.pallas import tpu as pltpu
from jax.sharding import PartitionSpec as P

WIDTH = 256
COLUMNS = 64
LANES = 128
F32 = jnp.float32
BF16 = jnp.bfloat16
SMEM = pl.BlockSpec(memory_space=pltpu.SMEM)
VMEM = pl.BlockSpec(memory_space=pltpu.VMEM)
HBM = pl.BlockSpec(memory_space=pltpu.HBM)
PARAMS = pltpu.CompilerParams(vmem_limit_bytes=24 * 2**20)


def place_of(height, distance):
    return height * (height - 1) // 2 + distance - 1


def shape_of(*dims, dtype=F32):
    return jax.ShapeDtypeStruct(dims, dtype)


def split(value):
    high = value.astype(BF16)
    return high, (value - high.astype(F32)).astype(BF16)


def dot(left, right):
    return jnp.dot(left, right, preferred_element_type=F32)


def dot_t(left, right):
    return lax.dot_general(left, right, (((1,), (1,)), ((), ())), preferred_element_type=F32)


def product(left, right_high, right_both):
    high, low = split(left)
    lanes = right_high.shape[1]
    both = dot(high, right_both)
    return both[:, :lanes] + both[:, lanes:] + dot(low, right_high)


def product_t(left, right_high, right_low):
    high, low = split(left)
    rows = left.shape[0]
    both = dot_t(jnp.concatenate([high, low], axis=0), right_high)
    return both[:rows] + both[rows:] + dot_t(high, right_low)


def gather_all(value, axes, count):
    return lax.all_to_all(jnp.broadcast_to(value[None], (count,) + value.shape), axes, 0, 0)


def input_kernel(gz_count, nodes, own, right, layer, out):
    gz = lax.axis_index("gz")
    tiles = right.shape[1]
    per_tile = LANES // COLUMNS
    block = lax.broadcasted_iota(jnp.int32, (1, LANES), 1) // own
    for level in range(right.shape[0]):
        for which in range(gz_count):
            mine = jnp.where(gz == which, 1.0, 0.0)
            for row in range(per_tile):
                total = jnp.zeros((tiles, LANES), F32)
                for node in range(nodes):
                    value = right[level, :, node, :] * mine - layer[level, :, node, :]
                    shift = (node * own - row * COLUMNS - which * own) % LANES
                    value = pltpu.roll(value, shift, 1) if shift else value
                    total = jnp.where(block == node, value, total)
                out[which, level, pl.ds(row, tiles, stride=per_tile), :] = total


def forward_kernel(height, sizes, *refs):
    nodes, part, own, row_count, col_count = sizes
    lanes = nodes * own
    full, parents, pattern, inverse_hbm = refs[:4]
    if height:
        blocks = refs[4]
        pending_in = refs[5 : 5 + height] if height < 3 else ()
        refs = refs[5 + len(pending_in) :]
        solved_ref, urgent = refs[:2]
        pending_out = refs[2 : 1 + height]
        inverse, sem = refs[1 + height :]
    else:
        other_hbm, solved_ref, next_ref, inverse, other, turned, sem = refs[4:]
        other_copy = pltpu.make_async_copy(other_hbm.at[0], other, sem.at[1])
        other_copy.start()
    copy = pltpu.make_async_copy(inverse_hbm.at[height], inverse, sem.at[0])
    copy.start()
    lane = lax.broadcasted_iota(jnp.int32, (1, lanes), 1) // own
    high, low = split(full[...])
    both = jnp.concatenate([high, low], axis=1)
    solved = jnp.zeros(full.shape, F32)
    copy.wait()
    for node in range(nodes):
        solved = jnp.where(lane == node, product(inverse[node], high, both), solved)
    solved_ref[...] = solved
    if height == 0:
        other_copy.wait()
        turn(solved, turned, other, next_ref, nodes, own, row_count)
        return
    col = lax.axis_index("col")
    high, low = split(solved)
    both = jnp.concatenate([high, low], axis=1)
    targets = []
    for level in range(height):
        target = urgent if level == height - 1 else pending_out[level]
        target[...] = pending_in[level][...] if pending_in else jnp.zeros(target.shape, F32)
        targets.append(target)
    for node in range(nodes):
        ancestor = col * nodes + node
        for distance in range(1, height + 1):
            place = place_of(height, distance)
            level = height - distance
            ancestor = parents[level, ancestor]
            slot = lax.rem(ancestor, nodes)
            term = product(blocks[place, node], high, both)
            term = pltpu.roll(term, lax.rem(slot - node + nodes, nodes) * own, 1)
            keep = jnp.where(pattern[place, node] != 0, slot, -1)
            targets[level][lax.div(ancestor, nodes)] += jnp.where(lane == keep, term, 0.0)


def forward_step(height, full, parents, pattern, inverse, blocks, pending, upper, sizes):
    nodes, part, own, row_count, col_count = sizes
    lanes = nodes * own
    rows = row_count * part
    stack = shape_of(col_count, part, lanes)
    kernel = functools.partial(forward_kernel, height, sizes)
    level_inverse = pltpu.VMEM((nodes, rows, rows), F32)
    if height == 0:
        return pl.pallas_call(
            kernel,
            out_shape=[shape_of(rows, lanes), shape_of(nodes, own // row_count, rows)],
            in_specs=[VMEM, SMEM, SMEM, HBM, HBM],
            out_specs=[VMEM] * 2,
            scratch_shapes=[
                level_inverse,
                level_inverse,
                pltpu.VMEM((lanes, rows), F32),
                pltpu.SemaphoreType.DMA((2,)),
            ],
            compiler_params=PARAMS,
            name="forward_last",
        )(full, parents, pattern, inverse, upper)
    out_shape = [shape_of(rows, lanes), stack] + [stack] * (height - 1)
    return pl.pallas_call(
        kernel,
        out_shape=out_shape,
        in_specs=[VMEM, SMEM, SMEM, HBM, VMEM] + [VMEM] * len(pending),
        out_specs=[VMEM] * len(out_shape),
        scratch_shapes=[level_inverse, pltpu.SemaphoreType.DMA((1,))],
        compiler_params=PARAMS,
        name="forward_level",
    )(full, parents, pattern, inverse, blocks, *pending)


def turn(solved, turned, inverse, out, nodes, own, row_count):
    turned[...] = solved.T
    few = own // row_count
    row = lax.axis_index("row")
    for node in range(nodes):
        start = pl.multiple_of(node * own + row * few, few)
        high, low = split(inverse[node])
        out[node] = product_t(turned[pl.ds(start, few), :], high, low)


def turn_kernel(height, sizes, solved, inverse_hbm, out, inverse, turned, sem):
    nodes, part, own, row_count, col_count = sizes
    copy = pltpu.make_async_copy(inverse_hbm.at[height], inverse, sem)
    copy.start()
    copy.wait()
    turn(solved[...], turned, inverse, out, nodes, own, row_count)


def turn_step(height, solved, inverse, sizes):
    nodes, part, own, row_count, col_count = sizes
    rows = row_count * part
    return pl.pallas_call(
        functools.partial(turn_kernel, height, sizes),
        out_shape=shape_of(nodes, own // row_count, rows),
        in_specs=[VMEM, HBM],
        out_specs=VMEM,
        scratch_shapes=[
            pltpu.VMEM((nodes, rows, rows), F32),
            pltpu.VMEM((nodes * own, rows), F32),
            pltpu.SemaphoreType.DMA,
        ],
        compiler_params=PARAMS,
        name="turn_level",
    )(solved, inverse)


def compose_kernel(nodes, gathered, inverse, high_out, low_out):
    for node in range(nodes):
        block = gathered[:, 0, node].reshape(WIDTH, WIDTH)
        right_high, right_low = split(block)
        high, low = split(inverse[0, node])
        whole = dot(high, right_high) + dot(low, right_high) + dot(high, right_low)
        high, low = split(whole)
        high_out[0, node] = high
        low_out[0, node] = low


def compose_step(height, gathered, inverse, row_count):
    per, nodes = gathered.shape[1:3]
    part = gathered.shape[3]
    first = place_of(height, 1)
    out = shape_of(height, nodes, WIDTH, WIDTH, dtype=BF16)
    out_spec = pl.BlockSpec((1, nodes, WIDTH, WIDTH), lambda i: (i, 0, 0, 0))
    return pl.pallas_call(
        functools.partial(compose_kernel, nodes),
        grid=(height,),
        out_shape=[out, out],
        in_specs=[
            pl.BlockSpec(
                (row_count, 1, nodes, part, WIDTH),
                lambda i: ((first + i) // per, (first + i) % per, 0, 0, 0),
            ),
            pl.BlockSpec((1, nodes, WIDTH, WIDTH), lambda i: (height, 0, 0, 0)),
        ],
        out_specs=[out_spec] * 2,
        compiler_params=PARAMS,
        cost_estimate=pl.CostEstimate(
            flops=6 * height * nodes * WIDTH**3,
            bytes_accessed=12 * height * nodes * WIDTH**2,
            transcendentals=0,
        ),
        name="compose_level",
    )(gathered, inverse)


def backward_kernel(height, nodes, parents, pattern, start, high, low, *refs):
    solved, out = refs[:height], refs[height]
    col = lax.axis_index("col")
    for node in range(nodes):
        total = start[node]
        ancestor = col * nodes + node
        for distance in range(1, height + 1):
            level = height - distance
            ancestor = parents[level, ancestor]
            value = solved[level][lax.div(ancestor, nodes), lax.rem(ancestor, nodes)]
            term = product_t(value, high[distance - 1, node], low[distance - 1, node])
            stored = pattern[place_of(height, distance), node] != 0
            total = total - jnp.where(stored, term, 0.0)
        out[node] = total


def backward_step(height, parents, pattern, start, composed, solved):
    return pl.pallas_call(
        functools.partial(backward_kernel, height, start.shape[0]),
        out_shape=shape_of(*start.shape),
        in_specs=[SMEM, SMEM] + [VMEM] * (3 + height),
        out_specs=VMEM,
        compiler_params=PARAMS,
        name="backward_level",
    )(parents, pattern, start, *composed, *solved)


def forward_out_kernel(gz_count, nodes, own, gathered, out):
    per_tile = LANES // COLUMNS
    tiles = out.shape[1]
    block = lax.broadcasted_iota(jnp.int32, (1, LANES), 1) // own
    for node in range(nodes):
        total = jnp.zeros((tiles, LANES), F32)
        for row in range(per_tile):
            for which in range(gz_count):
                value = gathered[which, 0, pl.ds(row, tiles, stride=per_tile), :]
                place = row * gz_count + which
                shift = ((place - node) * own) % LANES
                value = pltpu.roll(value, shift, 1) if shift else value
                total = jnp.where(block == place, value, total)
        out[0, :, node, :] = total


def backward_out_kernel(nodes, gathered, *refs):
    out, turned = refs[-2:]
    per_tile = LANES // COLUMNS
    tiles = out.shape[1]
    for node in range(nodes):
        turned[...] = gathered[:, 0, node].reshape(COLUMNS, WIDTH).T
        rows = [turned[pl.ds(row, tiles, stride=per_tile), :] for row in range(per_tile)]
        out[0, :, node, :] = jnp.concatenate(rows, axis=1)


def backward_out(gathered, before, first, nodes):
    count, levels, nodes, few, rows = gathered.shape
    tiles = rows * COLUMNS // LANES
    ready = [before] if before is not None else []
    return pl.pallas_call(
        functools.partial(backward_out_kernel, nodes),
        grid=(levels,),
        out_shape=shape_of(4, tiles, nodes, LANES),
        in_specs=[pl.BlockSpec((count, 1, nodes, few, rows), lambda i: (0, i, 0, 0, 0))]
        + [HBM] * len(ready),
        out_specs=pl.BlockSpec((1, tiles, nodes, LANES), lambda i: (first + i, 0, 0, 0)),
        scratch_shapes=[pltpu.VMEM((rows, COLUMNS), F32)],
        input_output_aliases={1: 0} if ready else {},
        compiler_params=PARAMS,
        name="backward_out",
    )(gathered, *ready)


def body(
    right_side,
    layer_sums,
    lower_blocks,
    upper_blocks,
    lower_inverse,
    upper_diagonal_inverses,
    pattern,
    parents,
):
    nodes = right_side.shape[1]
    part = lower_blocks.shape[2]
    gz_count = lax.axis_size("gz")
    row_count = lax.axis_size("row")
    col_count = lax.axis_size("col")
    own = COLUMNS // gz_count
    lanes = nodes * own
    layer_count = gz_count * row_count
    sizes = (nodes, part, own, row_count, col_count)
    gz = lax.axis_index("gz")

    per = upper_blocks.shape[0] // gz_count
    upper_rows = lax.all_gather(
        lax.dynamic_slice_in_dim(upper_blocks, gz * per, per, 0), ("gz", "row")
    )

    def tiled(value):
        return value.reshape(4, nodes, part * COLUMNS // LANES, LANES).transpose(0, 2, 1, 3)

    parts = pl.pallas_call(
        functools.partial(input_kernel, gz_count, nodes, own),
        out_shape=shape_of(gz_count, 4, part, lanes),
        in_specs=[VMEM, VMEM],
        out_specs=VMEM,
        compiler_params=PARAMS,
        name="input_parts",
    )(tiled(right_side), tiled(layer_sums[0]))

    top = jnp.broadcast_to(parts[:, None, 3], (gz_count, row_count, part, lanes))
    top = lax.all_to_all(top.reshape(layer_count, part, lanes), ("gz", "row"), 0, 0)
    full = top.reshape(gz_count, row_count * part, lanes).sum(0)
    rest = lax.all_to_all(parts[:, :3], "gz", 0, 0).sum(0)

    forward = [None] * 4
    pending = []
    for height in (3, 2, 1, 0):
        if height < 3:
            mine = rest[height] - lax.all_to_all(urgent, "col", 0, 0).sum(0)
            full = gather_all(mine, "row", row_count).reshape(row_count * part, lanes)
        results = forward_step(
            height,
            full,
            parents,
            pattern,
            lower_inverse,
            lower_blocks,
            pending,
            upper_diagonal_inverses,
            sizes,
        )
        forward[height], urgent, pending = results[0], results[1], results[2:]

    backward = [urgent, None, None, None]
    whole = []
    for height in (1, 2, 3):
        composed = compose_step(height, upper_rows, upper_diagonal_inverses, row_count)
        start = turn_step(height, forward[height], upper_diagonal_inverses, sizes)
        whole.append(gather_all(backward[height - 1], "col", col_count))
        backward[height] = backward_step(height, parents, pattern, start, composed, whole)

    tiles = WIDTH * COLUMNS // LANES
    forward_all = lax.all_gather(jnp.stack(forward), "gz")
    forward_all = pl.pallas_call(
        functools.partial(forward_out_kernel, gz_count, nodes, own),
        grid=(4,),
        out_shape=shape_of(4, tiles, nodes, LANES),
        in_specs=[pl.BlockSpec((gz_count, 1, WIDTH, lanes), lambda i: (0, i, 0, 0))],
        out_specs=pl.BlockSpec((1, tiles, nodes, LANES), lambda i: (i, 0, 0, 0)),
        compiler_params=PARAMS,
        name="forward_out",
    )(forward_all)
    early = lax.all_gather(jnp.stack(backward[:3]), ("gz", "row"))
    backward_all = backward_out(early, None, 0, nodes)
    late = gather_all(backward[3][None], ("gz", "row"), layer_count)
    backward_all = backward_out(late, backward_all, 3, nodes)
    return tuple(
        value.transpose(0, 2, 1, 3).reshape(4, nodes, WIDTH * COLUMNS)
        for value in (forward_all, backward_all)
    )


def solution(mesh):
    in_specs = (
        P(None, "col", "row"),
        P("gz", None, "col", "row"),
        P(None, "col", "row", None),
        P(None, "col", "row", None),
        P(None, "col", None, None),
        P(None, "col", None, None),
        P(None, "col"),
        P(),
    )
    out_specs = (P(None, "col", None), P(None, "col", None))
    return jax.shard_map(body, mesh=mesh, in_specs=in_specs, out_specs=out_specs, check_vma=False)
```

```python
import functools

import jax
import jax.numpy as jnp
from jax import lax
from jax.experimental import pallas as pl
from jax.experimental.pallas import tpu as pltpu
from jax.sharding import PartitionSpec as P

WIDTH = 256
COLUMNS = 64
LANES = 128
F32 = jnp.float32
BF16 = jnp.bfloat16
SMEM = pl.BlockSpec(memory_space=pltpu.SMEM)
VMEM = pl.BlockSpec(memory_space=pltpu.VMEM)
HBM = pl.BlockSpec(memory_space=pltpu.HBM)
PARAMS = pltpu.CompilerParams(vmem_limit_bytes=16 * 2**20)
STREAM_PARAMS = pltpu.CompilerParams(vmem_limit_bytes=44 * 2**20)


def place_of(height, distance):
    return height * (height - 1) // 2 + distance - 1


def shape_of(*dims, dtype=F32):
    return jax.ShapeDtypeStruct(dims, dtype)


def split(value):
    high = value.astype(BF16)
    return high, (value - high.astype(F32)).astype(BF16)


def dot(left, right):
    return jnp.dot(left, right, preferred_element_type=F32)


def dot_t(left, right):
    return lax.dot_general(left, right, (((1,), (1,)), ((), ())), preferred_element_type=F32)


def product(left, right):
    lanes = right[0].shape[1]
    both = dot(left[0], jnp.concatenate(right, axis=1))
    return both[:, :lanes] + both[:, lanes:] + dot(left[1], right[0])


def product_t(left, right):
    rows = left[0].shape[0]
    both = dot_t(jnp.concatenate(left, axis=0), right[0])
    return both[:rows] + both[rows:] + dot_t(left[0], right[1])


def bits_of(count):
    assert count & (count - 1) == 0
    return count.bit_length() - 1


def swap(value, axis, bit):
    return lax.ppermute(value, axis, [(i, i ^ 1 << bit) for i in range(lax.axis_size(axis))])


def reversed_bits(index, bits):
    total = index & 0
    for bit in range(bits):
        total = total | ((index >> bit) & 1) << (bits - 1 - bit)
    return total


def gather(value, steps):
    pieces = [value[None]]
    for axis, bit in steps:
        whole = jnp.concatenate(pieces, 0) if len(pieces) > 1 else pieces[0]
        pieces.append(swap(whole, axis, bit))
    return pieces


def col_steps(count):
    return [("col", bit) for bit in reversed(range(bits_of(count)))]


def row_steps(count):
    return [("row", bit) for bit in range(bits_of(count))]


def input_kernel(gz_count, nodes, own, right, layer, keep, *away):
    gz = lax.axis_index("gz")
    tiles = right.shape[1]
    per_tile = LANES // COLUMNS
    block = lax.broadcasted_iota(jnp.int32, (1, LANES), 1) // own
    for level in range(right.shape[0]):
        for row in range(per_tile):
            totals = []
            for which in range(gz_count):
                mine = jnp.where(gz == which, 1.0, 0.0)
                total = jnp.zeros((tiles, LANES), F32)
                for node in range(nodes):
                    value = right[level, :, node, :] * mine - layer[level, :, node, :]
                    shift = (node * own - row * COLUMNS - which * own) % LANES
                    value = pltpu.roll(value, shift, 1) if shift else value
                    total = jnp.where(block == node, value, total)
                totals.append(total)
            for step in range(gz_count):
                chosen = totals[0]
                for which in range(1, gz_count):
                    chosen = jnp.where((gz ^ step) == which, totals[which], chosen)
                target = keep if step == 0 else away[step - 1]
                target[level, pl.ds(row, tiles, stride=per_tile), :] = chosen


def prepare_kernel(nodes, blocks, lower, upper, m_high, m_low, z_high, z_low):
    step = pl.program_id(0)
    for node in range(nodes):
        right = split(lower[0, node])
        left = split(upper[0, node])
        z_high[0, node], z_low[0, node] = split(product(left, right))
    for height in range(1, 4):

        @pl.when(step == height)
        def _():
            for node in range(nodes):
                right = split(lower[0, node])
                for distance in range(1, height + 1):
                    place = place_of(height, distance)
                    m_high[place, node], m_low[place, node] = split(
                        product(split(blocks[place, node]), right)
                    )


def prepare_step(blocks, lower, upper):
    nodes = lower.shape[1]
    level = pl.BlockSpec((1, nodes, WIDTH, WIDTH), lambda i: (i, 0, 0, 0))
    whole = pl.BlockSpec(blocks.shape, lambda i: (0, 0, 0, 0))
    m_shape = shape_of(*blocks.shape, dtype=BF16)
    z_shape = shape_of(*lower.shape, dtype=BF16)
    m_high, m_low, z_high, z_low = pl.pallas_call(
        functools.partial(prepare_kernel, nodes),
        grid=(4,),
        out_shape=[m_shape, m_shape, z_shape, z_shape],
        in_specs=[whole, level, level],
        out_specs=[whole, whole, level, level],
        compiler_params=STREAM_PARAMS,
        cost_estimate=pl.CostEstimate(
            flops=6 * 5 * nodes * WIDTH**3, bytes_accessed=20 * 2**20, transcendentals=0
        ),
        name="prepare",
    )(blocks, lower, upper)
    return (m_high, m_low), (z_high, z_low)


def assemble(pieces, full, part):
    row = lax.axis_index("row")
    place = 0
    for piece in pieces:
        for i in range(piece.shape[0]):
            start = pl.multiple_of((row ^ place) * part, part)
            full[pl.ds(start, part), :] = piece[i]
            place += 1


def forward_kernel(height, sizes, *refs):
    nodes, part, own, row_count, col_count = sizes
    lanes = nodes * own
    pieces, refs = refs[: 1 + bits_of(row_count)], refs[1 + bits_of(row_count) :]
    parents, pattern, m_high, m_low = refs[:4]
    pending_in = refs[4 : 4 + height] if height < 3 else ()
    full, keep, send = refs[4 + len(pending_in) :][:3]
    pending_out = refs[7 + len(pending_in) :][: height - 1]
    urgent = refs[-1]
    assemble(pieces, full, part)
    lane = lax.broadcasted_iota(jnp.int32, (1, lanes), 1) // own
    col = lax.axis_index("col")
    right = split(full[...])
    targets = []
    for level in range(height):
        target = urgent if level == height - 1 else pending_out[level]
        target[...] = pending_in[level][...] if pending_in else jnp.zeros(target.shape, F32)
        targets.append(target)
    for node in range(nodes):
        ancestor = col * nodes + node
        for distance in range(1, height + 1):
            place = place_of(height, distance)
            level = height - distance
            ancestor = parents[level, ancestor]
            slot = lax.rem(ancestor, nodes)
            where = reversed_bits(lax.div(ancestor, nodes) ^ col, bits_of(col_count))
            term = product((m_high[place, node], m_low[place, node]), right)
            term = pltpu.roll(term, lax.rem(slot - node + nodes, nodes) * own, 1)
            stored = jnp.where(pattern[place, node] != 0, slot, -1)
            targets[level][where] += jnp.where(lane == stored, term, 0.0)
    keep[...] = urgent[: col_count // 2]
    send[...] = urgent[col_count // 2 :]


def forward_step(height, pieces, parents, pattern, m, pending, sizes):
    nodes, part, own, row_count, col_count = sizes
    lanes = nodes * own
    half = shape_of(col_count // 2, part, lanes)
    stack = shape_of(col_count, part, lanes)
    out_shape = [shape_of(row_count * part, lanes), half, half] + [stack] * (height - 1)
    results = pl.pallas_call(
        functools.partial(forward_kernel, height, sizes),
        out_shape=out_shape,
        in_specs=[VMEM] * len(pieces) + [SMEM, SMEM] + [VMEM] * (2 + len(pending)),
        out_specs=[VMEM] * len(out_shape),
        scratch_shapes=[pltpu.VMEM(stack.shape, F32)],
        compiler_params=PARAMS,
        name="forward_level",
    )(*pieces, parents, pattern, *m, *pending)
    return results[0], results[1], results[2], results[3:]


def turn(full, turned, z_high, z_low, out, own, row_count):
    turned[...] = full.T
    few = own // row_count
    row = lax.axis_index("row")
    for node in range(out.shape[0]):
        start = pl.multiple_of(node * own + row * few, few)
        left = split(turned[pl.ds(start, few), :])
        out[node] = product_t(left, (z_high[0, node], z_low[0, node]))


def last_kernel(sizes, *refs):
    nodes, part, own, row_count, col_count = sizes
    pieces = refs[: 1 + bits_of(row_count)]
    z_high, z_low, full, out, turned = refs[len(pieces) :]
    assemble(pieces, full, part)
    turn(full[...], turned, z_high, z_low, out, own, row_count)


def last_step(pieces, z, sizes):
    nodes, part, own, row_count, col_count = sizes
    lanes, rows = nodes * own, row_count * part

    def whole(value):
        return pl.BlockSpec(value.shape, lambda i: (0,) * value.ndim)

    level = pl.BlockSpec((1, nodes, rows, rows), lambda i: (0, 0, 0, 0))
    outs = [shape_of(rows, lanes), shape_of(nodes, own // row_count, rows)]
    return pl.pallas_call(
        functools.partial(last_kernel, sizes),
        grid=(1,),
        out_shape=outs,
        in_specs=[whole(piece) for piece in pieces] + [level] * 2,
        out_specs=[whole(out) for out in outs],
        scratch_shapes=[pltpu.VMEM((lanes, rows), F32)],
        compiler_params=PARAMS,
        name="forward_last",
    )(*pieces, *z)


def turn_kernel(sizes, full, z_high, z_low, out, turned):
    nodes, part, own, row_count, col_count = sizes
    turn(full[...], turned, z_high, z_low, out, own, row_count)


def turn_step(height, full, z, sizes):
    nodes, part, own, row_count, col_count = sizes
    rows, lanes = full.shape
    out = shape_of(nodes, own // row_count, rows)
    level = pl.BlockSpec((1, nodes, rows, rows), lambda i: (height, 0, 0, 0))
    return pl.pallas_call(
        functools.partial(turn_kernel, sizes),
        grid=(1,),
        out_shape=out,
        in_specs=[pl.BlockSpec(full.shape, lambda i: (0, 0)), level, level],
        out_specs=pl.BlockSpec(out.shape, lambda i: (0, 0, 0)),
        scratch_shapes=[pltpu.VMEM((lanes, rows), F32)],
        compiler_params=PARAMS,
        name="turn_level",
    )(full, *z)


def solve_kernel(nodes, own, first, second, third, fourth, lower, out):
    step = pl.program_id(0)
    lane = lax.broadcasted_iota(jnp.int32, (1, nodes * own), 1) // own
    for height, full in enumerate((first, second, third, fourth)):

        @pl.when(step == height)
        def _():
            right = split(full[...])
            solved = jnp.zeros(full.shape, F32)
            for node in range(nodes):
                solved = jnp.where(lane == node, product(split(lower[0, node]), right), solved)
            out[0] = solved


def solve_step(fulls, lower, own):
    nodes = lower.shape[1]
    rows, lanes = fulls[0].shape
    whole = pl.BlockSpec((rows, lanes), lambda i: (0, 0))
    return pl.pallas_call(
        functools.partial(solve_kernel, nodes, own),
        grid=(4,),
        out_shape=shape_of(4, rows, lanes),
        in_specs=[whole] * 4 + [pl.BlockSpec((1, nodes, rows, rows), lambda i: (i, 0, 0, 0))],
        out_specs=pl.BlockSpec((1, rows, lanes), lambda i: (i, 0, 0)),
        compiler_params=STREAM_PARAMS,
        name="solve_levels",
    )(*fulls, lower)


def compose_kernel(nodes, gathered, inverse, high_out, low_out):
    for node in range(nodes):
        block = gathered[:, 0, node].reshape(WIDTH, WIDTH)
        whole = product(split(inverse[0, node]), split(block))
        high_out[0, node], low_out[0, node] = split(whole)


def compose_step(gathered, inverse, row_count):
    per, nodes, part = gathered.shape[1:4]
    pairs = place_of(4, 1)
    out = shape_of(pairs, nodes, WIDTH, WIDTH, dtype=BF16)
    out_spec = pl.BlockSpec((1, nodes, WIDTH, WIDTH), lambda i: (i, 0, 0, 0))

    def height_of(i):
        return 1 + sum((i >= place_of(height, 1)).astype(jnp.int32) for height in (2, 3))

    return pl.pallas_call(
        functools.partial(compose_kernel, nodes),
        grid=(pairs,),
        out_shape=[out, out],
        in_specs=[
            pl.BlockSpec((row_count, 1, nodes, part, WIDTH), lambda i: (i // per, i % per, 0, 0, 0)),
            pl.BlockSpec((1, nodes, WIDTH, WIDTH), lambda i: (height_of(i), 0, 0, 0)),
        ],
        out_specs=[out_spec] * 2,
        compiler_params=STREAM_PARAMS,
        cost_estimate=pl.CostEstimate(
            flops=6 * pairs * nodes * WIDTH**3,
            bytes_accessed=12 * pairs * nodes * WIDTH**2,
            transcendentals=0,
        ),
        name="compose",
    )(gathered, inverse)


def backward_kernel(height, nodes, col_count, parents, pattern, start, high, low, *refs):
    pieces_each = 1 + bits_of(col_count)
    out = refs[height * pieces_each]
    early = refs[height * pieces_each + 1] if height == 2 else None
    solved = refs[-1]
    for level in range(height):
        place = 0
        for piece in refs[level * pieces_each : (level + 1) * pieces_each]:
            solved[level, place : place + piece.shape[0]] = piece[...]
            place += piece.shape[0]
    col = lax.axis_index("col")
    for node in range(nodes):
        total = start[node]
        ancestor = col * nodes + node
        for distance in range(1, height + 1):
            level = height - distance
            place = place_of(height, distance)
            ancestor = parents[level, ancestor]
            where = reversed_bits(lax.div(ancestor, nodes) ^ col, bits_of(col_count))
            left = split(solved[level, where, lax.rem(ancestor, nodes)])
            term = product_t(left, (high[place, node], low[place, node]))
            total = total - jnp.where(pattern[place, node] != 0, term, 0.0)
        out[node] = total
        if early is not None:
            early[height, node] = total
    if early is not None:
        for level in range(height):
            early[level] = solved[level, 0]


def backward_step(height, parents, pattern, start, composed, solved):
    nodes = start.shape[0]
    col_count = lax.axis_size("col")
    pieces = [piece for level in solved for piece in level]
    outs = [start.shape] + ([(height + 1,) + start.shape] if height == 2 else [])
    return pl.pallas_call(
        functools.partial(backward_kernel, height, nodes, col_count),
        out_shape=[shape_of(*out) for out in outs],
        in_specs=[SMEM, SMEM] + [VMEM] * (3 + len(pieces)),
        out_specs=[VMEM] * len(outs),
        scratch_shapes=[pltpu.VMEM((height, col_count) + start.shape, F32)],
        compiler_params=PARAMS,
        name="backward_level",
    )(parents, pattern, start, *composed, *pieces)


def forward_out_kernel(gz_count, nodes, own, *refs):
    parts, out = refs[:gz_count], refs[gz_count]
    gz = lax.axis_index("gz")
    per_tile = LANES // COLUMNS
    tiles = out.shape[1]
    block = lax.broadcasted_iota(jnp.int32, (1, LANES), 1) // own
    values = []
    for row in range(per_tile):
        found = [part[0, pl.ds(row, tiles, stride=per_tile), :] for part in parts]
        for which in range(gz_count):
            value = found[0]
            for step in range(1, gz_count):
                value = jnp.where((gz ^ step) == which, found[step], value)
            values.append(value)
    for node in range(nodes):
        total = jnp.zeros((tiles, LANES), F32)
        for place, value in enumerate(values):
            shift = ((place - node) * own) % LANES
            value = pltpu.roll(value, shift, 1) if shift else value
            total = jnp.where(block == place, value, total)
        out[0, :, node, :] = total


def forward_out(parts, nodes, own):
    rows, lanes = parts[0].shape[1:]
    tiles = rows * COLUMNS // LANES
    part_spec = pl.BlockSpec((1, rows, lanes), lambda i: (i, 0, 0))
    return pl.pallas_call(
        functools.partial(forward_out_kernel, len(parts), nodes, own),
        grid=(4,),
        out_shape=shape_of(4, tiles, nodes, LANES),
        in_specs=[part_spec] * len(parts),
        out_specs=pl.BlockSpec((1, tiles, nodes, LANES), lambda i: (i, 0, 0, 0)),
        compiler_params=PARAMS,
        name="forward_out",
    )(*parts)


def backward_out_kernel(nodes, row_count, piece_count, *refs):
    pieces, (out, columns, turned) = refs[:piece_count], refs[-3:]
    per_tile = LANES // COLUMNS
    tiles = out.shape[1]
    few = pieces[0].shape[3]
    row = lax.axis_index("row")
    gz = lax.axis_index("gz")
    for node in range(nodes):
        place = 0
        for piece in pieces:
            for i in range(piece.shape[0]):
                index = (gz ^ (place // row_count)) * row_count + (row ^ (place % row_count))
                columns[pl.ds(pl.multiple_of(index * few, few), few), :] = piece[i, 0, node]
                place += 1
        turned[...] = columns[...].T
        rows = [turned[pl.ds(step, tiles, stride=per_tile), :] for step in range(per_tile)]
        out[0, :, node, :] = jnp.concatenate(rows, axis=1)


def backward_out(pieces, before, first, nodes, row_count):
    levels, nodes, few, rows = pieces[0].shape[1:]
    tiles = rows * COLUMNS // LANES
    ready = [before] if before is not None else []
    return pl.pallas_call(
        functools.partial(backward_out_kernel, nodes, row_count, len(pieces)),
        grid=(levels,),
        out_shape=shape_of(4, tiles, nodes, LANES),
        in_specs=[
            pl.BlockSpec((piece.shape[0], 1, nodes, few, rows), lambda i: (0, i, 0, 0, 0))
            for piece in pieces
        ]
        + [HBM] * len(ready),
        out_specs=pl.BlockSpec((1, tiles, nodes, LANES), lambda i: (first + i, 0, 0, 0)),
        scratch_shapes=[pltpu.VMEM((COLUMNS, rows), F32), pltpu.VMEM((rows, COLUMNS), F32)],
        input_output_aliases={len(pieces): 0} if ready else {},
        compiler_params=PARAMS,
        name="backward_out",
    )(*pieces, *ready)


def body(
    right_side,
    layer_sums,
    lower_blocks,
    upper_blocks,
    lower_inverse,
    upper_diagonal_inverses,
    pattern,
    parents,
):
    nodes = right_side.shape[1]
    part = lower_blocks.shape[2]
    gz_count = lax.axis_size("gz")
    row_count = lax.axis_size("row")
    col_count = lax.axis_size("col")
    own = COLUMNS // gz_count
    lanes = nodes * own
    sizes = (nodes, part, own, row_count, col_count)
    gz = lax.axis_index("gz")

    def tiled(value):
        return value.reshape(4, nodes, part * COLUMNS // LANES, LANES).transpose(0, 2, 1, 3)

    parts = pl.pallas_call(
        functools.partial(input_kernel, gz_count, nodes, own),
        out_shape=[shape_of(4, part, lanes)] * gz_count,
        in_specs=[VMEM, VMEM],
        out_specs=[VMEM] * gz_count,
        compiler_params=STREAM_PARAMS,
        name="input_parts",
    )(tiled(right_side), tiled(layer_sums[0]))

    per = upper_blocks.shape[0] // gz_count
    upper_rows = lax.all_gather(
        lax.dynamic_slice_in_dim(upper_blocks, gz * per, per, 0), ("gz", "row")
    )
    m, z = prepare_step(lower_blocks, lower_inverse, upper_diagonal_inverses)

    initial = parts[0]
    for step in range(1, gz_count):
        pairs = [(i, i ^ step) for i in range(gz_count)]
        initial = initial + lax.ppermute(parts[step], "gz", pairs)

    fulls = [None] * 4
    pending = []
    mine = initial[3]
    for height in (3, 2, 1):
        pieces = gather(mine, row_steps(row_count))
        fulls[height], keep, send, pending = forward_step(
            height, pieces, parents, pattern, m, pending, sizes
        )
        for bit in range(bits_of(col_count)):
            taken = swap(send, "col", bit)
            half = keep.shape[0] // 2
            keep, send = keep[:half] + taken[:half] if half else keep + taken, (
                keep[half:] + taken[half:] if half else None
            )
        mine = initial[height - 1] - keep[0]
    fulls[0], solved = last_step(gather(mine, row_steps(row_count)), z, sizes)

    composed = compose_step(upper_rows, upper_diagonal_inverses, row_count)
    starts = [None] + [turn_step(height, fulls[height], z, sizes) for height in (1, 2, 3)]
    forward = solve_step(fulls, lower_inverse, own)
    forward_parts = [forward] + [
        lax.ppermute(forward, "gz", [(i, i ^ step) for i in range(gz_count)])
        for step in range(1, gz_count)
    ]
    whole = []
    for height in (1, 2, 3):
        whole.append(gather(solved, col_steps(col_count)))
        results = backward_step(height, parents, pattern, starts[height], composed, whole)
        solved = results[0]
        if height == 2:
            early = results[1]

    forward_all = forward_out(forward_parts, nodes, own)
    layer_steps = row_steps(row_count) + [("gz", bit) for bit in range(bits_of(gz_count))]
    backward_all = backward_out(gather(early, layer_steps), None, 0, nodes, row_count)
    late = gather(solved[None], layer_steps)
    backward_all = backward_out(late, backward_all, 3, nodes, row_count)
    return tuple(
        value.transpose(0, 2, 1, 3).reshape(4, nodes, WIDTH * COLUMNS)
        for value in (forward_all, backward_all)
    )


def solution(mesh):
    in_specs = (
        P(None, "col", "row"),
        P("gz", None, "col", "row"),
        P(None, "col", "row", None),
        P(None, "col", "row", None),
        P(None, "col", None, None),
        P(None, "col", None, None),
        P(None, "col"),
        P(),
    )
    out_specs = (P(None, "col", None), P(None, "col", None))
    return jax.shard_map(body, mesh=mesh, in_specs=in_specs, out_specs=out_specs, check_vma=False)
```

```python
import functools

import jax
import jax.numpy as jnp
from jax import lax
from jax.experimental import pallas as pl
from jax.experimental.pallas import tpu as pltpu
from jax.sharding import PartitionSpec as P

WIDTH = 256
COLUMNS = 64
LANES = 128
F32 = jnp.float32
BF16 = jnp.bfloat16
SPLIT = False
SMEM = pl.BlockSpec(memory_space=pltpu.SMEM)
VMEM = pl.BlockSpec(memory_space=pltpu.VMEM)
HBM = pl.BlockSpec(memory_space=pltpu.HBM)
PARAMS = pltpu.CompilerParams(vmem_limit_bytes=16 * 2**20)
STREAM_PARAMS = pltpu.CompilerParams(vmem_limit_bytes=53 * 2**20)


def place_of(height, distance):
    return height * (height - 1) // 2 + distance - 1


def shape_of(*dims, dtype=F32):
    return jax.ShapeDtypeStruct(dims, dtype)


def split(value):
    high = value.astype(BF16)
    return high, (value - high.astype(F32)).astype(BF16)


def dot(left, right):
    return jnp.dot(left, right, preferred_element_type=F32)


def dot_t(left, right):
    return lax.dot_general(left, right, (((1,), (1,)), ((), ())), preferred_element_type=F32)


def product(left, right):
    lanes = right[0].shape[1]
    both = dot(left[0], jnp.concatenate(right, axis=1))
    return both[:, :lanes] + both[:, lanes:] + dot(left[1], right[0])


def product_t(left, right):
    rows = left[0].shape[0]
    both = dot_t(jnp.concatenate(left, axis=0), right[0])
    return both[:rows] + both[rows:] + dot_t(left[0], right[1])


def steps_of(count):
    assert count & (count - 1) == 0
    return range(1, count)


def swap(value, axis, step):
    count = lax.axis_size(axis)
    gz_count = lax.axis_size("gz")
    cores = range(gz_count) if SPLIT else [gz_count - 1]
    pairs = [(g * count + i, g * count + (i ^ step)) for g in cores for i in range(count)]
    return lax.ppermute(value, ("gz", axis), pairs)


def swap_layers(value, step):
    return lax.ppermute(value, "gz", [(i, i ^ step) for i in range(lax.axis_size("gz"))])


def share_layers(value):
    gz_count = lax.axis_size("gz")
    if SPLIT:
        return [swap_layers(value, step) for step in steps_of(gz_count)]
    chief = gz_count - 1
    return [lax.ppermute(value, "gz", [(chief, chief ^ step)]) for step in steps_of(gz_count)]


def gather(value, axis):
    return [value] + [swap(value, axis, step) for step in steps_of(lax.axis_size(axis))]


def input_kernel(gz_count, nodes, own, right, layer, *outs):
    groups = COLUMNS // own
    kept, away, stage = outs[:4], outs[4:-1], outs[-1]
    gz = lax.axis_index("gz")
    tiles = right.shape[1]
    per_tile = LANES // COLUMNS
    block = lax.broadcasted_iota(jnp.int32, (1, LANES), 1) // own
    for level in range(right.shape[0]):
        for chunk in range(nodes * own // LANES):
            start = chunk * LANES
            lanes = slice(start, start + LANES)
            for row in range(per_tile):
                for which in range(groups):
                    mine = jnp.where(gz == (which if groups > 1 else gz_count - 1), 1.0, 0.0)
                    total = jnp.zeros((tiles, LANES), F32)
                    for node in range(start // own, (start + LANES) // own):
                        value = right[level, :, node, :] * mine - layer[level, :, node, :]
                        target = node * own - start
                        shift = (target - row * COLUMNS - which * own) % LANES
                        value = pltpu.roll(value, shift, 1) if shift else value
                        total = jnp.where(block == target // own, value, total)
                    stage[level, chunk, which, pl.ds(row, tiles, stride=per_tile), :] = total
            found = [stage[level, chunk, which] for which in range(groups)]
            for step in range(groups):
                chosen = found[0]
                for which in range(1, groups):
                    chosen = jnp.where((gz ^ step) == which, found[which], chosen)
                if step == 0:
                    kept[level][:, lanes] = chosen
                if step or groups == 1:
                    away[max(step - 1, 0)][level, :, lanes] = chosen


def lower_kernel(nodes, blocks, inverse, high_out, low_out, high, low):
    @pl.when(pl.program_id(0) == 0)
    def _():
        for node in range(nodes):
            high[node], low[node] = split(inverse[0, node])

    for node in range(nodes):
        high_out[0, node], low_out[0, node] = split(
            product(split(blocks[0, node]), (high[node], low[node]))
        )


def lower_step(height, blocks, inverse):
    nodes, part = blocks.shape[1:3]
    first = place_of(height, 1)
    out = shape_of(height, nodes, part, WIDTH, dtype=BF16)
    return pl.pallas_call(
        functools.partial(lower_kernel, nodes),
        grid=(height,),
        out_shape=[out, out],
        in_specs=[
            pl.BlockSpec((1, nodes, part, WIDTH), lambda i: (first + i, 0, 0, 0)),
            pl.BlockSpec((1, nodes, WIDTH, WIDTH), lambda i: (height, 0, 0, 0)),
        ],
        out_specs=[pl.BlockSpec((1, nodes, part, WIDTH), lambda i: (i, 0, 0, 0))] * 2,
        scratch_shapes=[pltpu.VMEM((nodes, WIDTH, WIDTH), BF16)] * 2,
        compiler_params=STREAM_PARAMS,
        name="lower_products",
    )(blocks, inverse)


def middle_kernel(nodes, upper, lower, high_out, low_out):
    for node in range(nodes):
        high_out[node], low_out[node] = split(product(split(upper[0, node]), split(lower[0, node])))


def middle_step(upper, lower):
    nodes = lower.shape[1]
    out = shape_of(nodes, WIDTH, WIDTH, dtype=BF16)
    level = pl.BlockSpec((1, nodes, WIDTH, WIDTH), lambda i: (0, 0, 0, 0))
    return pl.pallas_call(
        functools.partial(middle_kernel, nodes),
        grid=(1,),
        out_shape=[out, out],
        in_specs=[level, level],
        out_specs=[pl.BlockSpec((nodes, WIDTH, WIDTH), lambda i: (0, 0, 0))] * 2,
        compiler_params=STREAM_PARAMS,
        name="middle_product",
    )(upper, lower)


def assemble(pieces, full, part):
    row = lax.axis_index("row")
    for step, piece in enumerate(pieces):
        full[pl.ds(pl.multiple_of((row ^ step) * part, part), part), :] = piece[...]


def forward_kernel(height, sizes, *refs):
    nodes, part, own, row_count, col_count = sizes
    lanes = nodes * own
    pieces, refs = refs[:row_count], refs[row_count:]
    parents, pattern, m_high, m_low = refs[:4]
    pending_in = refs[4 : 4 + height] if height < 3 else ()
    refs = refs[4 + len(pending_in) :]
    full, sends = refs[0], refs[1 : 1 + col_count]
    pending_out = refs[1 + col_count : col_count + height]
    urgent = refs[-1]
    assemble(pieces, full, part)
    lane = lax.broadcasted_iota(jnp.int32, (1, lanes), 1) // own
    col = lax.axis_index("col")
    right = split(full[...])
    targets = []
    for level in range(height):
        target = urgent if level == height - 1 else pending_out[level]
        target[...] = pending_in[level][...] if pending_in else jnp.zeros(target.shape, F32)
        targets.append(target)
    for node in range(nodes):
        ancestor = col * nodes + node
        for distance in range(1, height + 1):
            level = height - distance
            ancestor = parents[level, ancestor]
            slot = lax.rem(ancestor, nodes)
            where = lax.div(ancestor, nodes) ^ col
            term = product((m_high[distance - 1, node], m_low[distance - 1, node]), right)
            term = pltpu.roll(term, lax.rem(slot - node + nodes, nodes) * own, 1)
            stored = jnp.where(pattern[place_of(height, distance), node] != 0, slot, -1)
            targets[level][where] += jnp.where(lane == stored, term, 0.0)
    for step in range(col_count):
        sends[step][...] = urgent[step]


def forward_step(height, pieces, parents, pattern, m, pending, sizes):
    nodes, part, own, row_count, col_count = sizes
    lanes = nodes * own
    piece = shape_of(part, lanes)
    stack = shape_of(col_count, part, lanes)
    out_shape = [shape_of(row_count * part, lanes)] + [piece] * col_count + [stack] * (height - 1)
    results = pl.pallas_call(
        functools.partial(forward_kernel, height, sizes),
        out_shape=out_shape,
        in_specs=[VMEM] * len(pieces) + [SMEM, SMEM] + [VMEM] * (2 + len(pending)),
        out_specs=[VMEM] * len(out_shape),
        scratch_shapes=[pltpu.VMEM(stack.shape, F32)],
        compiler_params=PARAMS,
        name="forward_level",
    )(*pieces, parents, pattern, *m, *pending)
    return results[0], results[1 : 1 + col_count], results[1 + col_count :]


def turn(value, turned, pair_of, out, own, row_count):
    turned[...] = value.T
    few = own // row_count
    row = lax.axis_index("row")
    for node in range(out.shape[0]):
        start = pl.multiple_of(node * own + row * few, few)
        out[node] = product_t(split(turned[pl.ds(start, few), :]), pair_of(node))


def last_kernel(sizes, *refs):
    nodes, part, own, row_count, col_count = sizes
    pieces = refs[:row_count]
    z_high, z_low, full, out, turned = refs[row_count:]
    assemble(pieces, full, part)
    turn(full[...], turned, lambda node: (z_high[node], z_low[node]), out, own, row_count)


def last_step(pieces, z, sizes):
    nodes, part, own, row_count, col_count = sizes
    lanes, rows = nodes * own, row_count * part
    return pl.pallas_call(
        functools.partial(last_kernel, sizes),
        out_shape=[shape_of(rows, lanes), shape_of(nodes, own // row_count, rows)],
        in_specs=[VMEM] * (len(pieces) + 2),
        out_specs=[VMEM] * 2,
        scratch_shapes=[pltpu.VMEM((lanes, rows), F32)],
        compiler_params=PARAMS,
        name="forward_last",
    )(*pieces, *z)


def solve_kernel(sizes, full, lower, *refs):
    nodes, part, own, row_count, col_count = sizes
    lane = lax.broadcasted_iota(jnp.int32, (1, nodes * own), 1) // own
    right = split(full[...])
    solved = jnp.zeros(full.shape, F32)
    for node in range(nodes):
        solved = jnp.where(lane == node, product(split(lower[0, node]), right), solved)
    if len(refs) == 1:
        refs[0][...] = solved
        return
    upper, out, start, turned = refs
    out[...] = solved
    turn(solved, turned, lambda node: split(upper[0, node]), start, own, row_count)


def solve_step(height, full, lower, upper, sizes):
    nodes, part, own, row_count, col_count = sizes
    rows, lanes = full.shape
    level = pl.BlockSpec((1, nodes, rows, rows), lambda i: (height, 0, 0, 0))
    whole = pl.BlockSpec((rows, lanes), lambda i: (0, 0))
    few = own // row_count
    more = height > 0
    return pl.pallas_call(
        functools.partial(solve_kernel, sizes),
        grid=(1,),
        out_shape=[shape_of(rows, lanes)] + [shape_of(nodes, few, rows)] * more,
        in_specs=[whole, level] + [level] * more,
        out_specs=[whole] + [pl.BlockSpec((nodes, few, rows), lambda i: (0, 0, 0))] * more,
        scratch_shapes=[pltpu.VMEM((lanes, rows), F32)] * more,
        compiler_params=STREAM_PARAMS,
        name="solve_level",
    )(full, lower, *([upper] * more))


def compose_kernel(nodes, gathered, inverse, high_out, low_out):
    for node in range(nodes):
        block = gathered[:, 0, node].reshape(WIDTH, WIDTH)
        whole = product(split(inverse[0, node]), split(block))
        high_out[0, node], low_out[0, node] = split(whole)


def compose_step(height, gathered, inverse, row_count):
    per, nodes, part = gathered.shape[1:4]
    first = place_of(height, 1)
    out = shape_of(height, nodes, WIDTH, WIDTH, dtype=BF16)
    out_spec = pl.BlockSpec((1, nodes, WIDTH, WIDTH), lambda i: (i, 0, 0, 0))
    return pl.pallas_call(
        functools.partial(compose_kernel, nodes),
        grid=(height,),
        out_shape=[out, out],
        in_specs=[
            pl.BlockSpec(
                (row_count, 1, nodes, part, WIDTH),
                lambda i: ((first + i) // per, (first + i) % per, 0, 0, 0),
            ),
            pl.BlockSpec((1, nodes, WIDTH, WIDTH), lambda i: (height, 0, 0, 0)),
        ],
        out_specs=[out_spec] * 2,
        compiler_params=STREAM_PARAMS,
        name="compose_level",
    )(gathered, inverse)


def backward_kernel(height, nodes, col_count, parents, pattern, start, high, low, *refs):
    pieces, out = refs[: height * col_count], refs[height * col_count]
    early = refs[height * col_count + 1] if height == 2 else None
    solved = refs[-1]
    for level in range(height):
        for step in range(col_count):
            solved[level, step] = pieces[level * col_count + step][...]
    col = lax.axis_index("col")
    for node in range(nodes):
        total = start[node]
        ancestor = col * nodes + node
        for distance in range(1, height + 1):
            level = height - distance
            ancestor = parents[level, ancestor]
            where = lax.div(ancestor, nodes) ^ col
            left = split(solved[level, where, lax.rem(ancestor, nodes)])
            term = product_t(left, (high[distance - 1, node], low[distance - 1, node]))
            stored = pattern[place_of(height, distance), node] != 0
            total = total - jnp.where(stored, term, 0.0)
        out[node] = total
        if early is not None:
            early[height, node] = total
    if early is not None:
        for level in range(height):
            early[level] = solved[level, 0]


def backward_step(height, parents, pattern, start, composed, solved):
    nodes = start.shape[0]
    col_count = lax.axis_size("col")
    pieces = [piece for level in solved for piece in level]
    outs = [start.shape] + ([(height + 1,) + start.shape] if height == 2 else [])
    return pl.pallas_call(
        functools.partial(backward_kernel, height, nodes, col_count),
        out_shape=[shape_of(*out) for out in outs],
        in_specs=[SMEM, SMEM] + [VMEM] * (3 + len(pieces)),
        out_specs=[VMEM] * len(outs),
        scratch_shapes=[pltpu.VMEM((height, col_count) + start.shape, F32)],
        compiler_params=PARAMS,
        name="backward_level",
    )(parents, pattern, start, *composed, *pieces)


def groups_found(found, groups):
    gz = lax.axis_index("gz")
    if groups == 1:
        others = found[1]
        for value in found[2:]:
            others = others + value
        return [jnp.where(gz == len(found) - 1, found[0], others)]
    values = []
    for which in range(groups):
        value = found[0]
        for step in range(1, groups):
            value = jnp.where((gz ^ step) == which, found[step], value)
        values.append(value)
    return values


def forward_out_kernel(gz_count, nodes, own, *refs):
    parts, out, stage = refs[:-2], refs[-2], refs[-1]
    groups = COLUMNS // own
    per_tile = LANES // COLUMNS
    tiles = out.shape[1]
    block = lax.broadcasted_iota(jnp.int32, (1, LANES), 1) // own
    for level in range(out.shape[0]):
        for chunk in range(nodes * own // LANES):
            start = chunk * LANES
            lanes = slice(start, start + LANES)
            found = [part[:, lanes] for part in parts[level * gz_count : (level + 1) * gz_count]]
            for which, value in enumerate(groups_found(found, groups)):
                stage[chunk, which] = value
            values = [
                stage[chunk, which, pl.ds(row, tiles, stride=per_tile), :]
                for row in range(per_tile)
                for which in range(groups)
            ]
            for node in range(start // own, (start + LANES) // own):
                total = jnp.zeros((tiles, LANES), F32)
                for place, value in enumerate(values):
                    shift = (place * own - (node * own - start)) % LANES
                    value = pltpu.roll(value, shift, 1) if shift else value
                    total = jnp.where(block == place, value, total)
                out[level, :, node, :] = total


def forward_out(parts, nodes, own, gz_count):
    rows, lanes = parts[0].shape
    tiles = rows * COLUMNS // LANES
    return pl.pallas_call(
        functools.partial(forward_out_kernel, gz_count, nodes, own),
        out_shape=shape_of(len(parts) // gz_count, tiles, nodes, LANES),
        in_specs=[VMEM] * len(parts),
        out_specs=VMEM,
        scratch_shapes=[pltpu.VMEM((lanes // LANES, COLUMNS // own, rows, LANES), F32)],
        compiler_params=PARAMS,
        name="forward_out",
    )(*parts)


def backward_out_kernel(nodes, gz_count, own, *refs):
    parts, (out, columns, turned) = refs[:gz_count], refs[-3:]
    groups = COLUMNS // own
    per_tile = LANES // COLUMNS
    tiles = out.shape[1]
    row_count, _, _, few, _ = parts[0].shape
    row = lax.axis_index("row")
    for node in range(nodes):
        for step in range(row_count):
            values = groups_found([part[step, 0, node] for part in parts], groups)
            for which, value in enumerate(values):
                index = which * row_count + (row ^ step)
                columns[pl.ds(pl.multiple_of(index * few, few), few), :] = value
        turned[...] = columns[...].T
        rows = [turned[pl.ds(step, tiles, stride=per_tile), :] for step in range(per_tile)]
        out[0, :, node, :] = jnp.concatenate(rows, axis=1)


def backward_out(parts, before, first, own):
    row_count, levels, nodes, few, rows = parts[0].shape
    tiles = rows * COLUMNS // LANES
    ready = [before] if before is not None else []
    return pl.pallas_call(
        functools.partial(backward_out_kernel, nodes, len(parts), own),
        grid=(levels,),
        out_shape=shape_of(4, tiles, nodes, LANES),
        in_specs=[
            pl.BlockSpec((row_count, 1, nodes, few, rows), lambda i: (0, i, 0, 0, 0))
            for part in parts
        ]
        + [HBM] * len(ready),
        out_specs=pl.BlockSpec((1, tiles, nodes, LANES), lambda i: (first + i, 0, 0, 0)),
        scratch_shapes=[pltpu.VMEM((COLUMNS, rows), F32), pltpu.VMEM((rows, COLUMNS), F32)],
        input_output_aliases={len(parts): 0} if ready else {},
        compiler_params=PARAMS,
        name="backward_out",
    )(*parts, *ready)


def layers_of(value):
    whole = jnp.stack(gather(value, "row"))
    return [whole] + share_layers(whole)


def body(
    right_side,
    layer_sums,
    lower_blocks,
    upper_blocks,
    lower_inverse,
    upper_diagonal_inverses,
    pattern,
    parents,
):
    nodes = right_side.shape[1]
    part = lower_blocks.shape[2]
    gz_count = lax.axis_size("gz")
    row_count = lax.axis_size("row")
    col_count = lax.axis_size("col")
    own = COLUMNS // gz_count if SPLIT else COLUMNS
    lanes = nodes * own
    sizes = (nodes, part, own, row_count, col_count)
    gz = lax.axis_index("gz")

    def tiled(value):
        return value.reshape(4, nodes, part * COLUMNS // LANES, LANES).transpose(0, 2, 1, 3)

    aways = gz_count - 1 if SPLIT else 1
    parts = pl.pallas_call(
        functools.partial(input_kernel, gz_count, nodes, own),
        out_shape=[shape_of(part, lanes)] * 4 + [shape_of(4, part, lanes)] * aways,
        in_specs=[VMEM, VMEM],
        out_specs=[VMEM] * (4 + aways),
        scratch_shapes=[pltpu.VMEM((4, lanes // LANES, COLUMNS // own, part, LANES), F32)],
        compiler_params=STREAM_PARAMS,
        name="input_parts",
    )(tiled(right_side), tiled(layer_sums[0]))
    kept, away = parts[:4], list(parts[4:])

    per = upper_blocks.shape[0] // gz_count
    later, away[0] = lax.optimization_barrier((upper_blocks, away[0]))
    upper_rows = lax.all_gather(
        lax.dynamic_slice_in_dim(later, gz * per, per, 0), ("gz", "row")
    )
    others = [swap_layers(away[min(step, aways) - 1], step) for step in steps_of(gz_count)]
    initial = [kept[level] + sum(other[level] for other in others) for level in range(4)]

    fulls = [None] * 4
    forward = [None] * 4
    starts = [None] * 4
    pending = []
    mine = initial[3]
    for height in (3, 2, 1):
        m = lower_step(height, lower_blocks, lower_inverse)
        fulls[height], sends, pending = forward_step(
            height, gather(mine, "row"), parents, pattern, m, pending, sizes
        )
        mine = initial[height - 1] - sends[0]
        for step in steps_of(col_count):
            mine = mine - swap(sends[step], "col", step)
    z = middle_step(upper_diagonal_inverses, lower_inverse)
    fulls[0], solved = last_step(gather(mine, "row"), z, sizes)

    for height in range(4):
        results = solve_step(height, fulls[height], lower_inverse, upper_diagonal_inverses, sizes)
        forward[height], starts[height] = results[0], results[-1]
    whole = []
    for height in (1, 2, 3):
        composed = compose_step(height, upper_rows, upper_diagonal_inverses, row_count)
        whole.append(gather(solved, "col"))
        results = backward_step(height, parents, pattern, starts[height], composed, whole)
        solved = results[0]
        if height == 2:
            early = results[1]

    forward_parts = []
    for value in forward:
        forward_parts += [value] + share_layers(value)
    forward_all = forward_out(forward_parts, nodes, own, gz_count)
    backward_all = backward_out(layers_of(early), None, 0, own)
    backward_all = backward_out(layers_of(solved[None]), backward_all, 3, own)
    return tuple(
        value.transpose(0, 2, 1, 3).reshape(4, nodes, WIDTH * COLUMNS)
        for value in (forward_all, backward_all)
    )


def solution(mesh):
    in_specs = (
        P(None, "col", "row"),
        P("gz", None, "col", "row"),
        P(None, "col", "row", None),
        P(None, "col", "row", None),
        P(None, "col", None, None),
        P(None, "col", None, None),
        P(None, "col"),
        P(),
    )
    out_specs = (P(None, "col", None), P(None, "col", None))
    return jax.shard_map(body, mesh=mesh, in_specs=in_specs, out_specs=out_specs, check_vma=False)
```

```python
import functools

import jax
import jax.numpy as jnp
from jax import lax
from jax.experimental import pallas as pl
from jax.experimental.pallas import tpu as pltpu
from jax.sharding import PartitionSpec as P

WIDTH = 256
COLUMNS = 64
LANES = 128
F32 = jnp.float32
BF16 = jnp.bfloat16
SPLIT = False
SMEM = pl.BlockSpec(memory_space=pltpu.SMEM)
VMEM = pl.BlockSpec(memory_space=pltpu.VMEM)
HBM = pl.BlockSpec(memory_space=pltpu.HBM)
PARAMS = pltpu.CompilerParams(vmem_limit_bytes=16 * 2**20)
STREAM_PARAMS = pltpu.CompilerParams(vmem_limit_bytes=53 * 2**20)


def place_of(height, distance):
    return height * (height - 1) // 2 + distance - 1


def shape_of(*dims, dtype=F32):
    return jax.ShapeDtypeStruct(dims, dtype)


def split(value):
    high = value.astype(BF16)
    return high, (value - high.astype(F32)).astype(BF16)


def dot(left, right):
    return jnp.dot(left, right, preferred_element_type=F32)


def dot_t(left, right):
    return lax.dot_general(left, right, (((1,), (1,)), ((), ())), preferred_element_type=F32)


def product(left, right):
    lanes = right[0].shape[1]
    both = dot(left[0], jnp.concatenate(right, axis=1))
    return both[:, :lanes] + both[:, lanes:] + dot(left[1], right[0])


def product_t(left, right):
    rows = left[0].shape[0]
    both = dot_t(jnp.concatenate(left, axis=0), right[0])
    return both[:rows] + both[rows:] + dot_t(left[0], right[1])


def steps_of(count):
    assert count & (count - 1) == 0
    return range(1, count)


def swap(value, axis, step):
    count = lax.axis_size(axis)
    gz_count = lax.axis_size("gz")
    cores = range(gz_count) if SPLIT else [gz_count - 1]
    pairs = [(g * count + i, g * count + (i ^ step)) for g in cores for i in range(count)]
    idle = range(gz_count * count - len(pairs))
    return lax.ppermute(value, ("gz", axis), pairs + [(i, i) for i in idle])


def swap_layers(value, step):
    return lax.ppermute(value, "gz", [(i, i ^ step) for i in range(lax.axis_size("gz"))])


def share_layers(value):
    gz_count = lax.axis_size("gz")
    if SPLIT:
        return [swap_layers(value, step) for step in steps_of(gz_count)]
    chief = gz_count - 1
    return [lax.ppermute(value, "gz", [(chief, chief ^ step)]) for step in steps_of(gz_count)]


def gather(value, axis):
    return [value] + [swap(value, axis, step) for step in steps_of(lax.axis_size(axis))]


def input_kernel(gz_count, nodes, own, right, layer, *outs):
    groups = COLUMNS // own
    kept, away, stage = outs[:4], outs[4:-1], outs[-1]
    gz = lax.axis_index("gz")
    tiles = right.shape[1]
    per_tile = LANES // COLUMNS
    block = lax.broadcasted_iota(jnp.int32, (1, LANES), 1) // own
    for level in range(right.shape[0]):
        for chunk in range(nodes * own // LANES):
            start = chunk * LANES
            lanes = slice(start, start + LANES)
            for row in range(per_tile):
                for which in range(groups):
                    mine = jnp.where(gz == (which if groups > 1 else gz_count - 1), 1.0, 0.0)
                    total = jnp.zeros((tiles, LANES), F32)
                    for node in range(start // own, (start + LANES) // own):
                        value = right[level, :, node, :] * mine - layer[level, :, node, :]
                        target = node * own - start
                        shift = (target - row * COLUMNS - which * own) % LANES
                        value = pltpu.roll(value, shift, 1) if shift else value
                        total = jnp.where(block == target // own, value, total)
                    stage[level, chunk, which, pl.ds(row, tiles, stride=per_tile), :] = total
            found = [stage[level, chunk, which] for which in range(groups)]
            for step in range(groups):
                chosen = found[0]
                for which in range(1, groups):
                    chosen = jnp.where((gz ^ step) == which, found[which], chosen)
                if step == 0:
                    kept[level][:, lanes] = chosen
                if step or groups == 1:
                    away[max(step - 1, 0)][level, :, lanes] = chosen


def lower_kernel(nodes, blocks, inverse, high_out, low_out, high, low):
    @pl.when(pl.program_id(0) == 0)
    def _():
        for node in range(nodes):
            high[node], low[node] = split(inverse[0, node])

    for node in range(nodes):
        high_out[0, node], low_out[0, node] = split(
            product(split(blocks[0, node]), (high[node], low[node]))
        )


def lower_step(height, blocks, inverse):
    nodes, part = blocks.shape[1:3]
    first = place_of(height, 1)
    out = shape_of(height, nodes, part, WIDTH, dtype=BF16)
    return pl.pallas_call(
        functools.partial(lower_kernel, nodes),
        grid=(height,),
        out_shape=[out, out],
        in_specs=[
            pl.BlockSpec((1, nodes, part, WIDTH), lambda i: (first + i, 0, 0, 0)),
            pl.BlockSpec((1, nodes, WIDTH, WIDTH), lambda i: (height, 0, 0, 0)),
        ],
        out_specs=[pl.BlockSpec((1, nodes, part, WIDTH), lambda i: (i, 0, 0, 0))] * 2,
        scratch_shapes=[pltpu.VMEM((nodes, WIDTH, WIDTH), BF16)] * 2,
        compiler_params=STREAM_PARAMS,
        name="lower_products",
    )(blocks, inverse)


def middle_kernel(nodes, upper, lower, high_out, low_out):
    for node in range(nodes):
        high_out[node], low_out[node] = split(product(split(upper[0, node]), split(lower[0, node])))


def middle_step(upper, lower):
    nodes = lower.shape[1]
    out = shape_of(nodes, WIDTH, WIDTH, dtype=BF16)
    level = pl.BlockSpec((1, nodes, WIDTH, WIDTH), lambda i: (0, 0, 0, 0))
    return pl.pallas_call(
        functools.partial(middle_kernel, nodes),
        grid=(1,),
        out_shape=[out, out],
        in_specs=[level, level],
        out_specs=[pl.BlockSpec((nodes, WIDTH, WIDTH), lambda i: (0, 0, 0))] * 2,
        compiler_params=STREAM_PARAMS,
        name="middle_product",
    )(upper, lower)


def assemble(pieces, full, part):
    row = lax.axis_index("row")
    for step, piece in enumerate(pieces):
        full[pl.ds(pl.multiple_of((row ^ step) * part, part), part), :] = piece[...]


def forward_kernel(height, sizes, *refs):
    nodes, part, own, row_count, col_count = sizes
    lanes = nodes * own
    pieces, refs = refs[:row_count], refs[row_count:]
    parents, pattern, m_high, m_low = refs[:4]
    pending_in = refs[4 : 4 + height] if height < 3 else ()
    refs = refs[4 + len(pending_in) :]
    full, sends = refs[0], refs[1 : 1 + col_count]
    pending_out = refs[1 + col_count : col_count + height]
    urgent = refs[-1]
    assemble(pieces, full, part)
    lane = lax.broadcasted_iota(jnp.int32, (1, lanes), 1) // own
    col = lax.axis_index("col")
    right = split(full[...])
    targets = []
    for level in range(height):
        target = urgent if level == height - 1 else pending_out[level]
        target[...] = pending_in[level][...] if pending_in else jnp.zeros(target.shape, F32)
        targets.append(target)
    for node in range(nodes):
        ancestor = col * nodes + node
        for distance in range(1, height + 1):
            level = height - distance
            ancestor = parents[level, ancestor]
            slot = lax.rem(ancestor, nodes)
            where = lax.div(ancestor, nodes) ^ col
            term = product((m_high[distance - 1, node], m_low[distance - 1, node]), right)
            term = pltpu.roll(term, lax.rem(slot - node + nodes, nodes) * own, 1)
            stored = jnp.where(pattern[place_of(height, distance), node] != 0, slot, -1)
            targets[level][where] += jnp.where(lane == stored, term, 0.0)
    for step in range(col_count):
        sends[step][...] = urgent[step]


def forward_step(height, pieces, parents, pattern, m, pending, sizes):
    nodes, part, own, row_count, col_count = sizes
    lanes = nodes * own
    piece = shape_of(part, lanes)
    stack = shape_of(col_count, part, lanes)
    out_shape = [shape_of(row_count * part, lanes)] + [piece] * col_count + [stack] * (height - 1)
    results = pl.pallas_call(
        functools.partial(forward_kernel, height, sizes),
        out_shape=out_shape,
        in_specs=[VMEM] * len(pieces) + [SMEM, SMEM] + [VMEM] * (2 + len(pending)),
        out_specs=[VMEM] * len(out_shape),
        scratch_shapes=[pltpu.VMEM(stack.shape, F32)],
        compiler_params=PARAMS,
        name="forward_level",
    )(*pieces, parents, pattern, *m, *pending)
    return results[0], results[1 : 1 + col_count], results[1 + col_count :]


def turn(value, turned, pair_of, out, own, row_count):
    turned[...] = value.T
    few = own // row_count
    row = lax.axis_index("row")
    for node in range(out.shape[0]):
        start = pl.multiple_of(node * own + row * few, few)
        out[node] = product_t(split(turned[pl.ds(start, few), :]), pair_of(node))


def last_kernel(sizes, *refs):
    nodes, part, own, row_count, col_count = sizes
    pieces = refs[:row_count]
    z_high, z_low, full, out, turned = refs[row_count:]
    assemble(pieces, full, part)
    turn(full[...], turned, lambda node: (z_high[node], z_low[node]), out, own, row_count)


def last_step(pieces, z, sizes):
    nodes, part, own, row_count, col_count = sizes
    lanes, rows = nodes * own, row_count * part
    return pl.pallas_call(
        functools.partial(last_kernel, sizes),
        out_shape=[shape_of(rows, lanes), shape_of(nodes, own // row_count, rows)],
        in_specs=[VMEM] * (len(pieces) + 2),
        out_specs=[VMEM] * 2,
        scratch_shapes=[pltpu.VMEM((lanes, rows), F32)],
        compiler_params=PARAMS,
        name="forward_last",
    )(*pieces, *z)


def solve_kernel(sizes, full, lower, *refs):
    nodes, part, own, row_count, col_count = sizes
    lane = lax.broadcasted_iota(jnp.int32, (1, nodes * own), 1) // own
    right = split(full[...])
    solved = jnp.zeros(full.shape, F32)
    for node in range(nodes):
        solved = jnp.where(lane == node, product(split(lower[0, node]), right), solved)
    if len(refs) == 1:
        refs[0][...] = solved
        return
    upper, out, start, turned = refs
    out[...] = solved
    turn(solved, turned, lambda node: split(upper[0, node]), start, own, row_count)


def solve_step(height, full, lower, upper, sizes):
    nodes, part, own, row_count, col_count = sizes
    rows, lanes = full.shape
    level = pl.BlockSpec((1, nodes, rows, rows), lambda i: (height, 0, 0, 0))
    whole = pl.BlockSpec((rows, lanes), lambda i: (0, 0))
    few = own // row_count
    more = height > 0
    return pl.pallas_call(
        functools.partial(solve_kernel, sizes),
        grid=(1,),
        out_shape=[shape_of(rows, lanes)] + [shape_of(nodes, few, rows)] * more,
        in_specs=[whole, level] + [level] * more,
        out_specs=[whole] + [pl.BlockSpec((nodes, few, rows), lambda i: (0, 0, 0))] * more,
        scratch_shapes=[pltpu.VMEM((lanes, rows), F32)] * more,
        compiler_params=STREAM_PARAMS,
        name="solve_level",
    )(full, lower, *([upper] * more))


def compose_kernel(nodes, gathered, inverse, high_out, low_out):
    for node in range(nodes):
        block = gathered[:, 0, node].reshape(WIDTH, WIDTH)
        whole = product(split(inverse[0, node]), split(block))
        high_out[0, node], low_out[0, node] = split(whole)


def compose_step(height, gathered, inverse, row_count):
    per, nodes, part = gathered.shape[1:4]
    first = place_of(height, 1)
    out = shape_of(height, nodes, WIDTH, WIDTH, dtype=BF16)
    out_spec = pl.BlockSpec((1, nodes, WIDTH, WIDTH), lambda i: (i, 0, 0, 0))
    return pl.pallas_call(
        functools.partial(compose_kernel, nodes),
        grid=(height,),
        out_shape=[out, out],
        in_specs=[
            pl.BlockSpec(
                (row_count, 1, nodes, part, WIDTH),
                lambda i: ((first + i) // per, (first + i) % per, 0, 0, 0),
            ),
            pl.BlockSpec((1, nodes, WIDTH, WIDTH), lambda i: (height, 0, 0, 0)),
        ],
        out_specs=[out_spec] * 2,
        compiler_params=STREAM_PARAMS,
        name="compose_level",
    )(gathered, inverse)


def backward_kernel(height, nodes, col_count, parents, pattern, start, high, low, *refs):
    pieces, out = refs[: height * col_count], refs[height * col_count]
    early = refs[height * col_count + 1] if height == 2 else None
    solved = refs[-1]
    for level in range(height):
        for step in range(col_count):
            solved[level, step] = pieces[level * col_count + step][...]
    col = lax.axis_index("col")
    for node in range(nodes):
        total = start[node]
        ancestor = col * nodes + node
        for distance in range(1, height + 1):
            level = height - distance
            ancestor = parents[level, ancestor]
            where = lax.div(ancestor, nodes) ^ col
            left = split(solved[level, where, lax.rem(ancestor, nodes)])
            term = product_t(left, (high[distance - 1, node], low[distance - 1, node]))
            stored = pattern[place_of(height, distance), node] != 0
            total = total - jnp.where(stored, term, 0.0)
        out[node] = total
        if early is not None:
            early[height, node] = total
    if early is not None:
        for level in range(height):
            early[level] = solved[level, 0]


def backward_step(height, parents, pattern, start, composed, solved):
    nodes = start.shape[0]
    col_count = lax.axis_size("col")
    pieces = [piece for level in solved for piece in level]
    outs = [start.shape] + ([(height + 1,) + start.shape] if height == 2 else [])
    return pl.pallas_call(
        functools.partial(backward_kernel, height, nodes, col_count),
        out_shape=[shape_of(*out) for out in outs],
        in_specs=[SMEM, SMEM] + [VMEM] * (3 + len(pieces)),
        out_specs=[VMEM] * len(outs),
        scratch_shapes=[pltpu.VMEM((height, col_count) + start.shape, F32)],
        compiler_params=PARAMS,
        name="backward_level",
    )(parents, pattern, start, *composed, *pieces)


def groups_found(found, groups):
    gz = lax.axis_index("gz")
    if groups == 1:
        others = found[1]
        for value in found[2:]:
            others = others + value
        return [jnp.where(gz == len(found) - 1, found[0], others)]
    values = []
    for which in range(groups):
        value = found[0]
        for step in range(1, groups):
            value = jnp.where((gz ^ step) == which, found[step], value)
        values.append(value)
    return values


def forward_out_kernel(gz_count, nodes, own, *refs):
    parts, out, stage = refs[:-2], refs[-2], refs[-1]
    groups = COLUMNS // own
    per_tile = LANES // COLUMNS
    tiles = out.shape[1]
    block = lax.broadcasted_iota(jnp.int32, (1, LANES), 1) // own
    for level in range(out.shape[0]):
        for chunk in range(nodes * own // LANES):
            start = chunk * LANES
            lanes = slice(start, start + LANES)
            found = [part[:, lanes] for part in parts[level * gz_count : (level + 1) * gz_count]]
            for which, value in enumerate(groups_found(found, groups)):
                stage[chunk, which] = value
            values = [
                stage[chunk, which, pl.ds(row, tiles, stride=per_tile), :]
                for row in range(per_tile)
                for which in range(groups)
            ]
            for node in range(start // own, (start + LANES) // own):
                total = jnp.zeros((tiles, LANES), F32)
                for place, value in enumerate(values):
                    shift = (place * own - (node * own - start)) % LANES
                    value = pltpu.roll(value, shift, 1) if shift else value
                    total = jnp.where(block == place, value, total)
                out[level, :, node, :] = total


def forward_out(parts, nodes, own, gz_count):
    rows, lanes = parts[0].shape
    tiles = rows * COLUMNS // LANES
    return pl.pallas_call(
        functools.partial(forward_out_kernel, gz_count, nodes, own),
        out_shape=shape_of(len(parts) // gz_count, tiles, nodes, LANES),
        in_specs=[VMEM] * len(parts),
        out_specs=VMEM,
        scratch_shapes=[pltpu.VMEM((lanes // LANES, COLUMNS // own, rows, LANES), F32)],
        compiler_params=PARAMS,
        name="forward_out",
    )(*parts)


def backward_out_kernel(nodes, gz_count, own, *refs):
    parts, (out, columns, turned) = refs[:gz_count], refs[-3:]
    groups = COLUMNS // own
    per_tile = LANES // COLUMNS
    tiles = out.shape[1]
    row_count, _, _, few, _ = parts[0].shape
    row = lax.axis_index("row")
    for node in range(nodes):
        for step in range(row_count):
            values = groups_found([part[step, 0, node] for part in parts], groups)
            for which, value in enumerate(values):
                index = which * row_count + (row ^ step)
                columns[pl.ds(pl.multiple_of(index * few, few), few), :] = value
        turned[...] = columns[...].T
        rows = [turned[pl.ds(step, tiles, stride=per_tile), :] for step in range(per_tile)]
        out[0, :, node, :] = jnp.concatenate(rows, axis=1)


def backward_out(parts, before, first, own):
    row_count, levels, nodes, few, rows = parts[0].shape
    tiles = rows * COLUMNS // LANES
    ready = [before] if before is not None else []
    return pl.pallas_call(
        functools.partial(backward_out_kernel, nodes, len(parts), own),
        grid=(levels,),
        out_shape=shape_of(4, tiles, nodes, LANES),
        in_specs=[
            pl.BlockSpec((row_count, 1, nodes, few, rows), lambda i: (0, i, 0, 0, 0))
            for part in parts
        ]
        + [HBM] * len(ready),
        out_specs=pl.BlockSpec((1, tiles, nodes, LANES), lambda i: (first + i, 0, 0, 0)),
        scratch_shapes=[pltpu.VMEM((COLUMNS, rows), F32), pltpu.VMEM((rows, COLUMNS), F32)],
        input_output_aliases={len(parts): 0} if ready else {},
        compiler_params=PARAMS,
        name="backward_out",
    )(*parts, *ready)


def layers_of(value):
    whole = jnp.stack(gather(value, "row"))
    return [whole] + share_layers(whole)


def body(
    right_side,
    layer_sums,
    lower_blocks,
    upper_blocks,
    lower_inverse,
    upper_diagonal_inverses,
    pattern,
    parents,
):
    nodes = right_side.shape[1]
    part = lower_blocks.shape[2]
    gz_count = lax.axis_size("gz")
    row_count = lax.axis_size("row")
    col_count = lax.axis_size("col")
    own = COLUMNS // gz_count if SPLIT else COLUMNS
    lanes = nodes * own
    sizes = (nodes, part, own, row_count, col_count)
    gz = lax.axis_index("gz")

    def tiled(value):
        return value.reshape(4, nodes, part * COLUMNS // LANES, LANES).transpose(0, 2, 1, 3)

    aways = gz_count - 1 if SPLIT else 1
    parts = pl.pallas_call(
        functools.partial(input_kernel, gz_count, nodes, own),
        out_shape=[shape_of(part, lanes)] * 4 + [shape_of(4, part, lanes)] * aways,
        in_specs=[VMEM, VMEM],
        out_specs=[VMEM] * (4 + aways),
        scratch_shapes=[pltpu.VMEM((4, lanes // LANES, COLUMNS // own, part, LANES), F32)],
        compiler_params=STREAM_PARAMS,
        name="input_parts",
    )(tiled(right_side), tiled(layer_sums[0]))
    kept, away = parts[:4], list(parts[4:])

    per = upper_blocks.shape[0] // gz_count
    later, away[0] = lax.optimization_barrier((upper_blocks, away[0]))
    upper_rows = lax.all_gather(
        lax.dynamic_slice_in_dim(later, gz * per, per, 0), ("gz", "row")
    )
    others = [swap_layers(away[min(step, aways) - 1], step) for step in steps_of(gz_count)]
    initial = [kept[level] + sum(other[level] for other in others) for level in range(4)]

    fulls = [None] * 4
    forward = [None] * 4
    starts = [None] * 4
    pending = []
    mine = initial[3]
    for height in (3, 2, 1):
        m = lower_step(height, lower_blocks, lower_inverse)
        fulls[height], sends, pending = forward_step(
            height, gather(mine, "row"), parents, pattern, m, pending, sizes
        )
        mine = initial[height - 1] - sends[0]
        for step in steps_of(col_count):
            mine = mine - swap(sends[step], "col", step)
    z = middle_step(upper_diagonal_inverses, lower_inverse)
    fulls[0], solved = last_step(gather(mine, "row"), z, sizes)

    for height in range(4):
        results = solve_step(height, fulls[height], lower_inverse, upper_diagonal_inverses, sizes)
        forward[height], starts[height] = results[0], results[-1]
    whole = []
    for height in (1, 2, 3):
        composed = compose_step(height, upper_rows, upper_diagonal_inverses, row_count)
        whole.append(gather(solved, "col"))
        results = backward_step(height, parents, pattern, starts[height], composed, whole)
        solved = results[0]
        if height == 2:
            early = results[1]

    forward_parts = []
    for value in forward:
        forward_parts += [value] + share_layers(value)
    forward_all = forward_out(forward_parts, nodes, own, gz_count)
    backward_all = backward_out(layers_of(early), None, 0, own)
    backward_all = backward_out(layers_of(solved[None]), backward_all, 3, own)
    return tuple(
        value.transpose(0, 2, 1, 3).reshape(4, nodes, WIDTH * COLUMNS)
        for value in (forward_all, backward_all)
    )


def solution(mesh):
    in_specs = (
        P(None, "col", "row"),
        P("gz", None, "col", "row"),
        P(None, "col", "row", None),
        P(None, "col", "row", None),
        P(None, "col", None, None),
        P(None, "col", None, None),
        P(None, "col"),
        P(),
    )
    out_specs = (P(None, "col", None), P(None, "col", None))
    return jax.shard_map(body, mesh=mesh, in_specs=in_specs, out_specs=out_specs, check_vma=False)
```

```python
import functools

import jax
import jax.numpy as jnp
from jax import lax
from jax.experimental import pallas as pl
from jax.experimental.pallas import tpu as pltpu
from jax.sharding import PartitionSpec as P

WIDTH = 256
COLUMNS = 64
LANES = 128
F32 = jnp.float32
BF16 = jnp.bfloat16
SMEM = pl.BlockSpec(memory_space=pltpu.SMEM)
VMEM = pl.BlockSpec(memory_space=pltpu.VMEM)
HBM = pl.BlockSpec(memory_space=pltpu.HBM)
PARAMS = pltpu.CompilerParams(vmem_limit_bytes=16 * 2**20)
STREAM_PARAMS = pltpu.CompilerParams(vmem_limit_bytes=52 * 2**20)


def place_of(height, distance):
    return height * (height - 1) // 2 + distance - 1


def shape_of(*dims, dtype=F32):
    return jax.ShapeDtypeStruct(dims, dtype)


def split(value):
    high = value.astype(BF16)
    return high, (value - high.astype(F32)).astype(BF16)


def dot(left, right):
    return jnp.dot(left, right, preferred_element_type=F32)


def dot_t(left, right):
    return lax.dot_general(left, right, (((1,), (1,)), ((), ())), preferred_element_type=F32)


def product(left, right):
    lanes = right[0].shape[1]
    both = dot(left[0], jnp.concatenate(right, axis=1))
    return both[:, :lanes] + both[:, lanes:] + dot(left[1], right[0])


def product_t(left, right):
    rows = left[0].shape[0]
    both = dot_t(jnp.concatenate(left, axis=0), right[0])
    return both[:rows] + both[rows:] + dot_t(left[0], right[1])


def steps_of(count):
    assert count & (count - 1) == 0
    return range(1, count)


def swap(value, axis, step):
    return lax.ppermute(value, axis, [(i, i ^ step) for i in range(lax.axis_size(axis))])


def with_layers(value):
    return [value] + [swap(value, "gz", step) for step in steps_of(lax.axis_size("gz"))]


def after(value, *others):
    return lax.optimization_barrier((value, *others))[0]


def gather(value, axis):
    return [value] + [swap(value, axis, step) for step in steps_of(lax.axis_size(axis))]


def input_kernel(gz_count, nodes, own, right, layer, *outs):
    groups = COLUMNS // own
    kept, away, stage = outs[:4], outs[4:-1], outs[-1]
    gz = lax.axis_index("gz")
    tiles = right.shape[1]
    per_tile = LANES // COLUMNS
    block = lax.broadcasted_iota(jnp.int32, (1, LANES), 1) // own
    for level in range(right.shape[0]):
        for chunk in range(nodes * own // LANES):
            start = chunk * LANES
            lanes = slice(start, start + LANES)
            for row in range(per_tile):
                for which in range(groups):
                    mine = jnp.where(gz == which, 1.0, 0.0)
                    total = jnp.zeros((tiles, LANES), F32)
                    for node in range(start // own, (start + LANES) // own):
                        value = right[level, :, node, :] * mine - layer[level, :, node, :]
                        target = node * own - start
                        shift = (target - row * COLUMNS - which * own) % LANES
                        value = pltpu.roll(value, shift, 1) if shift else value
                        total = jnp.where(block == target // own, value, total)
                    stage[level, chunk, which, pl.ds(row, tiles, stride=per_tile), :] = total
            found = [stage[level, chunk, which] for which in range(groups)]
            for step in range(groups):
                chosen = found[0]
                for which in range(1, groups):
                    chosen = jnp.where((gz ^ step) == which, found[which], chosen)
                if step == 0:
                    kept[level][:, lanes] = chosen
                else:
                    away[step - 1][level, :, lanes] = chosen


def lower_kernel(height, blocks, inverse, high_out, low_out):
    first = place_of(height, 1)
    part, width = blocks.shape[2:]
    left = blocks[first : first + height, 0].reshape(height * part, width)
    whole = product(split(left), split(inverse[0, 0])).reshape(height, part, width)
    high_out[:, 0], low_out[:, 0] = split(whole)


def lower_step(height, blocks, inverse):
    pairs, nodes, part = blocks.shape[:3]
    out = shape_of(height, nodes, part, WIDTH, dtype=BF16)
    return pl.pallas_call(
        functools.partial(lower_kernel, height),
        grid=(nodes,),
        out_shape=[out, out],
        in_specs=[
            pl.BlockSpec((pairs, 1, part, WIDTH), lambda i: (0, i, 0, 0)),
            pl.BlockSpec((1, 1, WIDTH, WIDTH), lambda i: (height, i, 0, 0)),
        ],
        out_specs=[pl.BlockSpec((height, 1, part, WIDTH), lambda i: (0, i, 0, 0))] * 2,
        compiler_params=STREAM_PARAMS,
        name="lower_products",
    )(blocks, inverse)


def middle_kernel(upper, lower, high_out, low_out):
    high_out[0], low_out[0] = split(product(split(upper[0, 0]), split(lower[0, 0])))


def middle_step(upper, lower):
    nodes = lower.shape[1]
    out = shape_of(nodes, WIDTH, WIDTH, dtype=BF16)
    return pl.pallas_call(
        middle_kernel,
        grid=(nodes,),
        out_shape=[out, out],
        in_specs=[pl.BlockSpec((1, 1, WIDTH, WIDTH), lambda i: (0, i, 0, 0))] * 2,
        out_specs=[pl.BlockSpec((1, WIDTH, WIDTH), lambda i: (i, 0, 0))] * 2,
        compiler_params=STREAM_PARAMS,
        name="middle_product",
    )(upper, lower)


def assemble(pieces, full, part):
    row = lax.axis_index("row")
    for step, piece in enumerate(pieces):
        full[pl.ds(pl.multiple_of((row ^ step) * part, part), part), :] = piece[...]


def forward_kernel(height, sizes, *refs):
    nodes, part, own, row_count, col_count = sizes
    lanes = nodes * own
    pieces, refs = refs[:row_count], refs[row_count:]
    parents, pattern, m_high, m_low = refs[:4]
    pending_in = refs[4 : 4 + height] if height < 3 else ()
    refs = refs[4 + len(pending_in) :]
    full, sends = refs[0], refs[1 : 1 + col_count]
    pending_out = refs[1 + col_count : col_count + height]
    urgent = refs[-1]
    assemble(pieces, full, part)
    lane = lax.broadcasted_iota(jnp.int32, (1, lanes), 1) // own
    col = lax.axis_index("col")
    right = split(full[...])
    targets = []
    for level in range(height):
        target = urgent if level == height - 1 else pending_out[level]
        target[...] = pending_in[level][...] if pending_in else jnp.zeros(target.shape, F32)
        targets.append(target)
    for node in range(nodes):
        ancestor = col * nodes + node
        for distance in range(1, height + 1):
            level = height - distance
            ancestor = parents[level, ancestor]
            slot = lax.rem(ancestor, nodes)
            where = lax.div(ancestor, nodes) ^ col
            term = product((m_high[distance - 1, node], m_low[distance - 1, node]), right)
            term = pltpu.roll(term, lax.rem(slot - node + nodes, nodes) * own, 1)
            stored = jnp.where(pattern[place_of(height, distance), node] != 0, slot, -1)
            targets[level][where] += jnp.where(lane == stored, term, 0.0)
    for step in range(col_count):
        sends[step][...] = urgent[step]


def forward_step(height, pieces, parents, pattern, m, pending, sizes):
    nodes, part, own, row_count, col_count = sizes
    lanes = nodes * own
    piece = shape_of(part, lanes)
    stack = shape_of(col_count, part, lanes)
    out_shape = [shape_of(row_count * part, lanes)] + [piece] * col_count + [stack] * (height - 1)
    results = pl.pallas_call(
        functools.partial(forward_kernel, height, sizes),
        out_shape=out_shape,
        in_specs=[VMEM] * len(pieces) + [SMEM, SMEM] + [VMEM] * (2 + len(pending)),
        out_specs=[VMEM] * len(out_shape),
        scratch_shapes=[pltpu.VMEM(stack.shape, F32)],
        compiler_params=PARAMS,
        name="forward_level",
    )(*pieces, parents, pattern, *m, *pending)
    return results[0], results[1 : 1 + col_count], results[1 + col_count :]


def own_rows(turned, node, own, row_count):
    few = own // row_count
    start = node * own + lax.axis_index("row") * few
    return turned[pl.ds(pl.multiple_of(start, few), few), :]


def last_kernel(sizes, *refs):
    nodes, part, own, row_count, col_count = sizes
    pieces = refs[:row_count]
    z_high, z_low, full, out, turned = refs[row_count:]
    assemble(pieces, full, part)
    turned[...] = full[...].T
    for node in range(nodes):
        left = split(own_rows(turned, node, own, row_count))
        out[node] = product_t(left, (z_high[node], z_low[node]))


def last_step(pieces, z, sizes):
    nodes, part, own, row_count, col_count = sizes
    lanes, rows = nodes * own, row_count * part
    return pl.pallas_call(
        functools.partial(last_kernel, sizes),
        out_shape=[shape_of(rows, lanes), shape_of(nodes, own // row_count, rows)],
        in_specs=[VMEM] * (len(pieces) + 2),
        out_specs=[VMEM] * 2,
        scratch_shapes=[pltpu.VMEM((lanes, rows), F32)],
        compiler_params=PARAMS,
        name="forward_last",
    )(*pieces, *z)


def solve_kernel(sizes, full, lower, out, own_out, turned):
    nodes, part, own, row_count, col_count = sizes
    node = pl.program_id(0)
    lane = lax.broadcasted_iota(jnp.int32, (1, nodes * own), 1) // own

    @pl.when(node == 0)
    def _():
        turned[...] = full[...].T
        out[...] = jnp.zeros(out.shape, F32)

    inverse = split(lower[0, 0])
    out[...] = jnp.where(lane == node, product(inverse, split(full[...])), out[...])
    own_out[0] = product_t(split(own_rows(turned, node, own, row_count)), inverse)


def solve_step(height, full, lower, sizes):
    nodes, part, own, row_count, col_count = sizes
    rows, lanes = full.shape
    few = own // row_count
    whole = pl.BlockSpec((rows, lanes), lambda i: (0, 0))
    return pl.pallas_call(
        functools.partial(solve_kernel, sizes),
        grid=(nodes,),
        out_shape=[shape_of(rows, lanes), shape_of(nodes, few, rows)],
        in_specs=[whole, pl.BlockSpec((1, 1, rows, rows), lambda i: (height, i, 0, 0))],
        out_specs=[whole, pl.BlockSpec((1, few, rows), lambda i: (i, 0, 0))],
        scratch_shapes=[pltpu.VMEM((lanes, rows), F32)],
        compiler_params=STREAM_PARAMS,
        name="solve_level",
    )(full, lower)


def start_kernel(height, nodes, col_count, parents, pattern, value, inverse, *refs):
    blocks, pieces, out = refs[: height - 1], refs[height - 1 : -1], refs[-1]
    col = lax.axis_index("col")
    node = pl.program_id(0)
    rest = value[0]
    ancestor = parents[height - 1, col * nodes + node]
    for distance in range(2, height + 1):
        level = height - distance
        ancestor = parents[level, ancestor]
        where = lax.div(ancestor, nodes) ^ col
        slot = lax.rem(ancestor, nodes)
        chosen = pieces[level * col_count][slot]
        for step in range(1, col_count):
            piece = pieces[level * col_count + step][slot]
            chosen = jnp.where(where == step, piece, chosen)
        block = blocks[distance - 2][:, 0, 0].reshape(WIDTH, WIDTH)
        term = product_t(split(chosen), split(block))
        stored = pattern[place_of(height, distance), node] != 0
        rest = rest - jnp.where(stored, term, 0.0)
    out[0] = product_t(split(rest), split(inverse[0, 0]))


def start_step(height, parents, pattern, value, gathered, inverse, solved, row_count):
    per, nodes, part = gathered.shape[1:4]
    col_count = lax.axis_size("col")
    few, rows = value.shape[1:]
    pieces = [piece for level in solved for piece in level]

    def block_spec(distance):
        place = place_of(height, distance)
        return pl.BlockSpec(
            (row_count, 1, 1, part, WIDTH), lambda i: (place // per, place % per, i, 0, 0)
        )

    each = pl.BlockSpec((1, few, rows), lambda i: (i, 0, 0))
    whole = pl.BlockSpec((nodes, few, rows), lambda i: (0, 0, 0))
    return pl.pallas_call(
        functools.partial(start_kernel, height, nodes, col_count),
        grid=(nodes,),
        out_shape=shape_of(nodes, few, rows),
        in_specs=[SMEM, SMEM, each]
        + [pl.BlockSpec((1, 1, WIDTH, WIDTH), lambda i: (height, i, 0, 0))]
        + [block_spec(distance) for distance in range(2, height + 1)]
        + [whole] * len(pieces),
        out_specs=each,
        compiler_params=STREAM_PARAMS,
        name="start_level",
    )(parents, pattern, value, inverse, *([gathered] * (height - 1)), *pieces)


def compose_kernel(gathered, inverse, high_out, low_out):
    block = gathered[:, 0, 0].reshape(WIDTH, WIDTH)
    high_out[0], low_out[0] = split(product(split(inverse[0, 0]), split(block)))


def compose_step(height, gathered, inverse, row_count):
    per, nodes, part = gathered.shape[1:4]
    place = place_of(height, 1)
    out = shape_of(nodes, WIDTH, WIDTH, dtype=BF16)
    return pl.pallas_call(
        compose_kernel,
        grid=(nodes,),
        out_shape=[out, out],
        in_specs=[
            pl.BlockSpec(
                (row_count, 1, 1, part, WIDTH), lambda i: (place // per, place % per, i, 0, 0)
            ),
            pl.BlockSpec((1, 1, WIDTH, WIDTH), lambda i: (height, i, 0, 0)),
        ],
        out_specs=[pl.BlockSpec((1, WIDTH, WIDTH), lambda i: (i, 0, 0))] * 2,
        compiler_params=STREAM_PARAMS,
        name="compose_level",
    )(gathered, inverse)


def backward_kernel(height, nodes, parents, pattern, start, high, low, *refs):
    pieces, out, solved = refs[:-2], refs[-2], refs[-1]
    for step, piece in enumerate(pieces):
        solved[step] = piece[...]
    col = lax.axis_index("col")
    for node in range(nodes):
        ancestor = parents[height - 1, col * nodes + node]
        where = lax.div(ancestor, nodes) ^ col
        left = split(solved[where, lax.rem(ancestor, nodes)])
        term = product_t(left, (high[node], low[node]))
        stored = pattern[place_of(height, 1), node] != 0
        out[node] = start[node] - jnp.where(stored, term, 0.0)


def backward_step(height, parents, pattern, start, composed, pieces):
    return pl.pallas_call(
        functools.partial(backward_kernel, height, start.shape[0]),
        out_shape=shape_of(*start.shape),
        in_specs=[SMEM, SMEM] + [VMEM] * (3 + len(pieces)),
        out_specs=VMEM,
        scratch_shapes=[pltpu.VMEM((len(pieces),) + start.shape, F32)],
        compiler_params=PARAMS,
        name="backward_level",
    )(parents, pattern, start, *composed, *pieces)


def groups_found(found, groups):
    gz = lax.axis_index("gz")
    values = []
    for which in range(groups):
        value = found[0]
        for step in range(1, groups):
            value = jnp.where((gz ^ step) == which, found[step], value)
        values.append(value)
    return values


def forward_out_kernel(gz_count, nodes, own, *refs):
    parts, out, stage = refs[:-2], refs[-2], refs[-1]
    groups = COLUMNS // own
    per_tile = LANES // COLUMNS
    tiles = out.shape[1]
    block = lax.broadcasted_iota(jnp.int32, (1, LANES), 1) // own
    for level in range(out.shape[0]):
        for chunk in range(nodes * own // LANES):
            start = chunk * LANES
            lanes = slice(start, start + LANES)
            found = [part[:, lanes] for part in parts[level * gz_count : (level + 1) * gz_count]]
            for which, value in enumerate(groups_found(found, groups)):
                stage[chunk, which] = value
            values = [
                stage[chunk, which, pl.ds(row, tiles, stride=per_tile), :]
                for row in range(per_tile)
                for which in range(groups)
            ]
            for node in range(start // own, (start + LANES) // own):
                total = jnp.zeros((tiles, LANES), F32)
                for place, value in enumerate(values):
                    shift = (place * own - (node * own - start)) % LANES
                    value = pltpu.roll(value, shift, 1) if shift else value
                    total = jnp.where(block == place, value, total)
                out[level, :, node, :] = total


def forward_out(parts, nodes, own, gz_count):
    rows, lanes = parts[0].shape
    tiles = rows * COLUMNS // LANES
    return pl.pallas_call(
        functools.partial(forward_out_kernel, gz_count, nodes, own),
        out_shape=shape_of(len(parts) // gz_count, tiles, nodes, LANES),
        in_specs=[VMEM] * len(parts),
        out_specs=VMEM,
        scratch_shapes=[pltpu.VMEM((lanes // LANES, COLUMNS // own, rows, LANES), F32)],
        compiler_params=PARAMS,
        name="forward_out",
    )(*parts)


def backward_out_kernel(nodes, gz_count, own, *refs):
    parts, (out, columns, turned) = refs[:gz_count], refs[-3:]
    groups = COLUMNS // own
    per_tile = LANES // COLUMNS
    tiles = out.shape[1]
    row_count, _, _, few, _ = parts[0].shape
    row = lax.axis_index("row")
    for node in range(nodes):
        for step in range(row_count):
            values = groups_found([part[step, 0, node] for part in parts], groups)
            for which, value in enumerate(values):
                index = which * row_count + (row ^ step)
                columns[pl.ds(pl.multiple_of(index * few, few), few), :] = value
        turned[...] = columns[...].T
        rows = [turned[pl.ds(step, tiles, stride=per_tile), :] for step in range(per_tile)]
        out[0, :, node, :] = jnp.concatenate(rows, axis=1)


def backward_out(parts, before, first, own):
    row_count, levels, nodes, few, rows = parts[0].shape
    tiles = rows * COLUMNS // LANES
    ready = [before] if before is not None else []
    return pl.pallas_call(
        functools.partial(backward_out_kernel, nodes, len(parts), own),
        grid=(levels,),
        out_shape=shape_of(4, tiles, nodes, LANES),
        in_specs=[
            pl.BlockSpec((row_count, 1, nodes, few, rows), lambda i: (0, i, 0, 0, 0))
            for part in parts
        ]
        + [HBM] * len(ready),
        out_specs=pl.BlockSpec((1, tiles, nodes, LANES), lambda i: (first + i, 0, 0, 0)),
        scratch_shapes=[pltpu.VMEM((COLUMNS, rows), F32), pltpu.VMEM((rows, COLUMNS), F32)],
        input_output_aliases={len(parts): 0} if ready else {},
        compiler_params=PARAMS,
        name="backward_out",
    )(*parts, *ready)


def layers_of(value):
    return with_layers(jnp.stack(gather(value, "row")))


def body(
    right_side,
    layer_sums,
    lower_blocks,
    upper_blocks,
    lower_inverse,
    upper_diagonal_inverses,
    pattern,
    parents,
):
    nodes = right_side.shape[1]
    part = lower_blocks.shape[2]
    gz_count = lax.axis_size("gz")
    row_count = lax.axis_size("row")
    col_count = lax.axis_size("col")
    own = COLUMNS // gz_count
    lanes = nodes * own
    sizes = (nodes, part, own, row_count, col_count)
    gz = lax.axis_index("gz")

    def tiled(value):
        return value.reshape(4, nodes, part * COLUMNS // LANES, LANES).transpose(0, 2, 1, 3)

    parts = pl.pallas_call(
        functools.partial(input_kernel, gz_count, nodes, own),
        out_shape=[shape_of(part, lanes)] * 4 + [shape_of(4, part, lanes)] * (gz_count - 1),
        in_specs=[VMEM, VMEM],
        out_specs=[VMEM] * (3 + gz_count),
        scratch_shapes=[pltpu.VMEM((4, lanes // LANES, COLUMNS // own, part, LANES), F32)],
        compiler_params=STREAM_PARAMS,
        name="input_parts",
    )(tiled(right_side), tiled(layer_sums[0]))
    kept, away = parts[:4], parts[4:]

    per = upper_blocks.shape[0] // gz_count
    half = lax.dynamic_slice_in_dim(after(upper_blocks, *away), gz * per, per, 0)
    upper_rows = lax.all_gather(half, ("gz", "row"))
    others = [swap(away[step - 1], "gz", step) for step in steps_of(gz_count)]
    initial = [kept[level] + sum(other[level] for other in others) for level in range(4)]

    fulls = [None] * 4
    forward = [None] * 4
    pending = []
    mine = initial[3]
    m = lower_step(3, lower_blocks, lower_inverse)
    for height in (3, 2, 1):
        pieces = gather(mine, "row")
        if height < 3:
            m = lower_step(height, lower_blocks, lower_inverse)
        fulls[height], sends, pending = forward_step(
            height, pieces, parents, pattern, m, pending, sizes
        )
        forward[height] = solve_step(height, fulls[height], lower_inverse, sizes)
        taken = [swap(sends[step], "col", step) for step in steps_of(col_count)]
        taken[-1] = after(taken[-1], *forward[height])
        mine = initial[height - 1] - sends[0] - sum(taken)
    z = middle_step(upper_diagonal_inverses, lower_inverse)
    fulls[0], solved = last_step(gather(mine, "row"), z, sizes)
    forward[0] = solve_step(0, fulls[0], lower_inverse, sizes)

    backward = [solved]
    whole = []
    for height in (1, 2, 3):
        composed = compose_step(height, upper_rows, upper_diagonal_inverses, row_count)
        start = start_step(
            height,
            parents,
            pattern,
            forward[height][1],
            upper_rows,
            upper_diagonal_inverses,
            whole,
            row_count,
        )
        whole = whole + [gather(backward[-1], "col")]
        backward.append(backward_step(height, parents, pattern, start, composed, whole[-1]))

    forward_parts = [piece for level in forward for piece in with_layers(level[0])]
    forward_all = forward_out(forward_parts, nodes, own, gz_count)
    backward_all = backward_out(layers_of(jnp.stack(backward[:3])), None, 0, own)
    backward_all = backward_out(layers_of(backward[3][None]), backward_all, 3, own)
    return tuple(
        value.transpose(0, 2, 1, 3).reshape(4, nodes, WIDTH * COLUMNS)
        for value in (forward_all, backward_all)
    )


def solution(mesh):
    in_specs = (
        P(None, "col", "row"),
        P("gz", None, "col", "row"),
        P(None, "col", "row", None),
        P(None, "col", "row", None),
        P(None, "col", None, None),
        P(None, "col", None, None),
        P(None, "col"),
        P(),
    )
    out_specs = (P(None, "col", None), P(None, "col", None))
    return jax.shard_map(body, mesh=mesh, in_specs=in_specs, out_specs=out_specs, check_vma=False)
```

```python
import functools

import jax
import jax.numpy as jnp
from jax import lax
from jax.experimental import pallas as pl
from jax.experimental.pallas import tpu as pltpu
from jax.sharding import PartitionSpec as P

WIDTH = 256
COLUMNS = 64
LANES = 128
F32 = jnp.float32
BF16 = jnp.bfloat16
SMEM = pl.BlockSpec(memory_space=pltpu.SMEM)
VMEM = pl.BlockSpec(memory_space=pltpu.VMEM)
HBM = pl.BlockSpec(memory_space=pltpu.HBM)
PARAMS = pltpu.CompilerParams(vmem_limit_bytes=16 * 2**20)
STREAM_PARAMS = pltpu.CompilerParams(vmem_limit_bytes=52 * 2**20)


def place_of(height, distance):
    return height * (height - 1) // 2 + distance - 1


def shape_of(*dims, dtype=F32):
    return jax.ShapeDtypeStruct(dims, dtype)


def split(value):
    high = value.astype(BF16)
    return high, (value - high.astype(F32)).astype(BF16)


def dot(left, right):
    return jnp.dot(left, right, preferred_element_type=F32)


def dot_t(left, right):
    return lax.dot_general(left, right, (((1,), (1,)), ((), ())), preferred_element_type=F32)


def product(left, right):
    lanes = right[0].shape[1]
    both = dot(left[0], jnp.concatenate(right, axis=1))
    return both[:, :lanes] + both[:, lanes:] + dot(left[1], right[0])


def product_t(left, right):
    rows = left[0].shape[0]
    both = dot_t(jnp.concatenate(left, axis=0), right[0])
    return both[:rows] + both[rows:] + dot_t(left[0], right[1])


def steps_of(count):
    assert count & (count - 1) == 0
    return range(1, count)


def swap(value, axis, step):
    return lax.ppermute(value, axis, [(i, i ^ step) for i in range(lax.axis_size(axis))])


def with_layers(value):
    return [value] + [swap(value, "gz", step) for step in steps_of(lax.axis_size("gz"))]


def after(value, *others):
    return lax.optimization_barrier((value, *others))[0]


def gather(value, axis):
    return [value] + [swap(value, axis, step) for step in steps_of(lax.axis_size(axis))]


def input_kernel(gz_count, nodes, own, right, layer, *outs):
    groups = COLUMNS // own
    kept, away, stage = outs[:4], outs[4:-1], outs[-1]
    gz = lax.axis_index("gz")
    tiles = right.shape[1]
    per_tile = LANES // COLUMNS
    block = lax.broadcasted_iota(jnp.int32, (1, LANES), 1) // own
    for level in range(right.shape[0]):
        for chunk in range(nodes * own // LANES):
            start = chunk * LANES
            lanes = slice(start, start + LANES)
            for row in range(per_tile):
                for which in range(groups):
                    mine = jnp.where(gz == which, 1.0, 0.0)
                    total = jnp.zeros((tiles, LANES), F32)
                    for node in range(start // own, (start + LANES) // own):
                        value = right[level, :, node, :] * mine - layer[level, :, node, :]
                        target = node * own - start
                        shift = (target - row * COLUMNS - which * own) % LANES
                        value = pltpu.roll(value, shift, 1) if shift else value
                        total = jnp.where(block == target // own, value, total)
                    stage[level, chunk, which, pl.ds(row, tiles, stride=per_tile), :] = total
            found = [stage[level, chunk, which] for which in range(groups)]
            for step in range(groups):
                chosen = found[0]
                for which in range(1, groups):
                    chosen = jnp.where((gz ^ step) == which, found[which], chosen)
                if step == 0:
                    kept[level][:, lanes] = chosen
                else:
                    away[step - 1][level, :, lanes] = chosen


def lower_kernel(height, blocks, inverse, high_out, low_out):
    first = place_of(height, 1)
    part, width = blocks.shape[2:]
    left = blocks[first : first + height, 0].reshape(height * part, width)
    whole = product(split(left), split(inverse[0, 0])).reshape(height, part, width)
    high_out[:, 0], low_out[:, 0] = split(whole)


def lower_step(height, blocks, inverse):
    pairs, nodes, part = blocks.shape[:3]
    out = shape_of(height, nodes, part, WIDTH, dtype=BF16)
    return pl.pallas_call(
        functools.partial(lower_kernel, height),
        grid=(nodes,),
        out_shape=[out, out],
        in_specs=[
            pl.BlockSpec((pairs, 1, part, WIDTH), lambda i: (0, i, 0, 0)),
            pl.BlockSpec((1, 1, WIDTH, WIDTH), lambda i: (height, i, 0, 0)),
        ],
        out_specs=[pl.BlockSpec((height, 1, part, WIDTH), lambda i: (0, i, 0, 0))] * 2,
        compiler_params=STREAM_PARAMS,
        name="lower_products",
    )(blocks, inverse)


def middle_kernel(upper, lower, high_out, low_out, lower_high, lower_low):
    right = split(lower[0, 0])
    lower_high[0], lower_low[0] = right
    high_out[0], low_out[0] = split(product(split(upper[0, 0]), right))


def middle_step(upper, lower):
    nodes = lower.shape[1]
    out = shape_of(nodes, WIDTH, WIDTH, dtype=BF16)
    return pl.pallas_call(
        middle_kernel,
        grid=(nodes,),
        out_shape=[out] * 4,
        in_specs=[pl.BlockSpec((1, 1, WIDTH, WIDTH), lambda i: (0, i, 0, 0))] * 2,
        out_specs=[pl.BlockSpec((1, WIDTH, WIDTH), lambda i: (i, 0, 0))] * 4,
        compiler_params=STREAM_PARAMS,
        name="middle_product",
    )(upper, lower)


def assemble(pieces, full, part):
    row = lax.axis_index("row")
    for step, piece in enumerate(pieces):
        full[pl.ds(pl.multiple_of((row ^ step) * part, part), part), :] = piece[...]


def forward_kernel(height, sizes, *refs):
    nodes, part, own, row_count, col_count = sizes
    lanes = nodes * own
    pieces, refs = refs[:row_count], refs[row_count:]
    parents, pattern, m_high, m_low = refs[:4]
    pending_in = refs[4 : 4 + height] if height < 3 else ()
    refs = refs[4 + len(pending_in) :]
    full, sends = refs[0], refs[1 : 1 + col_count]
    pending_out = refs[1 + col_count : col_count + height]
    urgent = refs[-1]
    assemble(pieces, full, part)
    lane = lax.broadcasted_iota(jnp.int32, (1, lanes), 1) // own
    col = lax.axis_index("col")
    right = split(full[...])
    targets = []
    for level in range(height):
        target = urgent if level == height - 1 else pending_out[level]
        target[...] = pending_in[level][...] if pending_in else jnp.zeros(target.shape, F32)
        targets.append(target)
    for node in range(nodes):
        ancestor = col * nodes + node
        for distance in range(1, height + 1):
            level = height - distance
            ancestor = parents[level, ancestor]
            slot = lax.rem(ancestor, nodes)
            where = lax.div(ancestor, nodes) ^ col
            term = product((m_high[distance - 1, node], m_low[distance - 1, node]), right)
            term = pltpu.roll(term, lax.rem(slot - node + nodes, nodes) * own, 1)
            stored = jnp.where(pattern[node, place_of(height, distance)] != 0, slot, -1)
            targets[level][where] += jnp.where(lane == stored, term, 0.0)
    for step in range(col_count):
        sends[step][...] = urgent[step]


def forward_step(height, pieces, parents, pattern, m, pending, sizes):
    nodes, part, own, row_count, col_count = sizes
    lanes = nodes * own
    piece = shape_of(part, lanes)
    stack = shape_of(col_count, part, lanes)
    out_shape = [shape_of(row_count * part, lanes)] + [piece] * col_count + [stack] * (height - 1)
    results = pl.pallas_call(
        functools.partial(forward_kernel, height, sizes),
        out_shape=out_shape,
        in_specs=[VMEM] * len(pieces) + [SMEM, SMEM] + [VMEM] * (2 + len(pending)),
        out_specs=[VMEM] * len(out_shape),
        scratch_shapes=[pltpu.VMEM(stack.shape, F32)],
        compiler_params=PARAMS,
        name="forward_level",
    )(*pieces, parents, pattern, *m, *pending)
    return results[0], results[1 : 1 + col_count], results[1 + col_count :]


def own_rows(turned, node, own, row_count):
    few = own // row_count
    start = node * own + lax.axis_index("row") * few
    return turned[pl.ds(pl.multiple_of(start, few), few), :]


def last_kernel(sizes, *refs):
    nodes, part, own, row_count, col_count = sizes
    pieces = refs[:row_count]
    z_high, z_low, lower_high, lower_low, solved_out, out, full, turned = refs[row_count:]
    assemble(pieces, full, part)
    turned[...] = full[...].T
    for node in range(nodes):
        left = split(own_rows(turned, node, own, row_count))
        out[node] = product_t(left, (z_high[node], z_low[node]))
    lane = lax.broadcasted_iota(jnp.int32, (1, nodes * own), 1) // own
    right = split(full[...])
    solved = jnp.zeros(full.shape, F32)
    for node in range(nodes):
        solved = jnp.where(lane == node, product((lower_high[node], lower_low[node]), right), solved)
    solved_out[...] = solved


def last_step(pieces, matrices, sizes):
    nodes, part, own, row_count, col_count = sizes
    lanes, rows = nodes * own, row_count * part
    return pl.pallas_call(
        functools.partial(last_kernel, sizes),
        out_shape=[shape_of(rows, lanes), shape_of(nodes, own // row_count, rows)],
        in_specs=[VMEM] * (len(pieces) + len(matrices)),
        out_specs=[VMEM] * 2,
        scratch_shapes=[pltpu.VMEM((rows, lanes), F32), pltpu.VMEM((lanes, rows), F32)],
        compiler_params=PARAMS,
        name="forward_last",
    )(*pieces, *matrices)


def solve_kernel(sizes, full, lower, out, own_out, turned):
    nodes, part, own, row_count, col_count = sizes
    node = pl.program_id(0)
    lane = lax.broadcasted_iota(jnp.int32, (1, nodes * own), 1) // own

    @pl.when(node == 0)
    def _():
        turned[...] = full[...].T
        out[...] = jnp.zeros(out.shape, F32)

    inverse = split(lower[0, 0])
    out[...] = jnp.where(lane == node, product(inverse, split(full[...])), out[...])
    own_out[0] = product_t(split(own_rows(turned, node, own, row_count)), inverse)


def solve_step(height, full, lower, sizes):
    nodes, part, own, row_count, col_count = sizes
    rows, lanes = full.shape
    few = own // row_count
    whole = pl.BlockSpec((rows, lanes), lambda i: (0, 0))
    return pl.pallas_call(
        functools.partial(solve_kernel, sizes),
        grid=(nodes,),
        out_shape=[shape_of(rows, lanes), shape_of(nodes, few, rows)],
        in_specs=[whole, pl.BlockSpec((1, 1, rows, rows), lambda i: (height, i, 0, 0))],
        out_specs=[whole, pl.BlockSpec((1, few, rows), lambda i: (i, 0, 0))],
        scratch_shapes=[pltpu.VMEM((lanes, rows), F32)],
        compiler_params=STREAM_PARAMS,
        name="solve_level",
    )(full, lower)


def descend_kernel(height, nodes, col_count, parents, pattern, value, inverse, *refs):
    blocks, pieces, (out, high_out, low_out) = refs[:height], refs[height:-3], refs[-3:]
    col = lax.axis_index("col")
    node = pl.program_id(0)
    rest = value[0]
    left = split(inverse[0, 0])
    ancestor = parents[height - 1, col * nodes + node]
    for distance in range(2, height + 1):
        level = height - distance
        ancestor = parents[level, ancestor]
        where = lax.div(ancestor, nodes) ^ col
        slot = lax.rem(ancestor, nodes)
        chosen = pieces[level * col_count][slot]
        for step in range(1, col_count):
            piece = pieces[level * col_count + step][slot]
            chosen = jnp.where(where == step, piece, chosen)
        block = blocks[distance - 1][:, 0, 0].reshape(WIDTH, WIDTH)
        term = product_t(split(chosen), split(block))
        stored = pattern[node, place_of(height, distance)] != 0
        rest = rest - jnp.where(stored, term, 0.0)
    out[0] = product_t(split(rest), left)
    nearest = blocks[0][:, 0, 0].reshape(WIDTH, WIDTH)
    high_out[0], low_out[0] = split(product(left, split(nearest)))


def descend_step(height, parents, pattern, value, gathered, inverse, solved, row_count):
    per, nodes, part = gathered.shape[1:4]
    col_count = lax.axis_size("col")
    few, rows = value.shape[1:]
    pieces = [piece for level in solved for piece in level]

    def block_spec(distance):
        place = place_of(height, distance)
        return pl.BlockSpec(
            (row_count, 1, 1, part, WIDTH), lambda i: (place // per, place % per, i, 0, 0)
        )

    each = pl.BlockSpec((1, few, rows), lambda i: (i, 0, 0))
    whole = pl.BlockSpec((nodes, few, rows), lambda i: (0, 0, 0))
    matrix = shape_of(nodes, WIDTH, WIDTH, dtype=BF16)
    return pl.pallas_call(
        functools.partial(descend_kernel, height, nodes, col_count),
        grid=(nodes,),
        out_shape=[shape_of(nodes, few, rows), matrix, matrix],
        in_specs=[SMEM, SMEM, each]
        + [pl.BlockSpec((1, 1, WIDTH, WIDTH), lambda i: (height, i, 0, 0))]
        + [block_spec(distance) for distance in range(1, height + 1)]
        + [whole] * len(pieces),
        out_specs=[each] + [pl.BlockSpec((1, WIDTH, WIDTH), lambda i: (i, 0, 0))] * 2,
        compiler_params=STREAM_PARAMS,
        name="descend_level",
    )(parents, pattern, value, inverse, *([gathered] * height), *pieces)


def backward_kernel(height, nodes, parents, pattern, start, high, low, *refs):
    pieces, out, solved = refs[:-2], refs[-2], refs[-1]
    for step, piece in enumerate(pieces):
        solved[step] = piece[...]
    col = lax.axis_index("col")
    for node in range(nodes):
        ancestor = parents[height - 1, col * nodes + node]
        where = lax.div(ancestor, nodes) ^ col
        left = split(solved[where, lax.rem(ancestor, nodes)])
        term = product_t(left, (high[node], low[node]))
        stored = pattern[node, place_of(height, 1)] != 0
        out[node] = start[node] - jnp.where(stored, term, 0.0)


def backward_step(height, parents, pattern, start, composed, pieces):
    return pl.pallas_call(
        functools.partial(backward_kernel, height, start.shape[0]),
        out_shape=shape_of(*start.shape),
        in_specs=[SMEM, SMEM] + [VMEM] * (3 + len(pieces)),
        out_specs=VMEM,
        scratch_shapes=[pltpu.VMEM((len(pieces),) + start.shape, F32)],
        compiler_params=PARAMS,
        name="backward_level",
    )(parents, pattern, start, *composed, *pieces)


def groups_found(found, groups):
    gz = lax.axis_index("gz")
    values = []
    for which in range(groups):
        value = found[0]
        for step in range(1, groups):
            value = jnp.where((gz ^ step) == which, found[step], value)
        values.append(value)
    return values


def forward_out_kernel(gz_count, nodes, own, *refs):
    parts, out, stage = refs[:-2], refs[-2], refs[-1]
    groups = COLUMNS // own
    per_tile = LANES // COLUMNS
    tiles = out.shape[1]
    block = lax.broadcasted_iota(jnp.int32, (1, LANES), 1) // own
    for level in range(out.shape[0]):
        for chunk in range(nodes * own // LANES):
            start = chunk * LANES
            lanes = slice(start, start + LANES)
            found = [part[:, lanes] for part in parts[level * gz_count : (level + 1) * gz_count]]
            for which, value in enumerate(groups_found(found, groups)):
                stage[chunk, which] = value
            values = [
                stage[chunk, which, pl.ds(row, tiles, stride=per_tile), :]
                for row in range(per_tile)
                for which in range(groups)
            ]
            for node in range(start // own, (start + LANES) // own):
                total = jnp.zeros((tiles, LANES), F32)
                for place, value in enumerate(values):
                    shift = (place * own - (node * own - start)) % LANES
                    value = pltpu.roll(value, shift, 1) if shift else value
                    total = jnp.where(block == place, value, total)
                out[level, :, node, :] = total


def forward_out(parts, nodes, own, gz_count):
    rows, lanes = parts[0].shape
    tiles = rows * COLUMNS // LANES
    return pl.pallas_call(
        functools.partial(forward_out_kernel, gz_count, nodes, own),
        out_shape=shape_of(len(parts) // gz_count, tiles, nodes, LANES),
        in_specs=[VMEM] * len(parts),
        out_specs=VMEM,
        scratch_shapes=[pltpu.VMEM((lanes // LANES, COLUMNS // own, rows, LANES), F32)],
        compiler_params=PARAMS,
        name="forward_out",
    )(*parts)


def backward_out_kernel(nodes, gz_count, own, *refs):
    parts, (out, columns, turned) = refs[:gz_count], refs[-3:]
    groups = COLUMNS // own
    per_tile = LANES // COLUMNS
    tiles = out.shape[1]
    row_count, _, _, few, _ = parts[0].shape
    row = lax.axis_index("row")
    for node in range(nodes):
        for step in range(row_count):
            values = groups_found([part[step, 0, node] for part in parts], groups)
            for which, value in enumerate(values):
                index = which * row_count + (row ^ step)
                columns[pl.ds(pl.multiple_of(index * few, few), few), :] = value
        turned[...] = columns[...].T
        rows = [turned[pl.ds(step, tiles, stride=per_tile), :] for step in range(per_tile)]
        out[0, :, node, :] = jnp.concatenate(rows, axis=1)


def backward_out(parts, before, first, own):
    row_count, levels, nodes, few, rows = parts[0].shape
    tiles = rows * COLUMNS // LANES
    ready = [before] if before is not None else []
    return pl.pallas_call(
        functools.partial(backward_out_kernel, nodes, len(parts), own),
        grid=(levels,),
        out_shape=shape_of(4, tiles, nodes, LANES),
        in_specs=[
            pl.BlockSpec((row_count, 1, nodes, few, rows), lambda i: (0, i, 0, 0, 0))
            for part in parts
        ]
        + [HBM] * len(ready),
        out_specs=pl.BlockSpec((1, tiles, nodes, LANES), lambda i: (first + i, 0, 0, 0)),
        scratch_shapes=[pltpu.VMEM((COLUMNS, rows), F32), pltpu.VMEM((rows, COLUMNS), F32)],
        input_output_aliases={len(parts): 0} if ready else {},
        compiler_params=PARAMS,
        name="backward_out",
    )(*parts, *ready)


def body(
    right_side,
    layer_sums,
    lower_blocks,
    upper_blocks,
    lower_inverse,
    upper_diagonal_inverses,
    pattern,
    parents,
):
    nodes = right_side.shape[1]
    part = lower_blocks.shape[2]
    gz_count = lax.axis_size("gz")
    row_count = lax.axis_size("row")
    col_count = lax.axis_size("col")
    own = COLUMNS // gz_count
    lanes = nodes * own
    sizes = (nodes, part, own, row_count, col_count)
    gz = lax.axis_index("gz")

    def tiled(value):
        return value.reshape(4, nodes, part * COLUMNS // LANES, LANES).transpose(0, 2, 1, 3)

    parts = pl.pallas_call(
        functools.partial(input_kernel, gz_count, nodes, own),
        out_shape=[shape_of(part, lanes)] * 4 + [shape_of(4, part, lanes)] * (gz_count - 1),
        in_specs=[VMEM, VMEM],
        out_specs=[VMEM] * (3 + gz_count),
        scratch_shapes=[pltpu.VMEM((4, lanes // LANES, COLUMNS // own, part, LANES), F32)],
        compiler_params=STREAM_PARAMS,
        name="input_parts",
    )(tiled(right_side), tiled(layer_sums[0]))
    kept, away = parts[:4], parts[4:]

    per = upper_blocks.shape[0] // gz_count
    half = lax.dynamic_slice_in_dim(after(upper_blocks, *away), gz * per, per, 0)
    upper_rows = lax.all_gather(half, ("gz", "row"))
    others = [after(swap(away[step - 1], "gz", step), half) for step in steps_of(gz_count)]
    pattern = pattern.T
    initial = [kept[level] + sum(other[level] for other in others) for level in range(4)]

    fulls = [None] * 4
    forward = [None] * 4
    pending = []
    mine = initial[3]
    m = lower_step(3, lower_blocks, lower_inverse)
    for height in (3, 2, 1):
        pieces = gather(mine, "row")
        if height < 3:
            m = lower_step(height, lower_blocks, lower_inverse)
        fulls[height], sends, pending = forward_step(
            height, pieces, parents, pattern, m, pending, sizes
        )
        forward[height] = solve_step(height, fulls[height], lower_inverse, sizes)
        taken = [swap(sends[step], "col", step) for step in steps_of(col_count)]
        taken[-1] = after(taken[-1], *forward[height])
        mine = initial[height - 1] - sends[0] - sum(taken)
    z = middle_step(upper_diagonal_inverses, lower_inverse)
    solved_forward, solved = last_step(gather(mine, "row"), z, sizes)
    forward[0] = (solved_forward,)

    backward = [solved]
    whole = []
    for height in (1, 2, 3):
        start, *composed = descend_step(
            height,
            parents,
            pattern,
            forward[height][1],
            upper_rows,
            upper_diagonal_inverses,
            whole,
            row_count,
        )
        whole = whole + [gather(backward[-1], "col")]
        if height == 3:
            early = gather(after(jnp.stack(backward), whole[-1][-1]), "row")
        backward.append(backward_step(height, parents, pattern, start, composed, whole[-1]))

    forward_parts = [piece for level in forward for piece in with_layers(level[0])]
    forward_all = forward_out(forward_parts, nodes, own, gz_count)
    late = gather(backward[3][None], "row")
    early = [after(piece, *late, forward_all) for piece in early]
    early, late = with_layers(jnp.stack(early)), with_layers(jnp.stack(late))
    backward_all = backward_out(early, None, 0, own)
    backward_all = backward_out(late, backward_all, 3, own)
    return tuple(
        value.transpose(0, 2, 1, 3).reshape(4, nodes, WIDTH * COLUMNS)
        for value in (forward_all, backward_all)
    )


def solution(mesh):
    in_specs = (
        P(None, "col", "row"),
        P("gz", None, "col", "row"),
        P(None, "col", "row", None),
        P(None, "col", "row", None),
        P(None, "col", None, None),
        P(None, "col", None, None),
        P(None, "col"),
        P(),
    )
    out_specs = (P(None, "col", None), P(None, "col", None))
    return jax.shard_map(body, mesh=mesh, in_specs=in_specs, out_specs=out_specs, check_vma=False)
```

```python
import functools

import jax
import jax.numpy as jnp
from jax import lax
from jax.experimental import pallas as pl
from jax.experimental.pallas import tpu as pltpu
from jax.sharding import PartitionSpec as P

WIDTH = 256
COLUMNS = 64
LANES = 128
F32 = jnp.float32
BF16 = jnp.bfloat16
SMEM = pl.BlockSpec(memory_space=pltpu.SMEM)
VMEM = pl.BlockSpec(memory_space=pltpu.VMEM)
HBM = pl.BlockSpec(memory_space=pltpu.HBM)
PARAMS = pltpu.CompilerParams(vmem_limit_bytes=16 * 2**20)
INPUT_PARAMS = pltpu.CompilerParams(vmem_limit_bytes=54 * 2**20)
MIDDLE_PARAMS = pltpu.CompilerParams(vmem_limit_bytes=51 * 2**20)
STREAM_PARAMS = pltpu.CompilerParams(vmem_limit_bytes=52 * 2**20)


def place_of(height, distance):
    return height * (height - 1) // 2 + distance - 1


def shape_of(*dims, dtype=F32):
    return jax.ShapeDtypeStruct(dims, dtype)


def split(value):
    high = value.astype(BF16)
    return high, (value - high.astype(F32)).astype(BF16)


def dot(left, right):
    return jnp.dot(left, right, preferred_element_type=F32)


def dot_t(left, right):
    return lax.dot_general(left, right, (((1,), (1,)), ((), ())), preferred_element_type=F32)


def product(left, right):
    lanes = right[0].shape[1]
    both = dot(left[0], jnp.concatenate(right, axis=1))
    return both[:, :lanes] + both[:, lanes:] + dot(left[1], right[0])


def product_t(left, right):
    rows = left[0].shape[0]
    both = dot_t(jnp.concatenate(left, axis=0), right[0])
    return both[:rows] + both[rows:] + dot_t(left[0], right[1])


def steps_of(count):
    assert count & (count - 1) == 0
    return range(1, count)


def swap(value, axis, step):
    return lax.ppermute(value, axis, [(i, i ^ step) for i in range(lax.axis_size(axis))])


def with_layers(value):
    return [value] + [swap(value, "gz", step) for step in steps_of(lax.axis_size("gz"))]


def after(value, *others):
    return lax.optimization_barrier((value, *others))[0]


def gather(value, axis):
    return [value] + [swap(value, axis, step) for step in steps_of(lax.axis_size(axis))]


def input_kernel(gz_count, nodes, own, right, layer, *outs):
    groups = COLUMNS // own
    kept, away, stage = outs[:4], outs[4:-1], outs[-1]
    gz = lax.axis_index("gz")
    tiles = right.shape[1]
    per_tile = LANES // COLUMNS
    block = lax.broadcasted_iota(jnp.int32, (1, LANES), 1) // own
    for level in range(right.shape[0]):
        for chunk in range(nodes * own // LANES):
            start = chunk * LANES
            lanes = slice(start, start + LANES)
            for row in range(per_tile):
                for which in range(groups):
                    mine = jnp.where(gz == which, 1.0, 0.0)
                    total = jnp.zeros((tiles, LANES), F32)
                    for node in range(start // own, (start + LANES) // own):
                        value = right[level, :, node, :] * mine - layer[level, :, node, :]
                        target = node * own - start
                        shift = (target - row * COLUMNS - which * own) % LANES
                        value = pltpu.roll(value, shift, 1) if shift else value
                        total = jnp.where(block == target // own, value, total)
                    stage[level, chunk, which, pl.ds(row, tiles, stride=per_tile), :] = total
            found = [stage[level, chunk, which] for which in range(groups)]
            for step in range(groups):
                chosen = found[0]
                for which in range(1, groups):
                    chosen = jnp.where((gz ^ step) == which, found[which], chosen)
                if step == 0:
                    kept[level][:, lanes] = chosen
                else:
                    away[step - 1][level, :, lanes] = chosen


def lower_kernel(height, blocks, inverse, high_out, low_out):
    first = place_of(height, 1)
    part, width = blocks.shape[2:]
    left = blocks[first : first + height, 0].reshape(height * part, width)
    whole = product(split(left), split(inverse[0, 0])).reshape(height, part, width)
    high_out[:, 0], low_out[:, 0] = split(whole)


def lower_step(height, blocks, inverse):
    pairs, nodes, part = blocks.shape[:3]
    out = shape_of(height, nodes, part, WIDTH, dtype=BF16)
    return pl.pallas_call(
        functools.partial(lower_kernel, height),
        grid=(nodes,),
        out_shape=[out, out],
        in_specs=[
            pl.BlockSpec((pairs, 1, part, WIDTH), lambda i: (0, i, 0, 0)),
            pl.BlockSpec((1, 1, WIDTH, WIDTH), lambda i: (height, i, 0, 0)),
        ],
        out_specs=[pl.BlockSpec((height, 1, part, WIDTH), lambda i: (0, i, 0, 0))] * 2,
        compiler_params=STREAM_PARAMS,
        name="lower_products",
    )(blocks, inverse)


def middle_kernel(upper, lower, high_out, low_out, lower_high, lower_low):
    right = split(lower[0, 0])
    lower_high[0], lower_low[0] = right
    high_out[0], low_out[0] = split(product(split(upper[0, 0]), right))


def middle_step(upper, lower):
    nodes = lower.shape[1]
    out = shape_of(nodes, WIDTH, WIDTH, dtype=BF16)
    return pl.pallas_call(
        middle_kernel,
        grid=(nodes,),
        out_shape=[out] * 4,
        in_specs=[pl.BlockSpec((1, 1, WIDTH, WIDTH), lambda i: (0, i, 0, 0))] * 2,
        out_specs=[pl.BlockSpec((1, WIDTH, WIDTH), lambda i: (i, 0, 0))] * 4,
        compiler_params=MIDDLE_PARAMS,
        name="middle_product",
    )(upper, lower)


def assemble(pieces, full, part):
    row = lax.axis_index("row")
    for step, piece in enumerate(pieces):
        full[pl.ds(pl.multiple_of((row ^ step) * part, part), part), :] = piece[...]


def forward_kernel(height, sizes, *refs):
    nodes, part, own, row_count, col_count = sizes
    lanes = nodes * own
    pieces, refs = refs[:row_count], refs[row_count:]
    parents, pattern, m_high, m_low = refs[:4]
    pending_in = refs[4 : 4 + height] if height < 3 else ()
    refs = refs[4 + len(pending_in) :]
    full, sends = refs[0], refs[1 : 1 + col_count]
    pending_out = refs[1 + col_count : col_count + height]
    urgent = refs[-1]
    assemble(pieces, full, part)
    lane = lax.broadcasted_iota(jnp.int32, (1, lanes), 1) // own
    col = lax.axis_index("col")
    right = split(full[...])
    targets = []
    for level in range(height):
        target = urgent if level == height - 1 else pending_out[level]
        target[...] = pending_in[level][...] if pending_in else jnp.zeros(target.shape, F32)
        targets.append(target)
    for node in range(nodes):
        ancestor = col * nodes + node
        for distance in range(1, height + 1):
            level = height - distance
            ancestor = parents[level, ancestor]
            slot = lax.rem(ancestor, nodes)
            where = lax.div(ancestor, nodes) ^ col
            term = product((m_high[distance - 1, node], m_low[distance - 1, node]), right)
            term = pltpu.roll(term, lax.rem(slot - node + nodes, nodes) * own, 1)
            stored = jnp.where(pattern[node, place_of(height, distance)] != 0, slot, -1)
            targets[level][where] += jnp.where(lane == stored, term, 0.0)
    for step in range(col_count):
        sends[step][...] = urgent[step]


def forward_step(height, pieces, parents, pattern, m, pending, sizes):
    nodes, part, own, row_count, col_count = sizes
    lanes = nodes * own
    piece = shape_of(part, lanes)
    stack = shape_of(col_count, part, lanes)
    out_shape = [shape_of(row_count * part, lanes)] + [piece] * col_count + [stack] * (height - 1)
    results = pl.pallas_call(
        functools.partial(forward_kernel, height, sizes),
        out_shape=out_shape,
        in_specs=[VMEM] * len(pieces) + [SMEM, SMEM] + [VMEM] * (2 + len(pending)),
        out_specs=[VMEM] * len(out_shape),
        scratch_shapes=[pltpu.VMEM(stack.shape, F32)],
        compiler_params=PARAMS,
        name="forward_level",
    )(*pieces, parents, pattern, *m, *pending)
    return results[0], results[1 : 1 + col_count], results[1 + col_count :]


def own_rows(turned, node, own, row_count):
    few = own // row_count
    start = node * own + lax.axis_index("row") * few
    return turned[pl.ds(pl.multiple_of(start, few), few), :]


def last_kernel(sizes, *refs):
    nodes, part, own, row_count, col_count = sizes
    pieces = refs[:row_count]
    z_high, z_low, lower_high, lower_low, solved_out, out, full, turned = refs[row_count:]
    assemble(pieces, full, part)
    turned[...] = full[...].T
    for node in range(nodes):
        left = split(own_rows(turned, node, own, row_count))
        out[node] = product_t(left, (z_high[node], z_low[node]))
    lane = lax.broadcasted_iota(jnp.int32, (1, nodes * own), 1) // own
    right = split(full[...])
    solved = jnp.zeros(full.shape, F32)
    for node in range(nodes):
        solved = jnp.where(lane == node, product((lower_high[node], lower_low[node]), right), solved)
    solved_out[...] = solved


def last_step(pieces, matrices, sizes):
    nodes, part, own, row_count, col_count = sizes
    lanes, rows = nodes * own, row_count * part
    return pl.pallas_call(
        functools.partial(last_kernel, sizes),
        out_shape=[shape_of(rows, lanes), shape_of(nodes, own // row_count, rows)],
        in_specs=[VMEM] * (len(pieces) + len(matrices)),
        out_specs=[VMEM] * 2,
        scratch_shapes=[pltpu.VMEM((rows, lanes), F32), pltpu.VMEM((lanes, rows), F32)],
        compiler_params=PARAMS,
        name="forward_last",
    )(*pieces, *matrices)


def solve_kernel(sizes, full, lower, out, own_out, turned):
    nodes, part, own, row_count, col_count = sizes
    node = pl.program_id(0)
    lane = lax.broadcasted_iota(jnp.int32, (1, nodes * own), 1) // own

    @pl.when(node == 0)
    def _():
        turned[...] = full[...].T
        out[...] = jnp.zeros(out.shape, F32)

    inverse = split(lower[0, 0])
    out[...] = jnp.where(lane == node, product(inverse, split(full[...])), out[...])
    own_out[0] = product_t(split(own_rows(turned, node, own, row_count)), inverse)


def solve_step(height, full, lower, sizes):
    nodes, part, own, row_count, col_count = sizes
    rows, lanes = full.shape
    few = own // row_count
    whole = pl.BlockSpec((rows, lanes), lambda i: (0, 0))
    return pl.pallas_call(
        functools.partial(solve_kernel, sizes),
        grid=(nodes,),
        out_shape=[shape_of(rows, lanes), shape_of(nodes, few, rows)],
        in_specs=[whole, pl.BlockSpec((1, 1, rows, rows), lambda i: (height, i, 0, 0))],
        out_specs=[whole, pl.BlockSpec((1, few, rows), lambda i: (i, 0, 0))],
        scratch_shapes=[pltpu.VMEM((lanes, rows), F32)],
        compiler_params=STREAM_PARAMS,
        name="solve_level",
    )(full, lower)


def descend_kernel(height, nodes, col_count, parents, pattern, value, inverse, *refs):
    blocks, pieces, (out, high_out, low_out) = refs[:height], refs[height:-3], refs[-3:]
    col = lax.axis_index("col")
    node = pl.program_id(0)
    rest = value[0]
    left = split(inverse[0, 0])
    ancestor = parents[height - 1, col * nodes + node]
    for distance in range(2, height + 1):
        level = height - distance
        ancestor = parents[level, ancestor]
        where = lax.div(ancestor, nodes) ^ col
        slot = lax.rem(ancestor, nodes)
        chosen = pieces[level * col_count][slot]
        for step in range(1, col_count):
            piece = pieces[level * col_count + step][slot]
            chosen = jnp.where(where == step, piece, chosen)
        block = blocks[distance - 1][:, 0, 0].reshape(WIDTH, WIDTH)
        term = product_t(split(chosen), split(block))
        stored = pattern[node, place_of(height, distance)] != 0
        rest = rest - jnp.where(stored, term, 0.0)
    out[0] = product_t(split(rest), left)
    nearest = blocks[0][:, 0, 0].reshape(WIDTH, WIDTH)
    high_out[0], low_out[0] = split(product(left, split(nearest)))


def descend_step(height, parents, pattern, value, gathered, inverse, solved, row_count):
    per, nodes, part = gathered.shape[1:4]
    col_count = lax.axis_size("col")
    few, rows = value.shape[1:]
    pieces = [piece for level in solved for piece in level]

    def block_spec(distance):
        place = place_of(height, distance)
        return pl.BlockSpec(
            (row_count, 1, 1, part, WIDTH), lambda i: (place // per, place % per, i, 0, 0)
        )

    each = pl.BlockSpec((1, few, rows), lambda i: (i, 0, 0))
    whole = pl.BlockSpec((nodes, few, rows), lambda i: (0, 0, 0))
    matrix = shape_of(nodes, WIDTH, WIDTH, dtype=BF16)
    return pl.pallas_call(
        functools.partial(descend_kernel, height, nodes, col_count),
        grid=(nodes,),
        out_shape=[shape_of(nodes, few, rows), matrix, matrix],
        in_specs=[SMEM, SMEM, each]
        + [pl.BlockSpec((1, 1, WIDTH, WIDTH), lambda i: (height, i, 0, 0))]
        + [block_spec(distance) for distance in range(1, height + 1)]
        + [whole] * len(pieces),
        out_specs=[each] + [pl.BlockSpec((1, WIDTH, WIDTH), lambda i: (i, 0, 0))] * 2,
        compiler_params=STREAM_PARAMS,
        name="descend_level",
    )(parents, pattern, value, inverse, *([gathered] * height), *pieces)


def backward_kernel(height, nodes, col_count, parents, pattern, start, high, low, *refs):
    pieces, earlier, (out, solved) = refs[:col_count], refs[col_count:-2], refs[-2:]
    for step, piece in enumerate(pieces):
        solved[step] = piece[...]
    for level, value in enumerate(earlier):
        out[level] = value[...]
    col = lax.axis_index("col")
    for node in range(nodes):
        ancestor = parents[height - 1, col * nodes + node]
        where = lax.div(ancestor, nodes) ^ col
        left = split(solved[where, lax.rem(ancestor, nodes)])
        term = product_t(left, (high[node], low[node]))
        stored = pattern[node, place_of(height, 1)] != 0
        total = start[node] - jnp.where(stored, term, 0.0)
        if earlier:
            out[height, node] = total
        else:
            out[node] = total


def backward_step(height, parents, pattern, start, composed, pieces, earlier):
    out = ((1 + len(earlier),) if earlier else ()) + start.shape
    return pl.pallas_call(
        functools.partial(backward_kernel, height, start.shape[0], len(pieces)),
        out_shape=shape_of(*out),
        in_specs=[SMEM, SMEM] + [VMEM] * (3 + len(pieces) + len(earlier)),
        out_specs=VMEM,
        scratch_shapes=[pltpu.VMEM((len(pieces),) + start.shape, F32)],
        compiler_params=PARAMS,
        name="backward_level",
    )(parents, pattern, start, *composed, *pieces, *earlier)


def groups_found(found, groups):
    gz = lax.axis_index("gz")
    values = []
    for which in range(groups):
        value = found[0]
        for step in range(1, groups):
            value = jnp.where((gz ^ step) == which, found[step], value)
        values.append(value)
    return values


def forward_out_kernel(gz_count, nodes, own, *refs):
    parts, out, stage = refs[:-2], refs[-2], refs[-1]
    groups = COLUMNS // own
    per_tile = LANES // COLUMNS
    tiles = out.shape[1]
    block = lax.broadcasted_iota(jnp.int32, (1, LANES), 1) // own
    for level in range(out.shape[0]):
        for chunk in range(nodes * own // LANES):
            start = chunk * LANES
            lanes = slice(start, start + LANES)
            found = [part[:, lanes] for part in parts[level * gz_count : (level + 1) * gz_count]]
            for which, value in enumerate(groups_found(found, groups)):
                stage[chunk, which] = value
            values = [
                stage[chunk, which, pl.ds(row, tiles, stride=per_tile), :]
                for row in range(per_tile)
                for which in range(groups)
            ]
            for node in range(start // own, (start + LANES) // own):
                total = jnp.zeros((tiles, LANES), F32)
                for place, value in enumerate(values):
                    shift = (place * own - (node * own - start)) % LANES
                    value = pltpu.roll(value, shift, 1) if shift else value
                    total = jnp.where(block == place, value, total)
                out[level, :, node, :] = total


def forward_out(parts, nodes, own, gz_count):
    rows, lanes = parts[0].shape
    tiles = rows * COLUMNS // LANES
    return pl.pallas_call(
        functools.partial(forward_out_kernel, gz_count, nodes, own),
        out_shape=shape_of(len(parts) // gz_count, tiles, nodes, LANES),
        in_specs=[VMEM] * len(parts),
        out_specs=VMEM,
        scratch_shapes=[pltpu.VMEM((lanes // LANES, COLUMNS // own, rows, LANES), F32)],
        compiler_params=PARAMS,
        name="forward_out",
    )(*parts)


def backward_out_kernel(nodes, gz_count, own, *refs):
    parts, (out, columns, turned) = refs[:-3], refs[-3:]
    groups = COLUMNS // own
    per_tile = LANES // COLUMNS
    tiles = out.shape[1]
    row_count, _, _, few, _ = parts[0].shape
    row = lax.axis_index("row")
    for node in range(nodes):
        for step in range(row_count):
            values = groups_found([part[step, 0, node] for part in parts], groups)
            for which, value in enumerate(values):
                index = which * row_count + (row ^ step)
                columns[node, pl.ds(pl.multiple_of(index * few, few), few), :] = value
        turned[node] = columns[node].T
        rows = [turned[node, pl.ds(step, tiles, stride=per_tile), :] for step in range(per_tile)]
        out[0, :, node, :] = jnp.concatenate(rows, axis=1)


def backward_out(parts, own):
    row_count, levels, nodes, few, rows = parts[0].shape
    tiles = rows * COLUMNS // LANES
    part_spec = pl.BlockSpec((row_count, 1, nodes, few, rows), lambda i: (0, i, 0, 0, 0))
    return pl.pallas_call(
        functools.partial(backward_out_kernel, nodes, len(parts), own),
        grid=(levels,),
        out_shape=shape_of(levels, tiles, nodes, LANES),
        in_specs=[part_spec] * len(parts),
        out_specs=pl.BlockSpec((1, tiles, nodes, LANES), lambda i: (i, 0, 0, 0)),
        scratch_shapes=[
            pltpu.VMEM((nodes, COLUMNS, rows), F32),
            pltpu.VMEM((nodes, rows, COLUMNS), F32),
        ],
        compiler_params=PARAMS,
        name="backward_out",
    )(*parts)


def body(
    right_side,
    layer_sums,
    lower_blocks,
    upper_blocks,
    lower_inverse,
    upper_diagonal_inverses,
    pattern,
    parents,
):
    nodes = right_side.shape[1]
    part = lower_blocks.shape[2]
    gz_count = lax.axis_size("gz")
    row_count = lax.axis_size("row")
    col_count = lax.axis_size("col")
    own = COLUMNS // gz_count
    lanes = nodes * own
    sizes = (nodes, part, own, row_count, col_count)
    gz = lax.axis_index("gz")

    def tiled(value):
        return value.reshape(4, nodes, part * COLUMNS // LANES, LANES).transpose(0, 2, 1, 3)

    parts = pl.pallas_call(
        functools.partial(input_kernel, gz_count, nodes, own),
        out_shape=[shape_of(part, lanes)] * 4 + [shape_of(4, part, lanes)] * (gz_count - 1),
        in_specs=[VMEM, VMEM],
        out_specs=[VMEM] * (3 + gz_count),
        scratch_shapes=[pltpu.VMEM((4, lanes // LANES, COLUMNS // own, part, LANES), F32)],
        compiler_params=INPUT_PARAMS,
        name="input_parts",
    )(tiled(right_side), tiled(layer_sums[0]))
    kept, away = parts[:4], parts[4:]

    per = upper_blocks.shape[0] // gz_count
    half = lax.dynamic_slice_in_dim(after(upper_blocks, *away), gz * per, per, 0)
    upper_rows = lax.all_gather(half, ("gz", "row"))
    others = [after(swap(away[step - 1], "gz", step), half) for step in steps_of(gz_count)]
    pattern = pattern.T
    initial = [kept[level] + sum(other[level] for other in others) for level in range(4)]

    fulls = [None] * 4
    forward = [None] * 4
    pending = []
    mine = initial[3]
    m = lower_step(3, lower_blocks, lower_inverse)
    for height in (3, 2, 1):
        pieces = gather(mine, "row")
        if height < 3:
            m = lower_step(height, lower_blocks, lower_inverse)
        fulls[height], sends, pending = forward_step(
            height, pieces, parents, pattern, m, pending, sizes
        )
        forward[height] = solve_step(height, fulls[height], lower_inverse, sizes)
        taken = [swap(sends[step], "col", step) for step in steps_of(col_count)]
        taken[-1] = after(taken[-1], *forward[height])
        mine = initial[height - 1] - sends[0] - sum(taken)
    z = middle_step(upper_diagonal_inverses, lower_inverse)
    solved_forward, solved = last_step(gather(mine, "row"), z, sizes)
    forward[0] = (solved_forward,)

    backward = [solved]
    whole = []
    for height in (1, 2, 3):
        start, *composed = descend_step(
            height,
            parents,
            pattern,
            forward[height][1],
            upper_rows,
            upper_diagonal_inverses,
            whole,
            row_count,
        )
        whole = whole + [gather(backward[-1], "col")]
        earlier = backward if height == 3 else []
        results = backward_step(height, parents, pattern, start, composed, whole[-1], earlier)
        backward.append(results)

    forward_parts = [piece for level in forward for piece in with_layers(level[0])]
    forward_all = forward_out(forward_parts, nodes, own, gz_count)
    pieces = gather(backward[3], "row")
    pieces[-1] = after(pieces[-1], forward_all)
    backward_all = backward_out(with_layers(jnp.stack(pieces)), own)
    return tuple(
        value.transpose(0, 2, 1, 3).reshape(4, nodes, WIDTH * COLUMNS)
        for value in (forward_all, backward_all)
    )


def solution(mesh):
    in_specs = (
        P(None, "col", "row"),
        P("gz", None, "col", "row"),
        P(None, "col", "row", None),
        P(None, "col", "row", None),
        P(None, "col", None, None),
        P(None, "col", None, None),
        P(None, "col"),
        P(),
    )
    out_specs = (P(None, "col", None), P(None, "col", None))
    return jax.shard_map(body, mesh=mesh, in_specs=in_specs, out_specs=out_specs, check_vma=False)
```

```python
import functools

import jax
import jax.numpy as jnp
from jax import lax
from jax.experimental import pallas as pl
from jax.experimental.pallas import tpu as pltpu
from jax.sharding import PartitionSpec as P

WIDTH = 256
COLUMNS = 64
LANES = 128
F32 = jnp.float32
BF16 = jnp.bfloat16
SMEM = pl.BlockSpec(memory_space=pltpu.SMEM)
VMEM = pl.BlockSpec(memory_space=pltpu.VMEM)
HBM = pl.BlockSpec(memory_space=pltpu.HBM)
PARAMS = pltpu.CompilerParams(vmem_limit_bytes=16 * 2**20)
INPUT_PARAMS = pltpu.CompilerParams(vmem_limit_bytes=53 * 2**20)
MIDDLE_PARAMS = pltpu.CompilerParams(vmem_limit_bytes=51 * 2**20)
STREAM_PARAMS = pltpu.CompilerParams(vmem_limit_bytes=52 * 2**20)


STEP = 2


def place_of(height, distance):
    return height * (height - 1) // 2 + distance - 1


def shape_of(*dims, dtype=F32):
    return jax.ShapeDtypeStruct(dims, dtype)


def split(value):
    high = value.astype(BF16)
    return high, (value - high.astype(F32)).astype(BF16)


def dot(left, right):
    return jnp.dot(left, right, preferred_element_type=F32)


def dot_t(left, right):
    return lax.dot_general(left, right, (((1,), (1,)), ((), ())), preferred_element_type=F32)


def product(left, right):
    lanes = right[0].shape[1]
    both = dot(left[0], jnp.concatenate(right, axis=1))
    return both[:, :lanes] + both[:, lanes:] + dot(left[1], right[0])


def product_t(left, right):
    rows = left[0].shape[0]
    both = dot_t(jnp.concatenate(left, axis=0), right[0])
    return both[:rows] + both[rows:] + dot_t(left[0], right[1])


def steps_of(count):
    assert count & (count - 1) == 0
    return range(1, count)


def swap(value, axis, step):
    return lax.ppermute(value, axis, [(i, i ^ step) for i in range(lax.axis_size(axis))])


def with_layers(value):
    return [value] + [swap(value, "gz", step) for step in steps_of(lax.axis_size("gz"))]


def after(value, *others):
    return lax.optimization_barrier((value, *others))[0]


def gather(value, axis):
    return [value] + [swap(value, axis, step) for step in steps_of(lax.axis_size(axis))]


def input_kernel(gz_count, nodes, own, right, layer, *outs):
    groups = COLUMNS // own
    kept, away, stage = outs[:4], outs[4:-1], outs[-1]
    gz = lax.axis_index("gz")
    tiles = right.shape[1]
    per_tile = LANES // COLUMNS
    block = lax.broadcasted_iota(jnp.int32, (1, LANES), 1) // own
    for level in range(right.shape[0]):
        for chunk in range(nodes * own // LANES):
            start = chunk * LANES
            lanes = slice(start, start + LANES)
            for row in range(per_tile):
                for which in range(groups):
                    mine = jnp.where(gz == which, 1.0, 0.0)
                    total = jnp.zeros((tiles, LANES), F32)
                    for node in range(start // own, (start + LANES) // own):
                        value = right[level, :, node, :] * mine - layer[level, :, node, :]
                        target = node * own - start
                        shift = (target - row * COLUMNS - which * own) % LANES
                        value = pltpu.roll(value, shift, 1) if shift else value
                        total = jnp.where(block == target // own, value, total)
                    stage[level, chunk, which, pl.ds(row, tiles, stride=per_tile), :] = total
            found = [stage[level, chunk, which] for which in range(groups)]
            for step in range(groups):
                chosen = found[0]
                for which in range(1, groups):
                    chosen = jnp.where((gz ^ step) == which, found[which], chosen)
                if step == 0:
                    kept[level][:, lanes] = chosen
                else:
                    away[step - 1][level, :, lanes] = chosen


def lower_kernel(height, blocks, inverse, high_out, low_out):
    first = place_of(height, 1)
    part, width = blocks.shape[2:]
    for node in range(blocks.shape[1]):
        left = blocks[first : first + height, node].reshape(height * part, width)
        whole = product(split(left), split(inverse[0, node])).reshape(height, part, width)
        high_out[:, node], low_out[:, node] = split(whole)


def lower_step(height, blocks, inverse):
    pairs, nodes, part = blocks.shape[:3]
    out = shape_of(height, nodes, part, WIDTH, dtype=BF16)
    return pl.pallas_call(
        functools.partial(lower_kernel, height),
        grid=(nodes // STEP,),
        out_shape=[out, out],
        in_specs=[
            pl.BlockSpec((pairs, STEP, part, WIDTH), lambda i: (0, i, 0, 0)),
            pl.BlockSpec((1, STEP, WIDTH, WIDTH), lambda i: (height, i, 0, 0)),
        ],
        out_specs=[pl.BlockSpec((height, STEP, part, WIDTH), lambda i: (0, i, 0, 0))] * 2,
        compiler_params=STREAM_PARAMS,
        name="lower_products",
    )(blocks, inverse)


def middle_kernel(upper, lower, high_out, low_out, lower_high, lower_low):
    for node in range(STEP):
        right = split(lower[0, node])
        lower_high[node], lower_low[node] = right
        high_out[node], low_out[node] = split(product(split(upper[0, node]), right))


def middle_step(upper, lower):
    nodes = lower.shape[1]
    out = shape_of(nodes, WIDTH, WIDTH, dtype=BF16)
    return pl.pallas_call(
        middle_kernel,
        grid=(nodes // STEP,),
        out_shape=[out] * 4,
        in_specs=[pl.BlockSpec((1, STEP, WIDTH, WIDTH), lambda i: (0, i, 0, 0))] * 2,
        out_specs=[pl.BlockSpec((STEP, WIDTH, WIDTH), lambda i: (i, 0, 0))] * 4,
        compiler_params=MIDDLE_PARAMS,
        name="middle_product",
    )(upper, lower)


def assemble(pieces, full, part):
    row = lax.axis_index("row")
    for step, piece in enumerate(pieces):
        full[pl.ds(pl.multiple_of((row ^ step) * part, part), part), :] = piece[...]


def forward_kernel(height, sizes, *refs):
    nodes, part, own, row_count, col_count = sizes
    lanes = nodes * own
    pieces, refs = refs[:row_count], refs[row_count:]
    parents, pattern, m_high, m_low = refs[:4]
    pending_in = refs[4 : 4 + height] if height < 3 else ()
    refs = refs[4 + len(pending_in) :]
    full, sends = refs[0], refs[1 : 1 + col_count]
    pending_out = refs[1 + col_count : col_count + height]
    urgent = refs[-1]
    assemble(pieces, full, part)
    lane = lax.broadcasted_iota(jnp.int32, (1, lanes), 1) // own
    col = lax.axis_index("col")
    right = split(full[...])
    targets = []
    for level in range(height):
        target = urgent if level == height - 1 else pending_out[level]
        target[...] = pending_in[level][...] if pending_in else jnp.zeros(target.shape, F32)
        targets.append(target)
    rows = height * nodes * part
    whole = product((m_high[...].reshape(rows, WIDTH), m_low[...].reshape(rows, WIDTH)), right)
    for node in range(nodes):
        ancestor = col * nodes + node
        for distance in range(1, height + 1):
            level = height - distance
            ancestor = parents[level, ancestor]
            slot = lax.rem(ancestor, nodes)
            where = lax.div(ancestor, nodes) ^ col
            start = ((distance - 1) * nodes + node) * part
            term = whole[start : start + part]
            term = pltpu.roll(term, lax.rem(slot - node + nodes, nodes) * own, 1)
            stored = jnp.where(pattern[node, place_of(height, distance)] != 0, slot, -1)
            targets[level][where] += jnp.where(lane == stored, term, 0.0)
    for step in range(col_count):
        sends[step][...] = urgent[step]


def forward_step(height, pieces, parents, pattern, m, pending, sizes):
    nodes, part, own, row_count, col_count = sizes
    lanes = nodes * own
    piece = shape_of(part, lanes)
    stack = shape_of(col_count, part, lanes)
    out_shape = [shape_of(row_count * part, lanes)] + [piece] * col_count + [stack] * (height - 1)
    results = pl.pallas_call(
        functools.partial(forward_kernel, height, sizes),
        out_shape=out_shape,
        in_specs=[VMEM] * len(pieces) + [SMEM, SMEM] + [VMEM] * (2 + len(pending)),
        out_specs=[VMEM] * len(out_shape),
        scratch_shapes=[pltpu.VMEM(stack.shape, F32)],
        compiler_params=PARAMS,
        name="forward_level",
    )(*pieces, parents, pattern, *m, *pending)
    return results[0], results[1 : 1 + col_count], results[1 + col_count :]


def own_rows(turned, node, own, row_count):
    few = own // row_count
    start = node * own + lax.axis_index("row") * few
    return turned[pl.ds(pl.multiple_of(start, few), few), :]


def last_kernel(sizes, *refs):
    nodes, part, own, row_count, col_count = sizes
    pieces = refs[:row_count]
    z_high, z_low, lower_high, lower_low, solved_out, out, full, turned = refs[row_count:]
    assemble(pieces, full, part)
    turned[...] = full[...].T
    for node in range(nodes):
        left = split(own_rows(turned, node, own, row_count))
        out[node] = product_t(left, (z_high[node], z_low[node]))
    lane = lax.broadcasted_iota(jnp.int32, (1, nodes * own), 1) // own
    rows = nodes * WIDTH
    left = (lower_high[...].reshape(rows, WIDTH), lower_low[...].reshape(rows, WIDTH))
    whole = product(left, split(full[...]))
    solved = whole[:WIDTH]
    for node in range(1, nodes):
        solved = jnp.where(lane == node, whole[node * WIDTH : (node + 1) * WIDTH], solved)
    solved_out[...] = solved


def last_step(pieces, matrices, sizes):
    nodes, part, own, row_count, col_count = sizes
    lanes, rows = nodes * own, row_count * part
    return pl.pallas_call(
        functools.partial(last_kernel, sizes),
        out_shape=[shape_of(rows, lanes), shape_of(nodes, own // row_count, rows)],
        in_specs=[VMEM] * (len(pieces) + len(matrices)),
        out_specs=[VMEM] * 2,
        scratch_shapes=[pltpu.VMEM((rows, lanes), F32), pltpu.VMEM((lanes, rows), F32)],
        compiler_params=PARAMS,
        name="forward_last",
    )(*pieces, *matrices)


def solve_kernel(sizes, full, lower, out, own_out, turned):
    nodes, part, own, row_count, col_count = sizes
    first = pl.program_id(0) * STEP
    lane = lax.broadcasted_iota(jnp.int32, (1, nodes * own), 1) // own

    @pl.when(first == 0)
    def _():
        turned[...] = full[...].T
        out[...] = jnp.zeros(out.shape, F32)

    high, low = split(lower[0].reshape(STEP * WIDTH, WIDTH))
    whole = product((high, low), split(full[...]))
    solved = out[...]
    for step in range(STEP):
        node, rows = first + step, slice(step * WIDTH, (step + 1) * WIDTH)
        solved = jnp.where(lane == node, whole[rows], solved)
        left = split(own_rows(turned, node, own, row_count))
        own_out[step] = product_t(left, (high[rows], low[rows]))
    out[...] = solved


def solve_step(height, full, lower, sizes):
    nodes, part, own, row_count, col_count = sizes
    rows, lanes = full.shape
    few = own // row_count
    whole = pl.BlockSpec((rows, lanes), lambda i: (0, 0))
    return pl.pallas_call(
        functools.partial(solve_kernel, sizes),
        grid=(nodes // STEP,),
        out_shape=[shape_of(rows, lanes), shape_of(nodes, few, rows)],
        in_specs=[whole, pl.BlockSpec((1, STEP, rows, rows), lambda i: (height, i, 0, 0))],
        out_specs=[whole, pl.BlockSpec((STEP, few, rows), lambda i: (i, 0, 0))],
        scratch_shapes=[pltpu.VMEM((lanes, rows), F32)],
        compiler_params=STREAM_PARAMS,
        name="solve_level",
    )(full, lower)


def descend_kernel(height, nodes, col_count, parents, pattern, value, inverse, *refs):
    blocks, pieces, (out, high_out, low_out) = refs[:height], refs[height:-3], refs[-3:]
    col = lax.axis_index("col")
    for index in range(STEP):
        node = pl.program_id(0) * STEP + index
        rest = value[index]
        left = split(inverse[0, index])
        ancestor = parents[height - 1, col * nodes + node]
        for distance in range(2, height + 1):
            level = height - distance
            ancestor = parents[level, ancestor]
            where = lax.div(ancestor, nodes) ^ col
            slot = lax.rem(ancestor, nodes)
            chosen = pieces[level * col_count][slot]
            for step in range(1, col_count):
                piece = pieces[level * col_count + step][slot]
                chosen = jnp.where(where == step, piece, chosen)
            block = blocks[distance - 1][:, 0, index].reshape(WIDTH, WIDTH)
            term = product_t(split(chosen), split(block))
            stored = pattern[node, place_of(height, distance)] != 0
            rest = rest - jnp.where(stored, term, 0.0)
        nearest = blocks[0][:, 0, index].reshape(WIDTH, WIDTH)
        high_out[index], low_out[index] = split(product(left, split(nearest)))
        out[index] = product_t(split(rest), left)


def descend_step(height, parents, pattern, value, gathered, inverse, solved, row_count):
    per, nodes, part = gathered.shape[1:4]
    col_count = lax.axis_size("col")
    few, rows = value.shape[1:]
    pieces = [piece for level in solved for piece in level]

    def block_spec(distance):
        place = place_of(height, distance)
        return pl.BlockSpec(
            (row_count, 1, STEP, part, WIDTH), lambda i: (place // per, place % per, i, 0, 0)
        )

    each = pl.BlockSpec((STEP, few, rows), lambda i: (i, 0, 0))
    whole = pl.BlockSpec((nodes, few, rows), lambda i: (0, 0, 0))
    matrix = shape_of(nodes, WIDTH, WIDTH, dtype=BF16)
    return pl.pallas_call(
        functools.partial(descend_kernel, height, nodes, col_count),
        grid=(nodes // STEP,),
        out_shape=[shape_of(nodes, few, rows), matrix, matrix],
        in_specs=[SMEM, SMEM, each]
        + [pl.BlockSpec((1, STEP, WIDTH, WIDTH), lambda i: (height, i, 0, 0))]
        + [block_spec(distance) for distance in range(1, height + 1)]
        + [whole] * len(pieces),
        out_specs=[each] + [pl.BlockSpec((STEP, WIDTH, WIDTH), lambda i: (i, 0, 0))] * 2,
        compiler_params=STREAM_PARAMS,
        name="descend_level",
    )(parents, pattern, value, inverse, *([gathered] * height), *pieces)


def backward_kernel(height, nodes, col_count, parents, pattern, start, high, low, *refs):
    pieces, earlier, (out, solved) = refs[:col_count], refs[col_count:-2], refs[-2:]
    for step, piece in enumerate(pieces):
        solved[step] = piece[...]
    for level, value in enumerate(earlier):
        out[level] = value[...]
    col = lax.axis_index("col")
    for node in range(nodes):
        ancestor = parents[height - 1, col * nodes + node]
        where = lax.div(ancestor, nodes) ^ col
        left = split(solved[where, lax.rem(ancestor, nodes)])
        term = product_t(left, (high[node], low[node]))
        stored = pattern[node, place_of(height, 1)] != 0
        total = start[node] - jnp.where(stored, term, 0.0)
        if earlier:
            out[height, node] = total
        else:
            out[node] = total


def backward_step(height, parents, pattern, start, composed, pieces, earlier):
    out = ((1 + len(earlier),) if earlier else ()) + start.shape
    return pl.pallas_call(
        functools.partial(backward_kernel, height, start.shape[0], len(pieces)),
        out_shape=shape_of(*out),
        in_specs=[SMEM, SMEM] + [VMEM] * (3 + len(pieces) + len(earlier)),
        out_specs=VMEM,
        scratch_shapes=[pltpu.VMEM((len(pieces),) + start.shape, F32)],
        compiler_params=PARAMS,
        name="backward_level",
    )(parents, pattern, start, *composed, *pieces, *earlier)


def groups_found(found, groups):
    gz = lax.axis_index("gz")
    values = []
    for which in range(groups):
        value = found[0]
        for step in range(1, groups):
            value = jnp.where((gz ^ step) == which, found[step], value)
        values.append(value)
    return values


def forward_out_kernel(gz_count, nodes, own, *refs):
    parts, out, stage = refs[:-2], refs[-2], refs[-1]
    groups = COLUMNS // own
    per_tile = LANES // COLUMNS
    tiles = out.shape[1]
    block = lax.broadcasted_iota(jnp.int32, (1, LANES), 1) // own
    for level in range(out.shape[0]):
        for chunk in range(nodes * own // LANES):
            start = chunk * LANES
            lanes = slice(start, start + LANES)
            found = [part[:, lanes] for part in parts[level * gz_count : (level + 1) * gz_count]]
            for which, value in enumerate(groups_found(found, groups)):
                stage[chunk, which] = value
            values = [
                stage[chunk, which, pl.ds(row, tiles, stride=per_tile), :]
                for row in range(per_tile)
                for which in range(groups)
            ]
            for node in range(start // own, (start + LANES) // own):
                total = jnp.zeros((tiles, LANES), F32)
                for place, value in enumerate(values):
                    shift = (place * own - (node * own - start)) % LANES
                    value = pltpu.roll(value, shift, 1) if shift else value
                    total = jnp.where(block == place, value, total)
                out[level, :, node, :] = total


def forward_out(parts, nodes, own, gz_count):
    rows, lanes = parts[0].shape
    tiles = rows * COLUMNS // LANES
    return pl.pallas_call(
        functools.partial(forward_out_kernel, gz_count, nodes, own),
        out_shape=shape_of(len(parts) // gz_count, tiles, nodes, LANES),
        in_specs=[VMEM] * len(parts),
        out_specs=VMEM,
        scratch_shapes=[pltpu.VMEM((lanes // LANES, COLUMNS // own, rows, LANES), F32)],
        compiler_params=PARAMS,
        name="forward_out",
    )(*parts)


def backward_out_kernel(nodes, gz_count, own, *refs):
    parts, (out, columns, turned) = refs[:-3], refs[-3:]
    groups = COLUMNS // own
    per_tile = LANES // COLUMNS
    tiles = out.shape[1]
    row_count, _, _, few, _ = parts[0].shape
    row = lax.axis_index("row")
    for node in range(nodes):
        for step in range(row_count):
            values = groups_found([part[step, 0, node] for part in parts], groups)
            for which, value in enumerate(values):
                index = which * row_count + (row ^ step)
                columns[node, pl.ds(pl.multiple_of(index * few, few), few), :] = value
        turned[node] = columns[node].T
        rows = [turned[node, pl.ds(step, tiles, stride=per_tile), :] for step in range(per_tile)]
        out[0, :, node, :] = jnp.concatenate(rows, axis=1)


def backward_out(parts, own):
    row_count, levels, nodes, few, rows = parts[0].shape
    tiles = rows * COLUMNS // LANES
    part_spec = pl.BlockSpec((row_count, 1, nodes, few, rows), lambda i: (0, i, 0, 0, 0))
    return pl.pallas_call(
        functools.partial(backward_out_kernel, nodes, len(parts), own),
        grid=(levels,),
        out_shape=shape_of(levels, tiles, nodes, LANES),
        in_specs=[part_spec] * len(parts),
        out_specs=pl.BlockSpec((1, tiles, nodes, LANES), lambda i: (i, 0, 0, 0)),
        scratch_shapes=[
            pltpu.VMEM((nodes, COLUMNS, rows), F32),
            pltpu.VMEM((nodes, rows, COLUMNS), F32),
        ],
        compiler_params=PARAMS,
        name="backward_out",
    )(*parts)


def body(
    right_side,
    layer_sums,
    lower_blocks,
    upper_blocks,
    lower_inverse,
    upper_diagonal_inverses,
    pattern,
    parents,
):
    nodes = right_side.shape[1]
    part = lower_blocks.shape[2]
    gz_count = lax.axis_size("gz")
    row_count = lax.axis_size("row")
    col_count = lax.axis_size("col")
    own = COLUMNS // gz_count
    lanes = nodes * own
    sizes = (nodes, part, own, row_count, col_count)
    gz = lax.axis_index("gz")

    def tiled(value):
        return value.reshape(4, nodes, part * COLUMNS // LANES, LANES).transpose(0, 2, 1, 3)

    parts = pl.pallas_call(
        functools.partial(input_kernel, gz_count, nodes, own),
        out_shape=[shape_of(part, lanes)] * 4 + [shape_of(4, part, lanes)] * (gz_count - 1),
        in_specs=[VMEM, VMEM],
        out_specs=[VMEM] * (3 + gz_count),
        scratch_shapes=[pltpu.VMEM((4, lanes // LANES, COLUMNS // own, part, LANES), F32)],
        compiler_params=INPUT_PARAMS,
        name="input_parts",
    )(tiled(right_side), tiled(layer_sums[0]))
    kept, away = parts[:4], parts[4:]

    per = upper_blocks.shape[0] // gz_count
    half = lax.dynamic_slice_in_dim(after(upper_blocks, *away), gz * per, per, 0)
    upper_rows = lax.all_gather(half, ("gz", "row"))
    others = [after(swap(away[step - 1], "gz", step), half) for step in steps_of(gz_count)]
    pattern = pattern.T
    initial = [kept[level] + sum(other[level] for other in others) for level in range(4)]

    fulls = [None] * 4
    forward = [None] * 4
    pending = []
    mine = initial[3]
    m = lower_step(3, lower_blocks, lower_inverse)
    for height in (3, 2, 1):
        pieces = gather(mine, "row")
        if height < 3:
            m = lower_step(height, lower_blocks, lower_inverse)
        fulls[height], sends, pending = forward_step(
            height, pieces, parents, pattern, m, pending, sizes
        )
        forward[height] = solve_step(height, fulls[height], lower_inverse, sizes)
        taken = [swap(sends[step], "col", step) for step in steps_of(col_count)]
        taken[-1] = after(taken[-1], *forward[height])
        mine = initial[height - 1] - sends[0] - sum(taken)
    z = middle_step(upper_diagonal_inverses, lower_inverse)
    solved_forward, solved = last_step(gather(mine, "row"), z, sizes)
    forward[0] = (solved_forward,)

    backward = [solved]
    whole = []
    for height in (1, 2, 3):
        start, *composed = descend_step(
            height,
            parents,
            pattern,
            forward[height][1],
            upper_rows,
            upper_diagonal_inverses,
            whole,
            row_count,
        )
        whole = whole + [gather(backward[-1], "col")]
        earlier = backward if height == 3 else []
        results = backward_step(height, parents, pattern, start, composed, whole[-1], earlier)
        backward.append(results)

    forward_parts = [piece for level in forward for piece in with_layers(level[0])]
    forward_all = forward_out(forward_parts, nodes, own, gz_count)
    pieces = gather(backward[3], "row")
    pieces[-1] = after(pieces[-1], forward_all)
    backward_all = backward_out(with_layers(jnp.stack(pieces)), own)
    return tuple(
        value.transpose(0, 2, 1, 3).reshape(4, nodes, WIDTH * COLUMNS)
        for value in (forward_all, backward_all)
    )


def solution(mesh):
    in_specs = (
        P(None, "col", "row"),
        P("gz", None, "col", "row"),
        P(None, "col", "row", None),
        P(None, "col", "row", None),
        P(None, "col", None, None),
        P(None, "col", None, None),
        P(None, "col"),
        P(),
    )
    out_specs = (P(None, "col", None), P(None, "col", None))
    return jax.shard_map(body, mesh=mesh, in_specs=in_specs, out_specs=out_specs, check_vma=False)
```

```python
import functools

import jax
import jax.numpy as jnp
from jax import lax
from jax.experimental import pallas as pl
from jax.experimental.pallas import tpu as pltpu
from jax.sharding import PartitionSpec as P

WIDTH = 256
COLUMNS = 64
LANES = 128
F32 = jnp.float32
BF16 = jnp.bfloat16
SMEM = pl.BlockSpec(memory_space=pltpu.SMEM)
VMEM = pl.BlockSpec(memory_space=pltpu.VMEM)
HBM = pl.BlockSpec(memory_space=pltpu.HBM)
PARAMS = pltpu.CompilerParams(vmem_limit_bytes=16 * 2**20)
INPUT_PARAMS = pltpu.CompilerParams(vmem_limit_bytes=107 * 2**19)
MIDDLE_PARAMS = pltpu.CompilerParams(vmem_limit_bytes=51 * 2**20)
STREAM_PARAMS = pltpu.CompilerParams(vmem_limit_bytes=52 * 2**20)


STEP = 2


def place_of(height, distance):
    return height * (height - 1) // 2 + distance - 1


def shape_of(*dims, dtype=F32):
    return jax.ShapeDtypeStruct(dims, dtype)


def split(value):
    high = value.astype(BF16)
    return high, (value - high.astype(F32)).astype(BF16)


def dot(left, right):
    return jnp.dot(left, right, preferred_element_type=F32)


def dot_t(left, right):
    return lax.dot_general(left, right, (((1,), (1,)), ((), ())), preferred_element_type=F32)


def product(left, right):
    lanes = right[0].shape[1]
    both = dot(left[0], jnp.concatenate(right, axis=1))
    return both[:, :lanes] + both[:, lanes:] + dot(left[1], right[0])


def product_t(left, right):
    rows = left[0].shape[0]
    both = dot_t(jnp.concatenate(left, axis=0), right[0])
    return both[:rows] + both[rows:] + dot_t(left[0], right[1])


def steps_of(count):
    assert count & (count - 1) == 0
    return range(1, count)


def swap(value, axis, step):
    return lax.ppermute(value, axis, [(i, i ^ step) for i in range(lax.axis_size(axis))])


def with_layers(value):
    return [value] + [swap(value, "gz", step) for step in steps_of(lax.axis_size("gz"))]


def after(value, *others):
    return lax.optimization_barrier((value, *others))[0]


def gather(value, axis):
    return [value] + [swap(value, axis, step) for step in steps_of(lax.axis_size(axis))]


def input_kernel(gz_count, nodes, own, right, layer, *outs):
    groups = COLUMNS // own
    kept, away, stage = outs[:4], outs[4:-1], outs[-1]
    gz = lax.axis_index("gz")
    tiles = right.shape[1]
    per_tile = LANES // COLUMNS
    block = lax.broadcasted_iota(jnp.int32, (1, LANES), 1) // own
    for level in range(right.shape[0]):
        for chunk in range(nodes * own // LANES):
            start = chunk * LANES
            lanes = slice(start, start + LANES)
            for row in range(per_tile):
                for which in range(groups):
                    mine = jnp.where(gz == which, 1.0, 0.0)
                    total = jnp.zeros((tiles, LANES), F32)
                    for node in range(start // own, (start + LANES) // own):
                        value = right[level, :, node, :] * mine - layer[level, :, node, :]
                        target = node * own - start
                        shift = (target - row * COLUMNS - which * own) % LANES
                        value = pltpu.roll(value, shift, 1) if shift else value
                        total = jnp.where(block == target // own, value, total)
                    stage[level, chunk, which, pl.ds(row, tiles, stride=per_tile), :] = total
            found = [stage[level, chunk, which] for which in range(groups)]
            for step in range(groups):
                chosen = found[0]
                for which in range(1, groups):
                    chosen = jnp.where((gz ^ step) == which, found[which], chosen)
                if step == 0:
                    kept[level][:, lanes] = chosen
                else:
                    away[step - 1][level, :, lanes] = chosen


def lower_kernel(height, blocks, inverse, high_out, low_out):
    first = place_of(height, 1)
    part, width = blocks.shape[2:]
    for node in range(blocks.shape[1]):
        left = blocks[first : first + height, node].reshape(height * part, width)
        whole = product(split(left), split(inverse[0, node])).reshape(height, part, width)
        high_out[:, node], low_out[:, node] = split(whole)


def lower_step(height, blocks, inverse):
    pairs, nodes, part = blocks.shape[:3]
    out = shape_of(height, nodes, part, WIDTH, dtype=BF16)
    return pl.pallas_call(
        functools.partial(lower_kernel, height),
        grid=(nodes // STEP,),
        out_shape=[out, out],
        in_specs=[
            pl.BlockSpec((pairs, STEP, part, WIDTH), lambda i: (0, i, 0, 0)),
            pl.BlockSpec((1, STEP, WIDTH, WIDTH), lambda i: (height, i, 0, 0)),
        ],
        out_specs=[pl.BlockSpec((height, STEP, part, WIDTH), lambda i: (0, i, 0, 0))] * 2,
        compiler_params=STREAM_PARAMS,
        name="lower_products",
    )(blocks, inverse)


def middle_kernel(upper, lower, high_out, low_out, lower_high, lower_low):
    for node in range(STEP):
        right = split(lower[0, node])
        lower_high[node], lower_low[node] = right
        high_out[node], low_out[node] = split(product(split(upper[0, node]), right))


def middle_step(upper, lower):
    nodes = lower.shape[1]
    out = shape_of(nodes, WIDTH, WIDTH, dtype=BF16)
    return pl.pallas_call(
        middle_kernel,
        grid=(nodes // STEP,),
        out_shape=[out] * 4,
        in_specs=[pl.BlockSpec((1, STEP, WIDTH, WIDTH), lambda i: (0, i, 0, 0))] * 2,
        out_specs=[pl.BlockSpec((STEP, WIDTH, WIDTH), lambda i: (i, 0, 0))] * 4,
        compiler_params=MIDDLE_PARAMS,
        name="middle_product",
    )(upper, lower)


def assemble(pieces, full, part):
    row = lax.axis_index("row")
    for step, piece in enumerate(pieces):
        full[pl.ds(pl.multiple_of((row ^ step) * part, part), part), :] = piece[...]


def forward_kernel(height, sizes, *refs):
    nodes, part, own, row_count, col_count = sizes
    lanes = nodes * own
    pieces, refs = refs[:row_count], refs[row_count:]
    parents, pattern, m_high, m_low = refs[:4]
    pending_in = refs[4 : 4 + height] if height < 3 else ()
    refs = refs[4 + len(pending_in) :]
    full, sends = refs[0], refs[1 : 1 + col_count]
    pending_out = refs[1 + col_count : col_count + height]
    urgent = refs[-1]
    assemble(pieces, full, part)
    lane = lax.broadcasted_iota(jnp.int32, (1, lanes), 1) // own
    col = lax.axis_index("col")
    right = split(full[...])
    targets = []
    for level in range(height):
        target = urgent if level == height - 1 else pending_out[level]
        target[...] = pending_in[level][...] if pending_in else jnp.zeros(target.shape, F32)
        targets.append(target)
    rows = height * nodes * part
    whole = product((m_high[...].reshape(rows, WIDTH), m_low[...].reshape(rows, WIDTH)), right)
    for node in range(nodes):
        ancestor = col * nodes + node
        for distance in range(1, height + 1):
            level = height - distance
            ancestor = parents[level, ancestor]
            slot = lax.rem(ancestor, nodes)
            where = lax.div(ancestor, nodes) ^ col
            start = ((distance - 1) * nodes + node) * part
            term = whole[start : start + part]
            term = pltpu.roll(term, lax.rem(slot - node + nodes, nodes) * own, 1)
            stored = jnp.where(pattern[node, place_of(height, distance)] != 0, slot, -1)
            targets[level][where] += jnp.where(lane == stored, term, 0.0)
    for step in range(col_count):
        sends[step][...] = urgent[step]


def forward_step(height, pieces, parents, pattern, m, pending, sizes):
    nodes, part, own, row_count, col_count = sizes
    lanes = nodes * own
    piece = shape_of(part, lanes)
    stack = shape_of(col_count, part, lanes)
    out_shape = [shape_of(row_count * part, lanes)] + [piece] * col_count + [stack] * (height - 1)
    results = pl.pallas_call(
        functools.partial(forward_kernel, height, sizes),
        out_shape=out_shape,
        in_specs=[VMEM] * len(pieces) + [SMEM, SMEM] + [VMEM] * (2 + len(pending)),
        out_specs=[VMEM] * len(out_shape),
        scratch_shapes=[pltpu.VMEM(stack.shape, F32)],
        compiler_params=PARAMS,
        name="forward_level",
    )(*pieces, parents, pattern, *m, *pending)
    return results[0], results[1 : 1 + col_count], results[1 + col_count :]


def own_rows(turned, node, own, row_count):
    few = own // row_count
    start = node * own + lax.axis_index("row") * few
    return turned[pl.ds(pl.multiple_of(start, few), few), :]


def last_kernel(sizes, *refs):
    nodes, part, own, row_count, col_count = sizes
    pieces = refs[:row_count]
    z_high, z_low, lower_high, lower_low, solved_out, out, full, turned = refs[row_count:]
    assemble(pieces, full, part)
    turned[...] = full[...].T
    for node in range(nodes):
        left = split(own_rows(turned, node, own, row_count))
        out[node] = product_t(left, (z_high[node], z_low[node]))
    lane = lax.broadcasted_iota(jnp.int32, (1, nodes * own), 1) // own
    rows = nodes * WIDTH
    left = (lower_high[...].reshape(rows, WIDTH), lower_low[...].reshape(rows, WIDTH))
    whole = product(left, split(full[...]))
    solved = whole[:WIDTH]
    for node in range(1, nodes):
        solved = jnp.where(lane == node, whole[node * WIDTH : (node + 1) * WIDTH], solved)
    solved_out[...] = solved


def last_step(pieces, matrices, sizes):
    nodes, part, own, row_count, col_count = sizes
    lanes, rows = nodes * own, row_count * part
    return pl.pallas_call(
        functools.partial(last_kernel, sizes),
        out_shape=[shape_of(rows, lanes), shape_of(nodes, own // row_count, rows)],
        in_specs=[VMEM] * (len(pieces) + len(matrices)),
        out_specs=[VMEM] * 2,
        scratch_shapes=[pltpu.VMEM((rows, lanes), F32), pltpu.VMEM((lanes, rows), F32)],
        compiler_params=PARAMS,
        name="forward_last",
    )(*pieces, *matrices)


def solve_kernel(sizes, full, lower, out, own_out, turned):
    nodes, part, own, row_count, col_count = sizes
    first = pl.program_id(0) * STEP
    lane = lax.broadcasted_iota(jnp.int32, (1, nodes * own), 1) // own

    @pl.when(first == 0)
    def _():
        turned[...] = full[...].T
        out[...] = jnp.zeros(out.shape, F32)

    high, low = split(lower[0].reshape(STEP * WIDTH, WIDTH))
    whole = product((high, low), split(full[...]))
    solved = out[...]
    for step in range(STEP):
        node, rows = first + step, slice(step * WIDTH, (step + 1) * WIDTH)
        solved = jnp.where(lane == node, whole[rows], solved)
        left = split(own_rows(turned, node, own, row_count))
        own_out[step] = product_t(left, (high[rows], low[rows]))
    out[...] = solved


def solve_step(height, full, lower, sizes):
    nodes, part, own, row_count, col_count = sizes
    rows, lanes = full.shape
    few = own // row_count
    whole = pl.BlockSpec((rows, lanes), lambda i: (0, 0))
    return pl.pallas_call(
        functools.partial(solve_kernel, sizes),
        grid=(nodes // STEP,),
        out_shape=[shape_of(rows, lanes), shape_of(nodes, few, rows)],
        in_specs=[whole, pl.BlockSpec((1, STEP, rows, rows), lambda i: (height, i, 0, 0))],
        out_specs=[whole, pl.BlockSpec((STEP, few, rows), lambda i: (i, 0, 0))],
        scratch_shapes=[pltpu.VMEM((lanes, rows), F32)],
        compiler_params=STREAM_PARAMS,
        name="solve_level",
    )(full, lower)


def descend_kernel(height, nodes, col_count, parents, pattern, value, inverse, *refs):
    blocks, pieces, outs = refs[:height], refs[height:-4], refs[-4:]
    out, high_out, low_out, choice = outs
    col = lax.axis_index("col")
    places = lax.broadcasted_iota(jnp.int32, choice.shape[1:], 0)
    for index in range(STEP):
        node = pl.program_id(0) * STEP + index
        rest = value[index]
        left = split(inverse[0, index])
        ancestor = parents[height - 1, col * nodes + node]
        place = (lax.div(ancestor, nodes) ^ col) * nodes + lax.rem(ancestor, nodes)
        place = jnp.where(pattern[node, place_of(height, 1)] != 0, place, -1)
        choice[index] = jnp.where(places == place, 1.0, 0.0)
        for distance in range(2, height + 1):
            level = height - distance
            ancestor = parents[level, ancestor]
            where = lax.div(ancestor, nodes) ^ col
            slot = lax.rem(ancestor, nodes)
            chosen = pieces[level * col_count][slot]
            for step in range(1, col_count):
                piece = pieces[level * col_count + step][slot]
                chosen = jnp.where(where == step, piece, chosen)
            block = blocks[distance - 1][:, 0, index].reshape(WIDTH, WIDTH)
            term = product_t(split(chosen), split(block))
            stored = pattern[node, place_of(height, distance)] != 0
            rest = rest - jnp.where(stored, term, 0.0)
        nearest = blocks[0][:, 0, index].reshape(WIDTH, WIDTH)
        high_out[index], low_out[index] = split(product(left, split(nearest)))
        out[index] = product_t(split(rest), left)


def descend_step(height, parents, pattern, value, gathered, inverse, solved, row_count):
    per, nodes, part = gathered.shape[1:4]
    col_count = lax.axis_size("col")
    few, rows = value.shape[1:]
    pieces = [piece for level in solved for piece in level]

    def block_spec(distance):
        place = place_of(height, distance)
        return pl.BlockSpec(
            (row_count, 1, STEP, part, WIDTH), lambda i: (place // per, place % per, i, 0, 0)
        )

    each = pl.BlockSpec((STEP, few, rows), lambda i: (i, 0, 0))
    whole = pl.BlockSpec((nodes, few, rows), lambda i: (0, 0, 0))
    matrix = shape_of(nodes, WIDTH, WIDTH, dtype=BF16)
    return pl.pallas_call(
        functools.partial(descend_kernel, height, nodes, col_count),
        grid=(nodes // STEP,),
        out_shape=[
            shape_of(nodes, few, rows),
            matrix,
            matrix,
            shape_of(nodes, col_count * nodes, rows),
        ],
        in_specs=[SMEM, SMEM, each]
        + [pl.BlockSpec((1, STEP, WIDTH, WIDTH), lambda i: (height, i, 0, 0))]
        + [block_spec(distance) for distance in range(1, height + 1)]
        + [whole] * len(pieces),
        out_specs=[each]
        + [pl.BlockSpec((STEP, WIDTH, WIDTH), lambda i: (i, 0, 0))] * 2
        + [pl.BlockSpec((STEP, col_count * nodes, rows), lambda i: (i, 0, 0))],
        compiler_params=STREAM_PARAMS,
        name="descend_level",
    )(parents, pattern, value, inverse, *([gathered] * height), *pieces)


def backward_kernel(height, start, high, low, choice, *refs):
    nodes, count = choice.shape[0], choice.shape[1] // choice.shape[0]
    pieces, earlier, out = refs[:count], refs[count:-1], refs[-1]
    for level, value in enumerate(earlier):
        out[level] = value[...]
    for node in range(nodes):
        chosen = jnp.zeros(start.shape[1:], F32)
        for place in range(count * nodes):
            weight = choice[node, place : place + 1, :]
            chosen = chosen + weight * pieces[place // nodes][place % nodes]
        total = start[node] - product_t(split(chosen), (high[node], low[node]))
        if earlier:
            out[height, node] = total
        else:
            out[node] = total


def backward_step(height, parts, pieces, earlier):
    start = parts[0].shape
    return pl.pallas_call(
        functools.partial(backward_kernel, height),
        out_shape=shape_of(*(((1 + len(earlier),) if earlier else ()) + start)),
        in_specs=[VMEM] * (len(parts) + len(pieces) + len(earlier)),
        out_specs=VMEM,
        compiler_params=PARAMS,
        name="backward_level",
    )(*parts, *pieces, *earlier)


def groups_found(found, groups):
    gz = lax.axis_index("gz")
    values = []
    for which in range(groups):
        value = found[0]
        for step in range(1, groups):
            value = jnp.where((gz ^ step) == which, found[step], value)
        values.append(value)
    return values


def forward_out_kernel(gz_count, nodes, own, *refs):
    parts, out, stage = refs[:-2], refs[-2], refs[-1]
    groups = COLUMNS // own
    per_tile = LANES // COLUMNS
    tiles = out.shape[1]
    block = lax.broadcasted_iota(jnp.int32, (1, LANES), 1) // own
    for level in range(out.shape[0]):
        for chunk in range(nodes * own // LANES):
            start = chunk * LANES
            lanes = slice(start, start + LANES)
            found = [part[:, lanes] for part in parts[level * gz_count : (level + 1) * gz_count]]
            for which, value in enumerate(groups_found(found, groups)):
                stage[chunk, which] = value
            values = [
                stage[chunk, which, pl.ds(row, tiles, stride=per_tile), :]
                for row in range(per_tile)
                for which in range(groups)
            ]
            for node in range(start // own, (start + LANES) // own):
                total = jnp.zeros((tiles, LANES), F32)
                for place, value in enumerate(values):
                    shift = (place * own - (node * own - start)) % LANES
                    value = pltpu.roll(value, shift, 1) if shift else value
                    total = jnp.where(block == place, value, total)
                out[level, :, node, :] = total


def forward_out(parts, nodes, own, gz_count):
    rows, lanes = parts[0].shape
    tiles = rows * COLUMNS // LANES
    return pl.pallas_call(
        functools.partial(forward_out_kernel, gz_count, nodes, own),
        out_shape=shape_of(len(parts) // gz_count, tiles, nodes, LANES),
        in_specs=[VMEM] * len(parts),
        out_specs=VMEM,
        scratch_shapes=[pltpu.VMEM((lanes // LANES, COLUMNS // own, rows, LANES), F32)],
        compiler_params=PARAMS,
        name="forward_out",
    )(*parts)


def backward_out_kernel(nodes, gz_count, own, *refs):
    parts, (out, columns, turned) = refs[:-3], refs[-3:]
    groups = COLUMNS // own
    per_tile = LANES // COLUMNS
    tiles = out.shape[1]
    row_count, _, _, few, _ = parts[0].shape
    row = lax.axis_index("row")
    for node in range(nodes):
        for step in range(row_count):
            values = groups_found([part[step, 0, node] for part in parts], groups)
            for which, value in enumerate(values):
                index = which * row_count + (row ^ step)
                columns[node, pl.ds(pl.multiple_of(index * few, few), few), :] = value
        turned[node] = columns[node].T
        rows = [turned[node, pl.ds(step, tiles, stride=per_tile), :] for step in range(per_tile)]
        out[0, :, node, :] = jnp.concatenate(rows, axis=1)


def backward_out(parts, own):
    row_count, levels, nodes, few, rows = parts[0].shape
    tiles = rows * COLUMNS // LANES
    part_spec = pl.BlockSpec((row_count, 1, nodes, few, rows), lambda i: (0, i, 0, 0, 0))
    return pl.pallas_call(
        functools.partial(backward_out_kernel, nodes, len(parts), own),
        grid=(levels,),
        out_shape=shape_of(levels, tiles, nodes, LANES),
        in_specs=[part_spec] * len(parts),
        out_specs=pl.BlockSpec((1, tiles, nodes, LANES), lambda i: (i, 0, 0, 0)),
        scratch_shapes=[
            pltpu.VMEM((nodes, COLUMNS, rows), F32),
            pltpu.VMEM((nodes, rows, COLUMNS), F32),
        ],
        compiler_params=PARAMS,
        name="backward_out",
    )(*parts)


def body(
    right_side,
    layer_sums,
    lower_blocks,
    upper_blocks,
    lower_inverse,
    upper_diagonal_inverses,
    pattern,
    parents,
):
    nodes = right_side.shape[1]
    part = lower_blocks.shape[2]
    gz_count = lax.axis_size("gz")
    row_count = lax.axis_size("row")
    col_count = lax.axis_size("col")
    own = COLUMNS // gz_count
    lanes = nodes * own
    sizes = (nodes, part, own, row_count, col_count)
    gz = lax.axis_index("gz")

    def tiled(value):
        return value.reshape(4, nodes, part * COLUMNS // LANES, LANES).transpose(0, 2, 1, 3)

    parts = pl.pallas_call(
        functools.partial(input_kernel, gz_count, nodes, own),
        out_shape=[shape_of(part, lanes)] * 4 + [shape_of(4, part, lanes)] * (gz_count - 1),
        in_specs=[VMEM, VMEM],
        out_specs=[VMEM] * (3 + gz_count),
        scratch_shapes=[pltpu.VMEM((4, lanes // LANES, COLUMNS // own, part, LANES), F32)],
        compiler_params=INPUT_PARAMS,
        name="input_parts",
    )(tiled(right_side), tiled(layer_sums[0]))
    kept, away = parts[:4], parts[4:]

    per = upper_blocks.shape[0] // gz_count
    half = lax.dynamic_slice_in_dim(after(upper_blocks, *away), gz * per, per, 0)
    upper_rows = lax.all_gather(half, ("gz", "row"))
    others = [after(swap(away[step - 1], "gz", step), half) for step in steps_of(gz_count)]
    pattern = pattern.T
    initial = [kept[level] + sum(other[level] for other in others) for level in range(4)]

    fulls = [None] * 4
    forward = [None] * 4
    pending = []
    mine = initial[3]
    m = lower_step(3, lower_blocks, lower_inverse)
    for height in (3, 2, 1):
        pieces = gather(mine, "row")
        if height < 3:
            m = lower_step(height, lower_blocks, lower_inverse)
        fulls[height], sends, pending = forward_step(
            height, pieces, parents, pattern, m, pending, sizes
        )
        forward[height] = solve_step(height, fulls[height], lower_inverse, sizes)
        taken = [swap(sends[step], "col", step) for step in steps_of(col_count)]
        taken[-1] = after(taken[-1], *forward[height])
        mine = initial[height - 1] - sends[0] - sum(taken)
    z = middle_step(upper_diagonal_inverses, lower_inverse)
    solved_forward, solved = last_step(gather(mine, "row"), z, sizes)
    forward[0] = (solved_forward,)

    backward = [solved]
    whole = []
    for height in (1, 2, 3):
        parts = descend_step(
            height,
            parents,
            pattern,
            forward[height][1],
            upper_rows,
            upper_diagonal_inverses,
            whole,
            row_count,
        )
        whole = whole + [gather(backward[-1], "col")]
        earlier = backward if height == 3 else []
        backward.append(backward_step(height, parts, whole[-1], earlier))

    forward_parts = [piece for level in forward for piece in with_layers(level[0])]
    forward_all = forward_out(forward_parts, nodes, own, gz_count)
    pieces = gather(backward[3], "row")
    pieces[-1] = after(pieces[-1], forward_all)
    backward_all = backward_out(with_layers(jnp.stack(pieces)), own)
    return tuple(
        value.transpose(0, 2, 1, 3).reshape(4, nodes, WIDTH * COLUMNS)
        for value in (forward_all, backward_all)
    )


def solution(mesh):
    in_specs = (
        P(None, "col", "row"),
        P("gz", None, "col", "row"),
        P(None, "col", "row", None),
        P(None, "col", "row", None),
        P(None, "col", None, None),
        P(None, "col", None, None),
        P(None, "col"),
        P(),
    )
    out_specs = (P(None, "col", None), P(None, "col", None))
    return jax.shard_map(body, mesh=mesh, in_specs=in_specs, out_specs=out_specs, check_vma=False)
```

```python
import functools

import jax
import jax.numpy as jnp
from jax import lax
from jax.experimental import pallas as pl
from jax.experimental.pallas import tpu as pltpu
from jax.sharding import PartitionSpec as P

WIDTH = 256
COLUMNS = 64
LANES = 128
F32 = jnp.float32
BF16 = jnp.bfloat16
SMEM = pl.BlockSpec(memory_space=pltpu.SMEM)
VMEM = pl.BlockSpec(memory_space=pltpu.VMEM)
HBM = pl.BlockSpec(memory_space=pltpu.HBM)
PARAMS = pltpu.CompilerParams(vmem_limit_bytes=16 * 2**20)
INPUT_PARAMS = pltpu.CompilerParams(vmem_limit_bytes=107 * 2**19)
MIDDLE_PARAMS = pltpu.CompilerParams(vmem_limit_bytes=51 * 2**20)
STREAM_PARAMS = pltpu.CompilerParams(vmem_limit_bytes=52 * 2**20)


STEP = 2


def place_of(height, distance):
    return height * (height - 1) // 2 + distance - 1


def shape_of(*dims, dtype=F32):
    return jax.ShapeDtypeStruct(dims, dtype)


def split(value):
    high = value.astype(BF16)
    return high, (value - high.astype(F32)).astype(BF16)


def dot(left, right):
    return jnp.dot(left, right, preferred_element_type=F32)


def dot_t(left, right):
    return lax.dot_general(left, right, (((1,), (1,)), ((), ())), preferred_element_type=F32)


def product(left, right):
    lanes = right[0].shape[1]
    both = dot(left[0], jnp.concatenate(right, axis=1))
    return both[:, :lanes] + both[:, lanes:] + dot(left[1], right[0])


def product_t(left, right):
    rows = left[0].shape[0]
    both = dot_t(jnp.concatenate(left, axis=0), right[0])
    return both[:rows] + both[rows:] + dot_t(left[0], right[1])


def steps_of(count):
    assert count & (count - 1) == 0
    return range(1, count)


def swap(value, axis, step):
    return lax.ppermute(value, axis, [(i, i ^ step) for i in range(lax.axis_size(axis))])


def with_layers(value):
    return [value] + [swap(value, "gz", step) for step in steps_of(lax.axis_size("gz"))]


def after(value, *others):
    return lax.optimization_barrier((value, *others))[0]


def gather(value, axis):
    return [value] + [swap(value, axis, step) for step in steps_of(lax.axis_size(axis))]


def input_kernel(gz_count, nodes, own, right, layer, *outs):
    groups = COLUMNS // own
    kept, away, stage = outs[:4], outs[4:-1], outs[-1]
    gz = lax.axis_index("gz")
    tiles = right.shape[1]
    per_tile = LANES // COLUMNS
    block = lax.broadcasted_iota(jnp.int32, (1, LANES), 1) // own
    for level in range(right.shape[0]):
        for chunk in range(nodes * own // LANES):
            start = chunk * LANES
            lanes = slice(start, start + LANES)
            for row in range(per_tile):
                for which in range(groups):
                    mine = jnp.where(gz == which, 1.0, 0.0)
                    total = jnp.zeros((tiles, LANES), F32)
                    for node in range(start // own, (start + LANES) // own):
                        value = right[level, :, node, :] * mine - layer[level, :, node, :]
                        target = node * own - start
                        shift = (target - row * COLUMNS - which * own) % LANES
                        value = pltpu.roll(value, shift, 1) if shift else value
                        total = jnp.where(block == target // own, value, total)
                    stage[level, chunk, which, pl.ds(row, tiles, stride=per_tile), :] = total
            found = [stage[level, chunk, which] for which in range(groups)]
            for step in range(groups):
                chosen = found[0]
                for which in range(1, groups):
                    chosen = jnp.where((gz ^ step) == which, found[which], chosen)
                if step == 0:
                    kept[level][:, lanes] = chosen
                else:
                    away[step - 1][level, :, lanes] = chosen


def lower_kernel(height, nodes, own, parents, pattern, blocks, inverse, high_out, low_out, route):
    first = place_of(height, 1)
    part, width = blocks.shape[2:]
    col = lax.axis_index("col")
    columns = lax.broadcasted_iota(jnp.int32, route.shape[2:], 0)
    slots = lax.broadcasted_iota(jnp.int32, route.shape[2:], 1) // own
    for index in range(STEP):
        node = pl.program_id(0) * STEP + index
        left = blocks[first : first + height, index].reshape(height * part, width)
        whole = product(split(left), split(inverse[0, index])).reshape(height, part, width)
        high_out[:, index], low_out[:, index] = split(whole)
        ancestor = col * nodes + node
        for distance in range(1, height + 1):
            ancestor = parents[height - distance, ancestor]
            stored = pattern[node, place_of(height, distance)] != 0
            slot = jnp.where(stored, lax.rem(ancestor, nodes), -1)
            here = (columns == (lax.div(ancestor, nodes) ^ col)) & (slots == slot)
            route[distance - 1, index] = jnp.where(here, 1.0, 0.0)


def lower_step(height, parents, pattern, blocks, inverse, sizes):
    pairs, nodes, part = blocks.shape[:3]
    own, col_count = sizes[2], sizes[4]
    out = shape_of(height, nodes, part, WIDTH, dtype=BF16)
    route = shape_of(height, nodes, col_count, nodes * own)
    return pl.pallas_call(
        functools.partial(lower_kernel, height, nodes, own),
        grid=(nodes // STEP,),
        out_shape=[out, out, route],
        in_specs=[
            SMEM,
            SMEM,
            pl.BlockSpec((pairs, STEP, part, WIDTH), lambda i: (0, i, 0, 0)),
            pl.BlockSpec((1, STEP, WIDTH, WIDTH), lambda i: (height, i, 0, 0)),
        ],
        out_specs=[pl.BlockSpec((height, STEP, part, WIDTH), lambda i: (0, i, 0, 0))] * 2
        + [pl.BlockSpec((height, STEP) + route.shape[2:], lambda i: (0, i, 0, 0))],
        compiler_params=STREAM_PARAMS,
        name="lower_products",
    )(parents, pattern, blocks, inverse)


def middle_kernel(upper, lower, high_out, low_out, lower_high, lower_low):
    for node in range(STEP):
        right = split(lower[0, node])
        lower_high[node], lower_low[node] = right
        high_out[node], low_out[node] = split(product(split(upper[0, node]), right))


def middle_step(upper, lower):
    nodes = lower.shape[1]
    out = shape_of(nodes, WIDTH, WIDTH, dtype=BF16)
    return pl.pallas_call(
        middle_kernel,
        grid=(nodes // STEP,),
        out_shape=[out] * 4,
        in_specs=[pl.BlockSpec((1, STEP, WIDTH, WIDTH), lambda i: (0, i, 0, 0))] * 2,
        out_specs=[pl.BlockSpec((STEP, WIDTH, WIDTH), lambda i: (i, 0, 0))] * 4,
        compiler_params=MIDDLE_PARAMS,
        name="middle_product",
    )(upper, lower)


def assemble(pieces, full, part):
    row = lax.axis_index("row")
    for step, piece in enumerate(pieces):
        full[pl.ds(pl.multiple_of((row ^ step) * part, part), part), :] = piece[...]


def forward_kernel(height, sizes, *refs):
    nodes, part, own, row_count, col_count = sizes
    lanes = nodes * own
    pieces, refs = refs[:row_count], refs[row_count:]
    m_high, m_low, route = refs[:3]
    pending_in = refs[3 : 3 + height] if height < 3 else ()
    refs = refs[3 + len(pending_in) :]
    full, sends, pending_out = refs[0], refs[1 : 1 + col_count], refs[1 + col_count :]
    assemble(pieces, full, part)
    lane = lax.broadcasted_iota(jnp.int32, (1, lanes), 1) // own
    right = split(full[...])
    rows = height * nodes * part
    whole = product((m_high[...].reshape(rows, WIDTH), m_low[...].reshape(rows, WIDTH)), right)
    for distance in range(1, height + 1):
        level = height - distance
        terms = []
        for node in range(nodes):
            start = ((distance - 1) * nodes + node) * part
            term = whole[start : start + part]
            spread = term
            for slot in range(nodes):
                if slot != node:
                    turned = pltpu.roll(term, (slot - node) * own % lanes, 1)
                    spread = jnp.where(lane == slot, turned, spread)
            terms.append(spread)
        for where in range(col_count):
            total = pending_in[level][where] if pending_in else jnp.zeros((part, lanes), F32)
            for node in range(nodes):
                total = total + route[distance - 1, node, where : where + 1, :] * terms[node]
            if distance == 1:
                sends[where][...] = total
            else:
                pending_out[level][where] = total


def forward_step(height, pieces, m, pending, sizes):
    nodes, part, own, row_count, col_count = sizes
    lanes = nodes * own
    piece = shape_of(part, lanes)
    stack = shape_of(col_count, part, lanes)
    out_shape = [shape_of(row_count * part, lanes)] + [piece] * col_count + [stack] * (height - 1)
    results = pl.pallas_call(
        functools.partial(forward_kernel, height, sizes),
        out_shape=out_shape,
        in_specs=[VMEM] * (len(pieces) + len(m) + len(pending)),
        out_specs=[VMEM] * len(out_shape),
        compiler_params=PARAMS,
        name="forward_level",
    )(*pieces, *m, *pending)
    return results[0], results[1 : 1 + col_count], results[1 + col_count :]


def own_rows(turned, node, own, row_count):
    few = own // row_count
    start = node * own + lax.axis_index("row") * few
    return turned[pl.ds(pl.multiple_of(start, few), few), :]


def last_kernel(sizes, *refs):
    nodes, part, own, row_count, col_count = sizes
    pieces = refs[:row_count]
    z_high, z_low, lower_high, lower_low, solved_out, out, full, turned = refs[row_count:]
    assemble(pieces, full, part)
    turned[...] = full[...].T
    for node in range(nodes):
        left = split(own_rows(turned, node, own, row_count))
        out[node] = product_t(left, (z_high[node], z_low[node]))
    lane = lax.broadcasted_iota(jnp.int32, (1, nodes * own), 1) // own
    rows = nodes * WIDTH
    left = (lower_high[...].reshape(rows, WIDTH), lower_low[...].reshape(rows, WIDTH))
    whole = product(left, split(full[...]))
    solved = whole[:WIDTH]
    for node in range(1, nodes):
        solved = jnp.where(lane == node, whole[node * WIDTH : (node + 1) * WIDTH], solved)
    solved_out[...] = solved


def last_step(pieces, matrices, sizes):
    nodes, part, own, row_count, col_count = sizes
    lanes, rows = nodes * own, row_count * part
    return pl.pallas_call(
        functools.partial(last_kernel, sizes),
        out_shape=[shape_of(rows, lanes), shape_of(nodes, own // row_count, rows)],
        in_specs=[VMEM] * (len(pieces) + len(matrices)),
        out_specs=[VMEM] * 2,
        scratch_shapes=[pltpu.VMEM((rows, lanes), F32), pltpu.VMEM((lanes, rows), F32)],
        compiler_params=PARAMS,
        name="forward_last",
    )(*pieces, *matrices)


def solve_kernel(sizes, full, lower, out, own_out, turned):
    nodes, part, own, row_count, col_count = sizes
    first = pl.program_id(0) * STEP
    lane = lax.broadcasted_iota(jnp.int32, (1, nodes * own), 1) // own

    @pl.when(first == 0)
    def _():
        turned[...] = full[...].T
        out[...] = jnp.zeros(out.shape, F32)

    high, low = split(lower[0].reshape(STEP * WIDTH, WIDTH))
    whole = product((high, low), split(full[...]))
    solved = out[...]
    for step in range(STEP):
        node, rows = first + step, slice(step * WIDTH, (step + 1) * WIDTH)
        solved = jnp.where(lane == node, whole[rows], solved)
        left = split(own_rows(turned, node, own, row_count))
        own_out[step] = product_t(left, (high[rows], low[rows]))
    out[...] = solved


def solve_step(height, full, lower, sizes):
    nodes, part, own, row_count, col_count = sizes
    rows, lanes = full.shape
    few = own // row_count
    whole = pl.BlockSpec((rows, lanes), lambda i: (0, 0))
    return pl.pallas_call(
        functools.partial(solve_kernel, sizes),
        grid=(nodes // STEP,),
        out_shape=[shape_of(rows, lanes), shape_of(nodes, few, rows)],
        in_specs=[whole, pl.BlockSpec((1, STEP, rows, rows), lambda i: (height, i, 0, 0))],
        out_specs=[whole, pl.BlockSpec((STEP, few, rows), lambda i: (i, 0, 0))],
        scratch_shapes=[pltpu.VMEM((lanes, rows), F32)],
        compiler_params=STREAM_PARAMS,
        name="solve_level",
    )(full, lower)


def descend_kernel(height, nodes, col_count, parents, pattern, value, inverse, *refs):
    blocks, pieces, outs = refs[:height], refs[height:-4], refs[-4:]
    out, high_out, low_out, choice = outs
    col = lax.axis_index("col")
    places = lax.broadcasted_iota(jnp.int32, choice.shape[1:], 0)
    for index in range(STEP):
        node = pl.program_id(0) * STEP + index
        rest = value[index]
        left = split(inverse[0, index])
        ancestor = parents[height - 1, col * nodes + node]
        place = (lax.div(ancestor, nodes) ^ col) * nodes + lax.rem(ancestor, nodes)
        place = jnp.where(pattern[node, place_of(height, 1)] != 0, place, -1)
        choice[index] = jnp.where(places == place, 1.0, 0.0)
        for distance in range(2, height + 1):
            level = height - distance
            ancestor = parents[level, ancestor]
            where = lax.div(ancestor, nodes) ^ col
            slot = lax.rem(ancestor, nodes)
            chosen = pieces[level * col_count][slot]
            for step in range(1, col_count):
                piece = pieces[level * col_count + step][slot]
                chosen = jnp.where(where == step, piece, chosen)
            block = blocks[distance - 1][:, 0, index].reshape(WIDTH, WIDTH)
            term = product_t(split(chosen), split(block))
            stored = pattern[node, place_of(height, distance)] != 0
            rest = rest - jnp.where(stored, term, 0.0)
        nearest = blocks[0][:, 0, index].reshape(WIDTH, WIDTH)
        high_out[index], low_out[index] = split(product(left, split(nearest)))
        out[index] = product_t(split(rest), left)


def descend_step(height, parents, pattern, value, gathered, inverse, solved, row_count):
    per, nodes, part = gathered.shape[1:4]
    col_count = lax.axis_size("col")
    few, rows = value.shape[1:]
    pieces = [piece for level in solved for piece in level]

    def block_spec(distance):
        place = place_of(height, distance)
        return pl.BlockSpec(
            (row_count, 1, STEP, part, WIDTH), lambda i: (place // per, place % per, i, 0, 0)
        )

    each = pl.BlockSpec((STEP, few, rows), lambda i: (i, 0, 0))
    whole = pl.BlockSpec((nodes, few, rows), lambda i: (0, 0, 0))
    matrix = shape_of(nodes, WIDTH, WIDTH, dtype=BF16)
    return pl.pallas_call(
        functools.partial(descend_kernel, height, nodes, col_count),
        grid=(nodes // STEP,),
        out_shape=[
            shape_of(nodes, few, rows),
            matrix,
            matrix,
            shape_of(nodes, col_count * nodes, rows),
        ],
        in_specs=[SMEM, SMEM, each]
        + [pl.BlockSpec((1, STEP, WIDTH, WIDTH), lambda i: (height, i, 0, 0))]
        + [block_spec(distance) for distance in range(1, height + 1)]
        + [whole] * len(pieces),
        out_specs=[each]
        + [pl.BlockSpec((STEP, WIDTH, WIDTH), lambda i: (i, 0, 0))] * 2
        + [pl.BlockSpec((STEP, col_count * nodes, rows), lambda i: (i, 0, 0))],
        compiler_params=STREAM_PARAMS,
        name="descend_level",
    )(parents, pattern, value, inverse, *([gathered] * height), *pieces)


def backward_kernel(height, start, high, low, choice, *refs):
    nodes, count = choice.shape[0], choice.shape[1] // choice.shape[0]
    pieces, earlier, out = refs[:count], refs[count:-1], refs[-1]
    for level, value in enumerate(earlier):
        out[level] = value[...]
    for node in range(nodes):
        chosen = jnp.zeros(start.shape[1:], F32)
        for place in range(count * nodes):
            weight = choice[node, place : place + 1, :]
            chosen = chosen + weight * pieces[place // nodes][place % nodes]
        total = start[node] - product_t(split(chosen), (high[node], low[node]))
        if earlier:
            out[height, node] = total
        else:
            out[node] = total


def backward_step(height, parts, pieces, earlier):
    start = parts[0].shape
    return pl.pallas_call(
        functools.partial(backward_kernel, height),
        out_shape=shape_of(*(((1 + len(earlier),) if earlier else ()) + start)),
        in_specs=[VMEM] * (len(parts) + len(pieces) + len(earlier)),
        out_specs=VMEM,
        compiler_params=PARAMS,
        name="backward_level",
    )(*parts, *pieces, *earlier)


def groups_found(found, groups):
    gz = lax.axis_index("gz")
    values = []
    for which in range(groups):
        value = found[0]
        for step in range(1, groups):
            value = jnp.where((gz ^ step) == which, found[step], value)
        values.append(value)
    return values


def forward_out_kernel(gz_count, nodes, own, *refs):
    parts, out, stage = refs[:-2], refs[-2], refs[-1]
    groups = COLUMNS // own
    per_tile = LANES // COLUMNS
    tiles = out.shape[1]
    block = lax.broadcasted_iota(jnp.int32, (1, LANES), 1) // own
    for level in range(out.shape[0]):
        for chunk in range(nodes * own // LANES):
            start = chunk * LANES
            lanes = slice(start, start + LANES)
            found = [part[:, lanes] for part in parts[level * gz_count : (level + 1) * gz_count]]
            for which, value in enumerate(groups_found(found, groups)):
                stage[chunk, which] = value
            values = [
                stage[chunk, which, pl.ds(row, tiles, stride=per_tile), :]
                for row in range(per_tile)
                for which in range(groups)
            ]
            for node in range(start // own, (start + LANES) // own):
                total = jnp.zeros((tiles, LANES), F32)
                for place, value in enumerate(values):
                    shift = (place * own - (node * own - start)) % LANES
                    value = pltpu.roll(value, shift, 1) if shift else value
                    total = jnp.where(block == place, value, total)
                out[level, :, node, :] = total


def forward_out(parts, nodes, own, gz_count):
    rows, lanes = parts[0].shape
    tiles = rows * COLUMNS // LANES
    return pl.pallas_call(
        functools.partial(forward_out_kernel, gz_count, nodes, own),
        out_shape=shape_of(len(parts) // gz_count, tiles, nodes, LANES),
        in_specs=[VMEM] * len(parts),
        out_specs=VMEM,
        scratch_shapes=[pltpu.VMEM((lanes // LANES, COLUMNS // own, rows, LANES), F32)],
        compiler_params=PARAMS,
        name="forward_out",
    )(*parts)


def backward_out_kernel(nodes, gz_count, own, *refs):
    parts, (out, columns, turned) = refs[:-3], refs[-3:]
    groups = COLUMNS // own
    per_tile = LANES // COLUMNS
    tiles = out.shape[1]
    row_count, _, _, few, _ = parts[0].shape
    row = lax.axis_index("row")
    for node in range(nodes):
        for step in range(row_count):
            values = groups_found([part[step, 0, node] for part in parts], groups)
            for which, value in enumerate(values):
                index = which * row_count + (row ^ step)
                columns[node, pl.ds(pl.multiple_of(index * few, few), few), :] = value
        turned[node] = columns[node].T
        rows = [turned[node, pl.ds(step, tiles, stride=per_tile), :] for step in range(per_tile)]
        out[0, :, node, :] = jnp.concatenate(rows, axis=1)


def backward_out(parts, own):
    row_count, levels, nodes, few, rows = parts[0].shape
    tiles = rows * COLUMNS // LANES
    part_spec = pl.BlockSpec((row_count, 1, nodes, few, rows), lambda i: (0, i, 0, 0, 0))
    return pl.pallas_call(
        functools.partial(backward_out_kernel, nodes, len(parts), own),
        grid=(levels,),
        out_shape=shape_of(levels, tiles, nodes, LANES),
        in_specs=[part_spec] * len(parts),
        out_specs=pl.BlockSpec((1, tiles, nodes, LANES), lambda i: (i, 0, 0, 0)),
        scratch_shapes=[
            pltpu.VMEM((nodes, COLUMNS, rows), F32),
            pltpu.VMEM((nodes, rows, COLUMNS), F32),
        ],
        compiler_params=PARAMS,
        name="backward_out",
    )(*parts)


def body(
    right_side,
    layer_sums,
    lower_blocks,
    upper_blocks,
    lower_inverse,
    upper_diagonal_inverses,
    pattern,
    parents,
):
    nodes = right_side.shape[1]
    part = lower_blocks.shape[2]
    gz_count = lax.axis_size("gz")
    row_count = lax.axis_size("row")
    col_count = lax.axis_size("col")
    own = COLUMNS // gz_count
    lanes = nodes * own
    sizes = (nodes, part, own, row_count, col_count)
    gz = lax.axis_index("gz")

    def tiled(value):
        return value.reshape(4, nodes, part * COLUMNS // LANES, LANES).transpose(0, 2, 1, 3)

    parts = pl.pallas_call(
        functools.partial(input_kernel, gz_count, nodes, own),
        out_shape=[shape_of(part, lanes)] * 4 + [shape_of(4, part, lanes)] * (gz_count - 1),
        in_specs=[VMEM, VMEM],
        out_specs=[VMEM] * (3 + gz_count),
        scratch_shapes=[pltpu.VMEM((4, lanes // LANES, COLUMNS // own, part, LANES), F32)],
        compiler_params=INPUT_PARAMS,
        name="input_parts",
    )(tiled(right_side), tiled(layer_sums[0]))
    kept, away = parts[:4], parts[4:]

    per = upper_blocks.shape[0] // gz_count
    half = lax.dynamic_slice_in_dim(after(upper_blocks, *away), gz * per, per, 0)
    upper_rows = lax.all_gather(half, ("gz", "row"))
    others = [after(swap(away[step - 1], "gz", step), half) for step in steps_of(gz_count)]
    pattern = pattern.T
    initial = [kept[level] + sum(other[level] for other in others) for level in range(4)]

    fulls = [None] * 4
    forward = [None] * 4
    pending = []
    mine = initial[3]
    m = lower_step(3, parents, pattern, lower_blocks, lower_inverse, sizes)
    for height in (3, 2, 1):
        pieces = gather(mine, "row")
        if height < 3:
            m = lower_step(height, parents, pattern, lower_blocks, lower_inverse, sizes)
        fulls[height], sends, pending = forward_step(
            height, pieces, m, pending, sizes
        )
        forward[height] = solve_step(height, fulls[height], lower_inverse, sizes)
        taken = [swap(sends[step], "col", step) for step in steps_of(col_count)]
        taken[-1] = after(taken[-1], *forward[height])
        mine = initial[height - 1] - sends[0] - sum(taken)
    z = middle_step(upper_diagonal_inverses, lower_inverse)
    solved_forward, solved = last_step(gather(mine, "row"), z, sizes)
    forward[0] = (solved_forward,)

    backward = [solved]
    whole = []
    for height in (1, 2, 3):
        parts = descend_step(
            height,
            parents,
            pattern,
            forward[height][1],
            upper_rows,
            upper_diagonal_inverses,
            whole,
            row_count,
        )
        whole = whole + [gather(backward[-1], "col")]
        earlier = backward if height == 3 else []
        backward.append(backward_step(height, parts, whole[-1], earlier))

    forward_parts = [piece for level in forward for piece in with_layers(level[0])]
    forward_all = forward_out(forward_parts, nodes, own, gz_count)
    pieces = gather(backward[3], "row")
    pieces[-1] = after(pieces[-1], forward_all)
    backward_all = backward_out(with_layers(jnp.stack(pieces)), own)
    return tuple(
        value.transpose(0, 2, 1, 3).reshape(4, nodes, WIDTH * COLUMNS)
        for value in (forward_all, backward_all)
    )


def solution(mesh):
    in_specs = (
        P(None, "col", "row"),
        P("gz", None, "col", "row"),
        P(None, "col", "row", None),
        P(None, "col", "row", None),
        P(None, "col", None, None),
        P(None, "col", None, None),
        P(None, "col"),
        P(),
    )
    out_specs = (P(None, "col", None), P(None, "col", None))
    return jax.shard_map(body, mesh=mesh, in_specs=in_specs, out_specs=out_specs, check_vma=False)
```

```python
import functools

import jax
import jax.numpy as jnp
from jax import lax
from jax.experimental import pallas as pl
from jax.experimental.pallas import tpu as pltpu
from jax.sharding import PartitionSpec as P

WIDTH = 256
COLUMNS = 64
LANES = 128
F32 = jnp.float32
BF16 = jnp.bfloat16
SMEM = pl.BlockSpec(memory_space=pltpu.SMEM)
VMEM = pl.BlockSpec(memory_space=pltpu.VMEM)
HBM = pl.BlockSpec(memory_space=pltpu.HBM)
PARAMS = pltpu.CompilerParams(vmem_limit_bytes=16 * 2**20)
INPUT_PARAMS = pltpu.CompilerParams(vmem_limit_bytes=107 * 2**19)
MIDDLE_PARAMS = pltpu.CompilerParams(vmem_limit_bytes=51 * 2**20)
STREAM_PARAMS = pltpu.CompilerParams(vmem_limit_bytes=52 * 2**20)


STEP = 2


def place_of(height, distance):
    return height * (height - 1) // 2 + distance - 1


def shape_of(*dims, dtype=F32):
    return jax.ShapeDtypeStruct(dims, dtype)


def split(value):
    high = value.astype(BF16)
    return high, (value - high.astype(F32)).astype(BF16)


def dot(left, right):
    return jnp.dot(left, right, preferred_element_type=F32)


def dot_t(left, right):
    return lax.dot_general(left, right, (((1,), (1,)), ((), ())), preferred_element_type=F32)


def product(left, right):
    lanes = right[0].shape[1]
    both = dot(left[0], jnp.concatenate(right, axis=1))
    return both[:, :lanes] + both[:, lanes:] + dot(left[1], right[0])


def product_t(left, right):
    rows = left[0].shape[0]
    both = dot_t(jnp.concatenate(left, axis=0), right[0])
    return both[:rows] + both[rows:] + dot_t(left[0], right[1])


def steps_of(count):
    assert count & (count - 1) == 0
    return range(1, count)


def swap(value, axis, step):
    return lax.ppermute(value, axis, [(i, i ^ step) for i in range(lax.axis_size(axis))])


def with_layers(value):
    return [value] + [swap(value, "gz", step) for step in steps_of(lax.axis_size("gz"))]


def after(value, *others):
    return lax.optimization_barrier((value, *others))[0]


def gather(value, axis):
    return [value] + [swap(value, axis, step) for step in steps_of(lax.axis_size(axis))]


def input_kernel(gz_count, nodes, own, right, layer, *outs):
    groups = COLUMNS // own
    kept, away, stage = outs[:4], outs[4:-1], outs[-1]
    gz = lax.axis_index("gz")
    tiles = right.shape[1]
    per_tile = LANES // COLUMNS
    block = lax.broadcasted_iota(jnp.int32, (1, LANES), 1) // own
    for level in range(right.shape[0]):
        for chunk in range(nodes * own // LANES):
            start = chunk * LANES
            lanes = slice(start, start + LANES)
            for row in range(per_tile):
                for which in range(groups):
                    mine = jnp.where(gz == which, 1.0, 0.0)
                    total = jnp.zeros((tiles, LANES), F32)
                    for node in range(start // own, (start + LANES) // own):
                        value = right[level, :, node, :] * mine - layer[level, :, node, :]
                        target = node * own - start
                        shift = (target - row * COLUMNS - which * own) % LANES
                        value = pltpu.roll(value, shift, 1) if shift else value
                        total = jnp.where(block == target // own, value, total)
                    stage[level, chunk, which, pl.ds(row, tiles, stride=per_tile), :] = total
            found = [stage[level, chunk, which] for which in range(groups)]
            for step in range(groups):
                chosen = found[0]
                for which in range(1, groups):
                    chosen = jnp.where((gz ^ step) == which, found[which], chosen)
                if step == 0:
                    kept[level][:, lanes] = chosen
                else:
                    away[step - 1][level, :, lanes] = chosen


def lower_kernel(height, nodes, own, parents, pattern, blocks, inverse, high_out, low_out, route):
    first = place_of(height, 1)
    part, width = blocks.shape[2:]
    col = lax.axis_index("col")
    columns = lax.broadcasted_iota(jnp.int32, route.shape[2:], 0)
    slots = lax.broadcasted_iota(jnp.int32, route.shape[2:], 1) // own
    for index in range(STEP):
        node = pl.program_id(0) * STEP + index
        left = blocks[first : first + height, index].reshape(height * part, width)
        whole = product(split(left), split(inverse[0, index])).reshape(height, part, width)
        high_out[:, index], low_out[:, index] = split(whole)
        ancestor = col * nodes + node
        for distance in range(1, height + 1):
            ancestor = parents[height - distance, ancestor]
            stored = pattern[node, place_of(height, distance)] != 0
            slot = jnp.where(stored, lax.rem(ancestor, nodes), -1)
            here = (columns == (lax.div(ancestor, nodes) ^ col)) & (slots == slot)
            route[distance - 1, index] = jnp.where(here, 1.0, 0.0)


def lower_step(height, parents, pattern, blocks, inverse, sizes):
    pairs, nodes, part = blocks.shape[:3]
    own, col_count = sizes[2], sizes[4]
    out = shape_of(height, nodes, part, WIDTH, dtype=BF16)
    route = shape_of(height, nodes, col_count, nodes * own)
    return pl.pallas_call(
        functools.partial(lower_kernel, height, nodes, own),
        grid=(nodes // STEP,),
        out_shape=[out, out, route],
        in_specs=[
            SMEM,
            SMEM,
            pl.BlockSpec((pairs, STEP, part, WIDTH), lambda i: (0, i, 0, 0)),
            pl.BlockSpec((1, STEP, WIDTH, WIDTH), lambda i: (height, i, 0, 0)),
        ],
        out_specs=[pl.BlockSpec((height, STEP, part, WIDTH), lambda i: (0, i, 0, 0))] * 2
        + [pl.BlockSpec((height, STEP) + route.shape[2:], lambda i: (0, i, 0, 0))],
        compiler_params=STREAM_PARAMS,
        name="lower_products",
    )(parents, pattern, blocks, inverse)


def middle_kernel(upper, lower, high_out, low_out, lower_high, lower_low):
    for node in range(STEP):
        right = split(lower[0, node])
        lower_high[node], lower_low[node] = right
        high_out[node], low_out[node] = split(product(split(upper[0, node]), right))


def middle_step(upper, lower):
    nodes = lower.shape[1]
    out = shape_of(nodes, WIDTH, WIDTH, dtype=BF16)
    return pl.pallas_call(
        middle_kernel,
        grid=(nodes // STEP,),
        out_shape=[out] * 4,
        in_specs=[pl.BlockSpec((1, STEP, WIDTH, WIDTH), lambda i: (0, i, 0, 0))] * 2,
        out_specs=[pl.BlockSpec((STEP, WIDTH, WIDTH), lambda i: (i, 0, 0))] * 4,
        compiler_params=MIDDLE_PARAMS,
        name="middle_product",
    )(upper, lower)


def assemble(pieces, full, part):
    row = lax.axis_index("row")
    for step, piece in enumerate(pieces):
        full[pl.ds(pl.multiple_of((row ^ step) * part, part), part), :] = piece[...]


def forward_kernel(height, sizes, *refs):
    nodes, part, own, row_count, col_count = sizes
    lanes = nodes * own
    pieces, refs = refs[:row_count], refs[row_count:]
    m_high, m_low, route = refs[:3]
    pending_in = refs[3 : 3 + height] if height < 3 else ()
    refs = refs[3 + len(pending_in) :]
    full, sends, pending_out = refs[0], refs[1 : 1 + col_count], refs[1 + col_count :]
    assemble(pieces, full, part)
    lane = lax.broadcasted_iota(jnp.int32, (1, lanes), 1) // own
    right = split(full[...])
    rows = height * nodes * part
    whole = product((m_high[...].reshape(rows, WIDTH), m_low[...].reshape(rows, WIDTH)), right)
    for distance in range(1, height + 1):
        level = height - distance
        terms = []
        for node in range(nodes):
            start = ((distance - 1) * nodes + node) * part
            term = whole[start : start + part]
            spread = term
            for slot in range(nodes):
                if slot != node:
                    turned = pltpu.roll(term, (slot - node) * own % lanes, 1)
                    spread = jnp.where(lane == slot, turned, spread)
            terms.append(spread)
        for where in range(col_count):
            total = pending_in[level][where] if pending_in else jnp.zeros((part, lanes), F32)
            for node in range(nodes):
                total = total + route[distance - 1, node, where : where + 1, :] * terms[node]
            if distance == 1:
                sends[where][...] = total
            else:
                pending_out[level][where] = total


def forward_step(height, pieces, m, pending, sizes):
    nodes, part, own, row_count, col_count = sizes
    lanes = nodes * own
    piece = shape_of(part, lanes)
    stack = shape_of(col_count, part, lanes)
    out_shape = [shape_of(row_count * part, lanes)] + [piece] * col_count + [stack] * (height - 1)
    results = pl.pallas_call(
        functools.partial(forward_kernel, height, sizes),
        out_shape=out_shape,
        in_specs=[VMEM] * (len(pieces) + len(m) + len(pending)),
        out_specs=[VMEM] * len(out_shape),
        compiler_params=PARAMS,
        name="forward_level",
    )(*pieces, *m, *pending)
    return results[0], results[1 : 1 + col_count], results[1 + col_count :]


def own_rows(turned, node, own, row_count):
    few = own // row_count
    start = node * own + lax.axis_index("row") * few
    return turned[pl.ds(pl.multiple_of(start, few), few), :]


def last_kernel(sizes, *refs):
    nodes, part, own, row_count, col_count = sizes
    pieces = refs[:row_count]
    z_high, z_low, lower_high, lower_low, solved_out, out, full, turned = refs[row_count:]
    assemble(pieces, full, part)
    turned[...] = full[...].T
    for node in range(nodes):
        left = split(own_rows(turned, node, own, row_count))
        out[node] = product_t(left, (z_high[node], z_low[node]))
    lane = lax.broadcasted_iota(jnp.int32, (1, nodes * own), 1) // own
    rows = nodes * WIDTH
    left = (lower_high[...].reshape(rows, WIDTH), lower_low[...].reshape(rows, WIDTH))
    whole = product(left, split(full[...]))
    solved = whole[:WIDTH]
    for node in range(1, nodes):
        solved = jnp.where(lane == node, whole[node * WIDTH : (node + 1) * WIDTH], solved)
    solved_out[...] = solved


def last_step(pieces, matrices, sizes):
    nodes, part, own, row_count, col_count = sizes
    lanes, rows = nodes * own, row_count * part
    return pl.pallas_call(
        functools.partial(last_kernel, sizes),
        out_shape=[shape_of(rows, lanes), shape_of(nodes, own // row_count, rows)],
        in_specs=[VMEM] * (len(pieces) + len(matrices)),
        out_specs=[VMEM] * 2,
        scratch_shapes=[pltpu.VMEM((rows, lanes), F32), pltpu.VMEM((lanes, rows), F32)],
        compiler_params=PARAMS,
        name="forward_last",
    )(*pieces, *matrices)


def solve_kernel(sizes, full, lower, out, own_out, turned):
    nodes, part, own, row_count, col_count = sizes
    first = pl.program_id(0) * STEP
    lane = lax.broadcasted_iota(jnp.int32, (1, nodes * own), 1) // own

    @pl.when(first == 0)
    def _():
        turned[...] = full[...].T
        out[...] = jnp.zeros(out.shape, F32)

    high, low = split(lower[0].reshape(STEP * WIDTH, WIDTH))
    whole = product((high, low), split(full[...]))
    solved = out[...]
    for step in range(STEP):
        node, rows = first + step, slice(step * WIDTH, (step + 1) * WIDTH)
        solved = jnp.where(lane == node, whole[rows], solved)
        left = split(own_rows(turned, node, own, row_count))
        own_out[step] = product_t(left, (high[rows], low[rows]))
    out[...] = solved


def solve_step(height, full, lower, sizes):
    nodes, part, own, row_count, col_count = sizes
    rows, lanes = full.shape
    few = own // row_count
    whole = pl.BlockSpec((rows, lanes), lambda i: (0, 0))
    return pl.pallas_call(
        functools.partial(solve_kernel, sizes),
        grid=(nodes // STEP,),
        out_shape=[shape_of(rows, lanes), shape_of(nodes, few, rows)],
        in_specs=[whole, pl.BlockSpec((1, STEP, rows, rows), lambda i: (height, i, 0, 0))],
        out_specs=[whole, pl.BlockSpec((STEP, few, rows), lambda i: (i, 0, 0))],
        scratch_shapes=[pltpu.VMEM((lanes, rows), F32)],
        compiler_params=STREAM_PARAMS,
        name="solve_level",
    )(full, lower)


def descend_kernel(height, nodes, col_count, parents, pattern, value, inverse, *refs):
    blocks, pieces, outs = refs[:height], refs[height:-4], refs[-4:]
    out, high_out, low_out, choice = outs
    col = lax.axis_index("col")
    places = lax.broadcasted_iota(jnp.int32, choice.shape[1:], 0)
    for index in range(STEP):
        node = pl.program_id(0) * STEP + index
        rest = value[index]
        left = split(inverse[0, index])
        ancestor = parents[height - 1, col * nodes + node]
        place = (lax.div(ancestor, nodes) ^ col) * nodes + lax.rem(ancestor, nodes)
        place = jnp.where(pattern[node, place_of(height, 1)] != 0, place, -1)
        choice[index] = jnp.where(places == place, 1.0, 0.0)
        for distance in range(2, height + 1):
            level = height - distance
            ancestor = parents[level, ancestor]
            where = lax.div(ancestor, nodes) ^ col
            slot = lax.rem(ancestor, nodes)
            chosen = pieces[level * col_count][slot]
            for step in range(1, col_count):
                piece = pieces[level * col_count + step][slot]
                chosen = jnp.where(where == step, piece, chosen)
            block = blocks[distance - 1][:, 0, index].reshape(WIDTH, WIDTH)
            term = product_t(split(chosen), split(block))
            stored = pattern[node, place_of(height, distance)] != 0
            rest = rest - jnp.where(stored, term, 0.0)
        nearest = blocks[0][:, 0, index].reshape(WIDTH, WIDTH)
        high_out[index], low_out[index] = split(product(left, split(nearest)))
        out[index] = product_t(split(rest), left)


def descend_step(height, parents, pattern, value, gathered, inverse, solved, row_count):
    per, nodes, part = gathered.shape[1:4]
    col_count = lax.axis_size("col")
    few, rows = value.shape[1:]
    pieces = [piece for level in solved for piece in level]

    def block_spec(distance):
        place = place_of(height, distance)
        return pl.BlockSpec(
            (row_count, 1, STEP, part, WIDTH), lambda i: (place // per, place % per, i, 0, 0)
        )

    each = pl.BlockSpec((STEP, few, rows), lambda i: (i, 0, 0))
    whole = pl.BlockSpec((nodes, few, rows), lambda i: (0, 0, 0))
    matrix = shape_of(nodes, WIDTH, WIDTH, dtype=BF16)
    return pl.pallas_call(
        functools.partial(descend_kernel, height, nodes, col_count),
        grid=(nodes // STEP,),
        out_shape=[
            shape_of(nodes, few, rows),
            matrix,
            matrix,
            shape_of(nodes, col_count * nodes, rows),
        ],
        in_specs=[SMEM, SMEM, each]
        + [pl.BlockSpec((1, STEP, WIDTH, WIDTH), lambda i: (height, i, 0, 0))]
        + [block_spec(distance) for distance in range(1, height + 1)]
        + [whole] * len(pieces),
        out_specs=[each]
        + [pl.BlockSpec((STEP, WIDTH, WIDTH), lambda i: (i, 0, 0))] * 2
        + [pl.BlockSpec((STEP, col_count * nodes, rows), lambda i: (i, 0, 0))],
        compiler_params=STREAM_PARAMS,
        name="descend_level",
    )(parents, pattern, value, inverse, *([gathered] * height), *pieces)


def backward_kernel(height, start, high, low, choice, *refs):
    nodes, count = choice.shape[0], choice.shape[1] // choice.shape[0]
    pieces, earlier, out = refs[:count], refs[count:-1], refs[-1]
    for level, value in enumerate(earlier):
        out[level] = value[...]
    for node in range(nodes):
        chosen = jnp.zeros(start.shape[1:], F32)
        for place in range(count * nodes):
            weight = choice[node, place : place + 1, :]
            chosen = chosen + weight * pieces[place // nodes][place % nodes]
        total = start[node] - product_t(split(chosen), (high[node], low[node]))
        if earlier:
            out[height, node] = total
        else:
            out[node] = total


def backward_step(height, parts, pieces, earlier):
    start = parts[0].shape
    return pl.pallas_call(
        functools.partial(backward_kernel, height),
        out_shape=shape_of(*(((1 + len(earlier),) if earlier else ()) + start)),
        in_specs=[VMEM] * (len(parts) + len(pieces) + len(earlier)),
        out_specs=VMEM,
        compiler_params=PARAMS,
        name="backward_level",
    )(*parts, *pieces, *earlier)


def groups_found(found, groups):
    gz = lax.axis_index("gz")
    values = []
    for which in range(groups):
        value = found[0]
        for step in range(1, groups):
            value = jnp.where((gz ^ step) == which, found[step], value)
        values.append(value)
    return values


def forward_out_kernel(gz_count, nodes, own, *refs):
    parts, out, stage = refs[:-2], refs[-2], refs[-1]
    groups = COLUMNS // own
    per_tile = LANES // COLUMNS
    tiles = out.shape[1]
    block = lax.broadcasted_iota(jnp.int32, (1, LANES), 1) // own
    for level in range(out.shape[0]):
        for chunk in range(nodes * own // LANES):
            start = chunk * LANES
            lanes = slice(start, start + LANES)
            found = [part[:, lanes] for part in parts[level * gz_count : (level + 1) * gz_count]]
            for which, value in enumerate(groups_found(found, groups)):
                stage[chunk, which] = value
            values = [
                stage[chunk, which, pl.ds(row, tiles, stride=per_tile), :]
                for row in range(per_tile)
                for which in range(groups)
            ]
            for node in range(start // own, (start + LANES) // own):
                total = jnp.zeros((tiles, LANES), F32)
                for place, value in enumerate(values):
                    shift = (place * own - (node * own - start)) % LANES
                    value = pltpu.roll(value, shift, 1) if shift else value
                    total = jnp.where(block == place, value, total)
                out[level, :, node, :] = total


def forward_out(parts, nodes, own, gz_count):
    rows, lanes = parts[0].shape
    tiles = rows * COLUMNS // LANES
    return pl.pallas_call(
        functools.partial(forward_out_kernel, gz_count, nodes, own),
        out_shape=shape_of(len(parts) // gz_count, tiles, nodes, LANES),
        in_specs=[VMEM] * len(parts),
        out_specs=VMEM,
        scratch_shapes=[pltpu.VMEM((lanes // LANES, COLUMNS // own, rows, LANES), F32)],
        compiler_params=PARAMS,
        name="forward_out",
    )(*parts)


def backward_out_kernel(nodes, gz_count, own, *refs):
    parts, (out, columns, turned) = refs[:-3], refs[-3:]
    groups = COLUMNS // own
    per_tile = LANES // COLUMNS
    tiles = out.shape[1]
    row_count, _, _, few, _ = parts[0].shape
    row = lax.axis_index("row")
    for level in range(STEP):
        for node in range(nodes):
            for step in range(row_count):
                values = groups_found([part[step, level, node] for part in parts], groups)
                for which, value in enumerate(values):
                    index = which * row_count + (row ^ step)
                    place = pl.ds(pl.multiple_of(index * few, few), few)
                    columns[level, node, place, :] = value
            turned[level, node] = columns[level, node].T
            rows = [
                turned[level, node, pl.ds(step, tiles, stride=per_tile), :]
                for step in range(per_tile)
            ]
            out[level, :, node, :] = jnp.concatenate(rows, axis=1)


def backward_out(parts, own):
    row_count, levels, nodes, few, rows = parts[0].shape
    tiles = rows * COLUMNS // LANES
    part_spec = pl.BlockSpec((row_count, STEP, nodes, few, rows), lambda i: (0, i, 0, 0, 0))
    return pl.pallas_call(
        functools.partial(backward_out_kernel, nodes, len(parts), own),
        grid=(levels // STEP,),
        out_shape=shape_of(levels, tiles, nodes, LANES),
        in_specs=[part_spec] * len(parts),
        out_specs=pl.BlockSpec((STEP, tiles, nodes, LANES), lambda i: (i, 0, 0, 0)),
        scratch_shapes=[
            pltpu.VMEM((STEP, nodes, COLUMNS, rows), F32),
            pltpu.VMEM((STEP, nodes, rows, COLUMNS), F32),
        ],
        compiler_params=PARAMS,
        name="backward_out",
    )(*parts)


def body(
    right_side,
    layer_sums,
    lower_blocks,
    upper_blocks,
    lower_inverse,
    upper_diagonal_inverses,
    pattern,
    parents,
):
    nodes = right_side.shape[1]
    part = lower_blocks.shape[2]
    gz_count = lax.axis_size("gz")
    row_count = lax.axis_size("row")
    col_count = lax.axis_size("col")
    own = COLUMNS // gz_count
    lanes = nodes * own
    sizes = (nodes, part, own, row_count, col_count)
    gz = lax.axis_index("gz")

    def tiled(value):
        return value.reshape(4, nodes, part * COLUMNS // LANES, LANES).transpose(0, 2, 1, 3)

    parts = pl.pallas_call(
        functools.partial(input_kernel, gz_count, nodes, own),
        out_shape=[shape_of(part, lanes)] * 4 + [shape_of(4, part, lanes)] * (gz_count - 1),
        in_specs=[VMEM, VMEM],
        out_specs=[VMEM] * (3 + gz_count),
        scratch_shapes=[pltpu.VMEM((4, lanes // LANES, COLUMNS // own, part, LANES), F32)],
        compiler_params=INPUT_PARAMS,
        name="input_parts",
    )(tiled(right_side), tiled(layer_sums[0]))
    kept, away = parts[:4], parts[4:]

    per = upper_blocks.shape[0] // gz_count
    half = lax.dynamic_slice_in_dim(after(upper_blocks, *away), gz * per, per, 0)
    upper_rows = lax.all_gather(half, ("gz", "row"))
    others = [after(swap(away[step - 1], "gz", step), half) for step in steps_of(gz_count)]
    pattern = pattern.T
    initial = [kept[level] + sum(other[level] for other in others) for level in range(4)]

    fulls = [None] * 4
    forward = [None] * 4
    pending = []
    mine = initial[3]
    m = lower_step(3, parents, pattern, lower_blocks, lower_inverse, sizes)
    for height in (3, 2, 1):
        pieces = gather(mine, "row")
        if height < 3:
            m = lower_step(height, parents, pattern, lower_blocks, lower_inverse, sizes)
        fulls[height], sends, pending = forward_step(
            height, pieces, m, pending, sizes
        )
        forward[height] = solve_step(height, fulls[height], lower_inverse, sizes)
        taken = [swap(sends[step], "col", step) for step in steps_of(col_count)]
        taken[-1] = after(taken[-1], *forward[height])
        mine = initial[height - 1] - sends[0] - sum(taken)
    z = middle_step(upper_diagonal_inverses, lower_inverse)
    solved_forward, solved = last_step(gather(mine, "row"), z, sizes)
    forward[0] = (solved_forward,)

    backward = [solved]
    whole = []
    for height in (1, 2, 3):
        parts = descend_step(
            height,
            parents,
            pattern,
            forward[height][1],
            upper_rows,
            upper_diagonal_inverses,
            whole,
            row_count,
        )
        whole = whole + [gather(backward[-1], "col")]
        earlier = backward if height == 3 else []
        backward.append(backward_step(height, parts, whole[-1], earlier))

    forward_parts = [piece for level in forward for piece in with_layers(level[0])]
    forward_all = forward_out(forward_parts, nodes, own, gz_count)
    pieces = gather(backward[3], "row")
    pieces[-1] = after(pieces[-1], forward_all)
    backward_all = backward_out(with_layers(jnp.stack(pieces)), own)
    return tuple(
        value.transpose(0, 2, 1, 3).reshape(4, nodes, WIDTH * COLUMNS)
        for value in (forward_all, backward_all)
    )


def solution(mesh):
    in_specs = (
        P(None, "col", "row"),
        P("gz", None, "col", "row"),
        P(None, "col", "row", None),
        P(None, "col", "row", None),
        P(None, "col", None, None),
        P(None, "col", None, None),
        P(None, "col"),
        P(),
    )
    out_specs = (P(None, "col", None), P(None, "col", None))
    return jax.shard_map(body, mesh=mesh, in_specs=in_specs, out_specs=out_specs, check_vma=False)
```
